32 devices in a mesh: group: 2 (over x), dp: 4 (over z), mp: 4 (over y, core).
Axes of the slice: x: 2, y: 2, z: 4, core: 2. Of those that a mesh axis runs over, the one named last changes fastest.
Arguments:
- patch_rows: bfloat16 [8, 128, 1280], P(('group', 'dp')), may hold values from -6 to 6
- ln_gain: float32 [1280], replicated, may hold values from 0.5 to 1.5
- ln_bias: float32 [1280], replicated, may hold values from -1.5 to 1.5
- merge_up: bfloat16 [5120, 5120], P(None, 'mp'), may hold values from -0.078125 to 0.078125
- merge_up_bias: float32 [5120], P('mp'), may hold values from -2.5 to 2.5
- merge_down: bfloat16 [5120, 8192], P('mp'), may hold values from -0.078125 to 0.078125
- merge_down_bias: float32 [8192], P('mp'), may hold values from -2.5 to 2.5
- row_owner: int32 [256, 1], replicated, may hold values from 0 to 7; in each aligned block of 32 rows (0 to 31, 32 to 63, ...) at most 8 rows name the same one
- text_embed: bfloat16 [8, 256, 8192], P(('group', 'dp')), may hold values from -6 to 6
- doc_ids: int32 [8, 256], P(('group', 'dp')), may hold values from 0 to 7, never falling along the last dimension, each value on 1 to 64 neighbouring positions
- rms_gain: float32 [8192], replicated, may hold values from 0.5 to 1.5
- w_query: bfloat16 [8192, 8192], P(None, 'mp'), as said below
- query_bias: float32 [8192], P('mp'), may hold values from -2.5 to 2.5
- w_keyval: bfloat16 [8192, 2, 1024], P(None, None, 'mp'), may hold values from -0.0625 to 0.0625
- keyval_bias: float32 [2, 1024], P(None, 'mp'), may hold values from -2.5 to 2.5
Outputs:
- attention: bfloat16 [8, 256, 8192], P(('group', 'dp'), None, 'mp')
The draws below stay inside these ranges and needn't reach their ends.
Inputs may be any that keep to these rules, and one draw needn't show every extreme that they name: `row_owner`: in each aligned block of 32 rows (the rows of one image owner) no owner is named more than 8 times, a bound that some block reaches. `w_query`: columns are independent with entries of scale about D ** -0.5 or larger.
All inputs are finite; a program needn't handle non-finite values.
Results may differ from the reference program's by a relative error of at most 0.014.
The reference program's roundings to bfloat16 on the way count: a program that leaves them out, or rounds other values in their place, can miss the bound.
Values may be sent and summed in bfloat16 or wider, within the bound.
No kernel may reach another device: no remote copies, remote signals or barrier semaphores. Data moves between devices by JAX's collectives and lax.ppermute only.
A program may use at most 128 MiB of HBM per device.

```python
import math
import jax
import jax.numpy as jnp
import numpy as np
from jax import lax

D = 8192
HEADS = 64
KV_HEADS = 8
HEAD_DIM = 128
VIS_WIDTH = 1280
MERGE_HIDDEN = 5120
M_DEV = 32
S_DEV = 256
OWNERS = 8
CAP = 8
M_ALL = 256
TOKENS = 2048


def draw_w_query(key, part):
    values = jax.random.normal(key, (D, HEADS * HEAD_DIM), jnp.float32)
    values = jnp.clip(values, -6.0, 6.0) * D ** (-0.5)
    return values.astype(jnp.bfloat16)


def level_of(stream_key, dims, pieces, least, largest):
    factor_of, own = 1.0, jax.random.fold_in(stream_key, 6)
    for position, shards_of in pieces:
        draws = jnp.exp(jax.random.uniform(jax.random.fold_in(own, position), (shards_of,), jnp.float32, least / len(pieces), largest / len(pieces)))
        factor_of = factor_of * jnp.repeat(draws, dims[position] // shards_of).reshape([-1 if axis == position else 1 for axis in range(len(dims))])
    return factor_of


def split_up(amount, total, most, lean):
    loads = [(1 << 20) // math.isqrt(rank ** lean) + 1 for rank in range(2, amount + 1)]
    surplus, counts = total - most - (amount - 1), [1] * (amount - 1)
    while surplus > 0:
        free = [i for i in range(amount - 1) if counts[i] < most]
        whole, remaining = sum([loads[i] for i in free]), surplus
        for i in free:
            addition = min(most - counts[i], max(1, remaining * loads[i] // whole), surplus)
            counts[i] = counts[i] + addition
            surplus = surplus - addition
    return np.array([most] + counts)


def ragged_sizes(key, count, total, reach, lean):
    if count == 2:
        one = jax.random.randint(key, (), max(1, total - reach), min(reach, total - 1) + 1)
        return jnp.stack([one, total - one])
    tallies = jnp.asarray(split_up(count, total, reach, lean), jnp.int32)
    twos = (count - 1) // 2
    donor, sink = tallies[1:1 + 2 * twos:2], tallies[2:2 + 2 * twos:2]
    room = jnp.minimum(donor - 1, reach - sink)
    moved = jax.random.randint(jax.random.fold_in(key, 1), (twos,), 0, 1 << 20) % (room + 1)
    tallies = tallies.at[1:1 + 2 * twos:2].set(donor - moved).at[2:2 + 2 * twos:2].set(sink + moved)
    return tallies[jax.random.permutation(jax.random.fold_in(key, 2), count)]


def assign_block(stream_key, own, number, rows, count, top, reach, lean):
    order = jax.random.permutation(stream_key, count)
    crowded, ordinary = portions_of(count, rows * top, reach, lean, True), portions_of(count, rows * top, reach, lean, False)
    places = jnp.arange(count)

    def named(tallies, offset_by):
        used = int((tallies > 0).sum())
        fixed = max(1, used // 4)
        shifted = fixed + (places - fixed + offset_by * (used - fixed)) % max(1, count - fixed)
        return jnp.zeros((count,), jnp.int32).at[order[jnp.where(places < fixed, places, shifted)]].set(jnp.asarray(tallies, jnp.int32))

    tallies = jnp.where(number % 4 == 0, named(crowded, number // 4), named(ordinary, number - number // 4 - 1))
    mixed = jax.random.permutation(jax.random.fold_in(own, 3), count)
    source_of, receiver = mixed[0:count // 2 * 2:2], mixed[1:count // 2 * 2:2]
    room = jnp.minimum(tallies[source_of] - 1, reach - tallies[receiver]) // 2
    room = jnp.where((source_of == order[0]) | (receiver == order[0]) | (tallies[receiver] == 0), 0, jnp.maximum(room, 0))
    shifted = jax.random.randint(jax.random.fold_in(own, 4), (count // 2,), 0, 1 << 20) % (room + 1)
    tallies = tallies.at[source_of].add(-shifted).at[receiver].add(shifted)
    labels = jnp.searchsorted(jnp.cumsum(tallies), jnp.arange(rows * top), side="right").astype(jnp.int32)
    grid = labels.reshape(top, rows).T
    grid = grid[jax.random.permutation(jax.random.fold_in(own, 1), rows)]
    offset_by = jax.random.randint(jax.random.fold_in(own, 2), (rows, 1), 0, top)
    return jnp.take_along_axis(grid, (jnp.arange(top)[None, :] + offset_by) % top, axis=1)


def portions_of(count, total, bound, skew, full):
    portions = [(1 << 20) // math.isqrt(rank ** skew) + 1 for rank in range(1, count + 1)]
    largest = bound if full else min(bound, max(-(-total // count), total * portions[0] // sum(portions)))
    least = 1 if total - largest >= count - 1 else 0
    holding, spare = [largest] + [least] * (count - 1), total - largest - least * (count - 1)
    while spare > 0:
        movable = [i for i in range(1, count) if holding[i] < largest] or [i for i in range(1, count) if holding[i] < bound]
        mass, left = sum([portions[i] for i in movable]), spare
        for i in movable:
            extra = min(bound - holding[i], max(1, left * portions[i] // mass), spare)
            holding[i] = holding[i] + extra
            spare = spare - extra
    return np.array(holding)


def noise(own_key, shape, scale, most, shards=(), kind=jnp.bfloat16):
    level = level_of(own_key, shape, shards, -0.22, 0.18) if shards else 1.0
    values = jax.random.normal(own_key, shape, jnp.float32) * scale * level
    return jnp.minimum(jnp.maximum(values, -most), most).astype(kind)


def setup_inputs(seed: int = 0) -> dict:
    arg_keys = jax.random.split(jax.random.key(seed), 16)
    patch_rows = noise(arg_keys[0], (OWNERS, 4 * M_DEV, VIS_WIDTH), 1.0, 6.0, ((0, 8),))
    ln_gain = jnp.clip(1.0 + 0.1 * jax.random.normal(arg_keys[1], (VIS_WIDTH,), jnp.float32), 0.5, 1.5)
    ln_bias = noise(arg_keys[2], (VIS_WIDTH,), 0.3, 1.5, (), jnp.float32)
    merge_up = noise(arg_keys[3], (4 * VIS_WIDTH, MERGE_HIDDEN), (4 * VIS_WIDTH) ** -0.5, 0.078125, ((1, 4),))
    merge_up_bias = noise(arg_keys[4], (MERGE_HIDDEN,), 0.5, 2.5, ((0, 4),), jnp.float32)
    merge_down = noise(arg_keys[5], (MERGE_HIDDEN, D), MERGE_HIDDEN ** -0.5, 0.078125, ((0, 4),))
    merge_down_bias = noise(arg_keys[6], (D,), 0.5, 2.5, ((0, 4),), jnp.float32)
    row_owner_keys = jax.random.split(jax.random.fold_in(arg_keys[7], 1), M_ALL // M_DEV)
    row_owner_turns = jax.random.permutation(jax.random.fold_in(arg_keys[7], 3), M_ALL // M_DEV)
    row_owner = jax.vmap(lambda own, number: assign_block(jax.random.fold_in(arg_keys[7], 2), own, number, M_DEV, OWNERS, 1, CAP, 2))(row_owner_keys, row_owner_turns).reshape((M_ALL, 1))
    text_embed = noise(arg_keys[8], (OWNERS, S_DEV, D), 1.0, 6.0, ((0, 8),))
    doc_ids = jax.vmap(lambda own: jnp.searchsorted(jnp.cumsum(ragged_sizes(own, 8, S_DEV, S_DEV // 4, 2)), jnp.arange(S_DEV), side="right"))(jax.random.split(arg_keys[9], OWNERS)).reshape((OWNERS, S_DEV)).astype(jnp.int32)
    rms_gain = jnp.clip(1.0 + 0.1 * jax.random.normal(arg_keys[10], (D,), jnp.float32), 0.5, 1.5)
    w_query = draw_w_query(jax.random.fold_in(arg_keys[15], 71), 0)
    query_bias = noise(arg_keys[12], (HEADS * HEAD_DIM,), 0.5, 2.5, ((0, 4),), jnp.float32)
    w_keyval = noise(arg_keys[13], (D, 2, HEAD_DIM * KV_HEADS), D ** -0.5, 0.0625, ((2, 4),))
    keyval_bias = noise(arg_keys[14], (2, HEAD_DIM * KV_HEADS), 0.5, 2.5, ((1, 4),), jnp.float32)
    return dict(patch_rows=patch_rows, ln_gain=ln_gain, ln_bias=ln_bias, merge_up=merge_up, merge_up_bias=merge_up_bias, merge_down=merge_down, merge_down_bias=merge_down_bias, row_owner=row_owner, text_embed=text_embed, doc_ids=doc_ids, rms_gain=rms_gain, w_query=w_query, query_bias=query_bias, w_keyval=w_keyval, keyval_bias=keyval_bias)


def attend_owner(inputs):
    queries, keyval, documents = inputs
    group_size = HEADS // KV_HEADS
    query_f = queries.astype(jnp.float32)
    keys = jnp.repeat(keyval[:, 0], group_size, axis=1).astype(jnp.float32)
    values = jnp.repeat(keyval[:, 1], group_size, axis=1).astype(jnp.float32)
    scores = jnp.einsum('qhd,khd->hqk', query_f, keys) / math.sqrt(HEAD_DIM)
    positions = jnp.arange(S_DEV, dtype=jnp.int32)
    allowed = (documents[:, None] == documents[None, :]) & (positions[None, :] <= positions[:, None])
    scores = jnp.where(allowed[None], scores, jnp.float32(-1e+30))
    highest = lax.optimization_barrier(jnp.max(scores, axis=-1, keepdims=True))
    weights = jnp.exp(scores - highest)
    probs = (weights / lax.optimization_barrier(jnp.sum(weights, axis=-1, keepdims=True))).astype(jnp.bfloat16)
    output = jnp.einsum('hqk,khd->qhd', probs.astype(jnp.float32), values)
    return output.astype(jnp.bfloat16).reshape(S_DEV, HEADS * HEAD_DIM)

def reference(patch_rows, ln_gain, ln_bias, merge_up, merge_up_bias, merge_down, merge_down_bias, row_owner, text_embed, doc_ids, rms_gain, w_query, query_bias, w_keyval, keyval_bias):
    pixels = patch_rows.astype(jnp.float32)
    center = pixels - lax.optimization_barrier(jnp.mean(pixels, axis=-1, keepdims=True))
    spread = lax.optimization_barrier(jnp.mean(center * center, axis=-1, keepdims=True))
    normed_patch = (center * lax.rsqrt(spread + 1e-06) * ln_gain + ln_bias).astype(jnp.bfloat16)
    merged = normed_patch.reshape(OWNERS * M_DEV, 4 * VIS_WIDTH)
    hidden = jax.nn.gelu(jnp.dot(merged, merge_up, preferred_element_type=jnp.float32) + merge_up_bias, approximate=False).astype(jnp.bfloat16)
    vision = (jnp.dot(hidden, merge_down, preferred_element_type=jnp.float32) + merge_down_bias).astype(jnp.bfloat16)
    owner = row_owner[:, 0]
    onehot = (owner[:, None] == jnp.arange(OWNERS, dtype=jnp.int32)[None, :]).astype(jnp.int32)
    ranks = lax.optimization_barrier(jnp.sum((jnp.cumsum(onehot, axis=0) - onehot) * onehot, axis=1)).astype(jnp.int32)
    sequence = text_embed.at[owner, ranks].set(vision)
    seq_f = sequence.astype(jnp.float32)
    normed_seq = (seq_f * lax.rsqrt(lax.optimization_barrier(jnp.mean(seq_f * seq_f, axis=-1, keepdims=True)) + 1e-06) * rms_gain).astype(jnp.bfloat16)
    flat = normed_seq.reshape(TOKENS, D)
    queries = (jnp.dot(flat, w_query, preferred_element_type=jnp.float32) + query_bias).astype(jnp.bfloat16)
    queries = queries.reshape(OWNERS, S_DEV, HEADS, HEAD_DIM)
    keyval = jnp.dot(flat, w_keyval.reshape(D, 2 * KV_HEADS * HEAD_DIM), preferred_element_type=jnp.float32) + keyval_bias.reshape(2 * KV_HEADS * HEAD_DIM)
    keyval = keyval.astype(jnp.bfloat16).reshape(OWNERS, S_DEV, 2, HEAD_DIM, KV_HEADS)
    keyval = jnp.transpose(keyval, (0, 1, 2, 4, 3))
    return lax.map(attend_owner, (queries, keyval, doc_ids))
```

```python
import functools
import math

import jax
import jax.numpy as jnp
from jax import lax
from jax.experimental import pallas as pl
from jax.experimental.pallas import tpu as pltpu
from jax.sharding import PartitionSpec as P

HEADS = 64
KV_HEADS = 8
HEAD_DIM = 128
DOC_MAX = 64

BF16 = jnp.bfloat16
F32 = jnp.float32
VMEM = pl.BlockSpec(memory_space=pltpu.VMEM)
SMEM = pl.BlockSpec(memory_space=pltpu.SMEM)
ANY = pl.BlockSpec(memory_space=pl.ANY)
MIB = 1 << 20


def dot(a, b):
    return jnp.dot(a, b, preferred_element_type=F32)


def params(mib):
    return pltpu.CompilerParams(vmem_limit_bytes=mib * MIB)


def cost(flops, nbytes):
    return pl.CostEstimate(flops=flops, bytes_accessed=nbytes, transcendentals=0)


def rms_scale(x, width):
    return lax.rsqrt(jnp.sum(x * x, axis=-1, keepdims=True) / width + 1e-06)


def merger_kernel(
    where, patch, gain, bias, up, up_bias, down, down_bias, send, keep,
    normed, merged, up_buf, down_buf, bias_row, up_sem, down_sem,
):
    up_parts, down_parts = up_buf.shape[0], down_buf.shape[0]
    step = up_buf.shape[1]
    width = down_buf.shape[2]
    half = send.shape[1]
    per_half = half // width
    mp = where[0]
    mine = mp % 2

    def up_copy(i):
        return pltpu.make_async_copy(up.at[pl.ds(i * step, step)], up_buf.at[i], up_sem.at[i])

    def down_copy(i):
        first = (1 - mine) if i < per_half else mine
        column = pl.multiple_of(first * half + (i % per_half) * width, 128)
        return pltpu.make_async_copy(down.at[:, pl.ds(column, width)], down_buf.at[i], down_sem.at[i])

    for i in range(up_parts):
        up_copy(i).start()
    for i in range(down_parts):
        down_copy(i).start()

    pixels = patch[...].astype(F32)
    features = pixels.shape[1]
    center = pixels - jnp.mean(pixels, axis=-1, keepdims=True)
    spread = jnp.mean(center * center, axis=-1, keepdims=True)
    patches = center * lax.rsqrt(spread + 1e-06) * gain[...] + bias[...]
    rows = send.shape[0]
    joined = patch.shape[0] // rows
    for c in range(features // 128):
        normed[c] = patches[:, c * 128 : (c + 1) * 128]
        for j in range(joined):
            merged[:, pl.ds(j * features + c * 128, 128)] = normed[c, pl.ds(j, rows, stride=joined), :].astype(BF16)
    bias_row[...] = jnp.zeros_like(bias_row)
    own = down_bias.shape[1]
    bias_row[:, pl.ds(pl.multiple_of(mp * own, 128), own)] = down_bias[...]

    total = jnp.zeros((rows, up.shape[1]), F32)
    for i in range(up_parts):
        up_copy(i).wait()
        total = total + dot(merged[:, pl.ds(i * step, step)], up_buf[i])
    total = total + up_bias[...]
    hidden = (0.5 * total * (1.0 + lax.erf(total * math.sqrt(0.5)))).astype(BF16)
    for i in range(down_parts):
        first = (1 - mine) if i < per_half else mine
        column = (i % per_half) * width
        out = send if i < per_half else keep
        add = bias_row[:, pl.ds(pl.multiple_of(first * half + column, 128), width)]
        down_copy(i).wait()
        out[:, pl.ds(column, width)] = (dot(hidden, down_buf[i]) + add).astype(BF16)


def merger(where, patch, gain, bias, up, up_bias, down, down_bias, rows):
    features = patch.shape[1]
    depth, hidden = up.shape
    columns = down.shape[1]
    step = features // 2
    width = columns // 8
    return pl.pallas_call(
        merger_kernel,
        out_shape=[jax.ShapeDtypeStruct((rows, columns // 2), BF16)] * 2,
        in_specs=[SMEM, VMEM, VMEM, VMEM, ANY, VMEM, ANY, VMEM],
        out_specs=[VMEM, VMEM],
        scratch_shapes=[
            pltpu.VMEM((features // 128, patch.shape[0], 128), F32),
            pltpu.VMEM((rows, depth), BF16),
            pltpu.VMEM((depth // step, step, hidden), BF16),
            pltpu.VMEM((8, hidden, width), BF16),
            pltpu.VMEM((1, columns), F32),
            pltpu.SemaphoreType.DMA((depth // step,)),
            pltpu.SemaphoreType.DMA((8,)),
        ],
        compiler_params=params(44),
        cost_estimate=cost(2 * rows * hidden * (depth + columns), 2 * hidden * (depth + columns)),
        name="merger",
    )(where, patch, gain, bias, up, up_bias, down, down_bias)


def text_norm_kernel(text, gain, out):
    x = text[...].astype(F32)
    out[...] = (x * rms_scale(x, x.shape[1]) * gain[...]).astype(BF16)


def text_norm(text, gain):
    rows, width = text.shape
    block = 32
    return pl.pallas_call(
        text_norm_kernel,
        out_shape=jax.ShapeDtypeStruct((rows, width), BF16),
        grid=(rows // block,),
        in_specs=[pl.BlockSpec((block, width), lambda i: (i, 0)), pl.BlockSpec((1, width), lambda i: (0, 0))],
        out_specs=pl.BlockSpec((block, width), lambda i: (i, 0)),
        compiler_params=params(12),
        cost_estimate=cost(4 * rows * width, 4 * rows * width),
        name="text_norm",
    )(text, gain)


def keyval_kernel(where, text, own, sibling, gain, weight, bias, image, *rest):
    parts = rest[:-3]
    rows_all, buf, sem = rest[-3:]
    steps = buf.shape[0]
    depth = weight.shape[1]
    step = depth // (steps // 2)
    copies = []
    for i in range(steps):
        t, k = i % 2, (i // 2) * step
        copies.append(pltpu.make_async_copy(weight.at[t, pl.ds(k, step)], buf.at[i], sem.at[i]))
        copies[-1].start()
    mp = where[0]
    half = own.shape[1]
    texts, images = text.shape[0], own.shape[0]
    mine = mp % 2
    first, second = own[...].astype(F32), sibling[...].astype(F32)
    squares = jnp.sum(first * first, axis=-1, keepdims=True) + jnp.sum(second * second, axis=-1, keepdims=True)
    scale = lax.rsqrt(squares / (2 * half) + 1e-06)
    for values, which in ((first, mine), (second, 1 - mine)):
        here = pl.ds(pl.multiple_of(which * half, 128), half)
        image[:, here] = (values * scale * gain[:, here]).astype(BF16)
    rows_all[pl.ds(0, texts), :] = text[...]
    rows_all[pl.ds(texts, images), :] = image[...]
    columns = weight.shape[2]
    totals = [jnp.zeros((texts + images, columns), F32)] * 2
    for i in range(steps):
        t, k = i % 2, (i // 2) * step
        copies[i].wait()
        totals[t] = totals[t] + dot(rows_all[:, pl.ds(k, step)], buf[i])
    keyval = [(totals[t] + bias[pl.ds(t, 1), :]).astype(BF16) for t in range(2)]
    count = len(parts)
    width = parts[0].shape[1]
    heads = KV_HEADS // count
    coords = columns // KV_HEADS
    row = lax.broadcasted_iota(jnp.int32, (columns, width // 2), 0)
    column = lax.broadcasted_iota(jnp.int32, (columns, width // 2), 1)
    for x in range(count):
        head = (mp ^ x) * heads + column // coords
        pick = (row == (column % coords) * KV_HEADS + head).astype(BF16)
        for t in range(2):
            parts[x][:, pl.ds(t * (width // 2), width // 2)] = dot(keyval[t], pick).astype(BF16)


def keyval_parts(where, text, own, sibling, gain, weight, bias, count):
    texts, depth = text.shape
    images = own.shape[0]
    columns = weight.shape[2]
    rows = texts + images
    steps = 8
    width = 2 * columns // count
    outs = pl.pallas_call(
        keyval_kernel,
        out_shape=[jax.ShapeDtypeStruct((images, depth), BF16)]
        + [jax.ShapeDtypeStruct((rows, width), BF16)] * count,
        in_specs=[SMEM, VMEM, VMEM, VMEM, VMEM, ANY, VMEM],
        out_specs=[VMEM] * (1 + count),
        scratch_shapes=[
            pltpu.VMEM((rows, depth), BF16),
            pltpu.VMEM((steps, depth // (steps // 2), columns), BF16),
            pltpu.SemaphoreType.DMA((steps,)),
        ],
        compiler_params=params(32),
        cost_estimate=cost(4 * rows * depth * columns, 4 * depth * columns),
        name="keyval",
    )(where, text, own, sibling, gain, weight, bias)
    return outs[0], outs[1:]


def query_kernel(text, image, weight, bias, text_out, image_out, rows_all, buf, sem):
    steps = buf.shape[0]
    width = buf.shape[2]
    copies = []
    for i in range(steps):
        copies.append(pltpu.make_async_copy(weight.at[:, pl.ds(i * width, width)], buf.at[i], sem.at[i]))
        copies[-1].start()
    texts, images = text.shape[0], image.shape[0]
    rows_all[pl.ds(0, texts), :] = text[...]
    rows_all[pl.ds(texts, images), :] = image[...]
    for i in range(steps):
        here = pl.ds(i * width, width)
        copies[i].wait()
        out = (dot(rows_all[...], buf[i]) + bias[:, here]).astype(BF16)
        text_out[:, here] = out[:texts]
        image_out[:, here] = out[texts:]


def query_rows(text, image, weight, bias):
    texts, depth = text.shape
    images = image.shape[0]
    columns = weight.shape[1]
    steps = columns // 256
    return pl.pallas_call(
        query_kernel,
        out_shape=[jax.ShapeDtypeStruct((texts, columns), BF16), jax.ShapeDtypeStruct((images, columns), BF16)],
        in_specs=[VMEM, VMEM, ANY, VMEM],
        out_specs=[VMEM, VMEM],
        scratch_shapes=[
            pltpu.VMEM((texts + images, depth), BF16),
            pltpu.VMEM((steps, depth, columns // steps), BF16),
            pltpu.SemaphoreType.DMA((steps,)),
        ],
        compiler_params=params(52),
        cost_estimate=cost(2 * (texts + images) * depth * columns, 2 * depth * columns),
        name="query",
    )(text, image, weight, bias)


def join_parts(mp, parts, first_row, rows):
    count = len(parts)
    width = parts[0].shape[1]
    heads = KV_HEADS // count
    coords = HEAD_DIM // count
    full = 2 * heads * HEAD_DIM
    row = lax.broadcasted_iota(jnp.int32, (width, full), 0)
    column = lax.broadcasted_iota(jnp.int32, (width, full), 1)
    total = jnp.zeros((rows, full), F32)
    for x in range(count):
        coordinate = (mp ^ x) * coords + row % coords
        place = (column == (row // coords) * HEAD_DIM + coordinate).astype(BF16)
        total = total + dot(parts[x][pl.ds(first_row, rows), :], place)
    return total.astype(BF16)


def slots_kernel(where, owner_rows, owner_columns, queries, *rest):
    parts, out = rest[:-1], rest[-1]
    owners = owner_rows.shape[0]
    rows, columns = queries.shape
    slots = out.shape[0]
    mp, me = where[0], where[1]
    down = owner_columns[pl.ds(pl.multiple_of(me * rows, rows), rows), :]
    across = owner_rows[pl.ds(me, 1), :]
    earlier = lax.broadcasted_iota(jnp.int32, (rows, rows), 0) < lax.broadcasted_iota(jnp.int32, (rows, rows), 1)
    rank = jnp.sum(jnp.where((down == across) & earlier, 1, 0), axis=0, keepdims=True)
    slot = across * (slots // owners) + rank
    select = (lax.broadcasted_iota(jnp.int32, (slots, rows), 0) == slot).astype(F32).astype(BF16)
    out[:, pl.ds(0, columns)] = dot(select, queries[...]).astype(BF16)
    keyval = join_parts(mp, parts, parts[0].shape[0] - rows, rows)
    out[:, pl.ds(columns, out.shape[1] - columns)] = dot(select, keyval).astype(BF16)


def slots_of(where, owner_rows, owner_columns, queries, parts, capacity):
    slots = owner_rows.shape[0] * capacity
    width = queries.shape[1] + 2 * (KV_HEADS // len(parts)) * HEAD_DIM
    return pl.pallas_call(
        slots_kernel,
        out_shape=jax.ShapeDtypeStruct((slots, width), BF16),
        in_specs=[SMEM] + [VMEM] * (3 + len(parts)),
        out_specs=VMEM,
        compiler_params=params(12),
        name="slots",
    )(where, owner_rows, owner_columns, queries, *parts)


def attention_kernel(where, owner_rows, doc_row, doc_column, queries, arrived, *rest):
    parts = rest[:-4]
    out, q_all, kv_all, window = rest[-4:]
    mp, me = where[0], where[1]
    seq = queries.shape[0]
    columns = queries.shape[1]
    slots = arrived.shape[0]
    owners = owner_rows.shape[0]
    capacity = slots // owners
    incoming = jnp.sum(jnp.where(owner_rows[...] == me, 1, 0), axis=1, keepdims=True)
    source = lax.broadcasted_iota(jnp.int32, (owners, slots), 0)
    slot = lax.broadcasted_iota(jnp.int32, (owners, slots), 1)
    offset = jnp.sum(jnp.where(source < slot // capacity, incoming, 0), axis=0, keepdims=True)
    here = jnp.sum(jnp.where(source == slot // capacity, incoming, 0), axis=0, keepdims=True)
    index = lax.broadcasted_iota(jnp.int32, (1, slots), 1) % capacity
    target = jnp.where(index < here, offset + index, -1)
    position = lax.broadcasted_iota(jnp.int32, (slots, slots), 0)
    place = (position == target).astype(F32).astype(BF16)
    placed = dot(place, arrived[...]).astype(BF16)
    count = jnp.sum(incoming, axis=0, keepdims=True)
    is_image = lax.broadcasted_iota(jnp.int32, (slots, 1), 0) < count

    keyval = join_parts(mp, parts, 0, seq)
    kv_all[...] = keyval
    kv_all[pl.ds(0, slots), :] = jnp.where(is_image, placed[:, columns:], keyval[:slots])
    q_all[...] = queries[...]
    q_all[pl.ds(0, slots), :] = jnp.where(is_image, placed[:, :columns], queries[pl.ds(0, slots), :])

    heads = columns // HEAD_DIM
    groups = kv_all.shape[1] // (2 * HEAD_DIM)
    shared = heads // groups
    block = DOC_MAX
    scale = 1.0 / math.sqrt(HEAD_DIM)
    for b in range(seq // block):
        q0 = b * block
        k0 = max(0, q0 - block)
        q_doc = doc_column[pl.ds(q0, block), :]
        k_doc = doc_row[:, pl.ds((k0 // 128) * 128, 128)] if k0 % 128 == 0 else window[pl.ds(b, 1), :]
        q_pos = q0 + lax.broadcasted_iota(jnp.int32, (block, 2 * block), 0)
        k_pos = k0 + lax.broadcasted_iota(jnp.int32, (block, 2 * block), 1)
        allowed = (q_doc == k_doc) & (k_pos <= q_pos)
        allowed = jnp.concatenate([allowed.astype(jnp.int32)] * shared, axis=0) > 0
        for g in range(groups):
            keys = kv_all[pl.ds(k0, 2 * block), pl.ds(g * HEAD_DIM, HEAD_DIM)]
            values = kv_all[pl.ds(k0, 2 * block), pl.ds((groups + g) * HEAD_DIM, HEAD_DIM)]
            q = jnp.concatenate(
                [q_all[pl.ds(q0, block), pl.ds((g * shared + h) * HEAD_DIM, HEAD_DIM)] for h in range(shared)], axis=0
            )
            scores = lax.dot_general(q, keys, (((1,), (1,)), ((), ())), preferred_element_type=F32) * scale
            scores = jnp.where(allowed, scores, F32(-1e30))
            weights = jnp.exp(scores - jnp.max(scores, axis=-1, keepdims=True))
            probs = (weights / jnp.sum(weights, axis=-1, keepdims=True)).astype(BF16)
            result = dot(probs, values).astype(BF16)
            for h in range(shared):
                out[pl.ds(q0, block), pl.ds((g * shared + h) * HEAD_DIM, HEAD_DIM)] = result[h * block : (h + 1) * block]


def attention(where, owner_rows, documents, queries, arrived, parts):
    seq, columns = queries.shape
    width = 2 * (KV_HEADS // len(parts)) * HEAD_DIM

    def body(where, owner_rows, doc_row, doc_column, doc_windows, *rest):
        attention_kernel(where, owner_rows, doc_row, doc_column, *rest, doc_windows)

    blocks = seq // DOC_MAX
    windows = jnp.stack([documents[max(0, b - 1) * DOC_MAX :][: 2 * DOC_MAX] for b in range(blocks)])
    return pl.pallas_call(
        body,
        out_shape=jax.ShapeDtypeStruct((seq, columns), BF16),
        in_specs=[SMEM] + [VMEM] * (6 + len(parts)),
        out_specs=VMEM,
        scratch_shapes=[pltpu.VMEM((seq, columns), BF16), pltpu.VMEM((seq, width), BF16)],
        compiler_params=params(24),
        name="attention",
    )(where, owner_rows, documents[None, :], documents[:, None], windows, queries, arrived, *parts)


def exchange(x, count, bit):
    return lax.ppermute(x, "mp", [(i, i ^ bit) for i in range(count)])


def per_device(
    patch_rows,
    ln_gain,
    ln_bias,
    merge_up,
    merge_up_bias,
    merge_down,
    merge_down_bias,
    row_owner,
    text_embed,
    doc_ids,
    rms_gain,
    w_query,
    query_bias,
    w_keyval,
    keyval_bias,
):
    owners = lax.axis_size(("group", "dp"))
    count = lax.axis_size("mp")
    mp_index = lax.axis_index("mp")
    where = jnp.stack([mp_index, lax.axis_index(("group", "dp"))]).astype(jnp.int32)
    rows = row_owner.shape[0] // owners
    capacity = max(2, 2 * rows // owners)
    gain = rms_gain[None, :]
    owner_rows = row_owner.reshape(owners, rows)

    send, keep = merger(
        where, patch_rows[0], ln_gain[None, :], ln_bias[None, :], merge_up, merge_up_bias[None, :],
        merge_down, merge_down_bias[None, :], rows,
    )
    text = text_norm(text_embed[0], gain)
    weight = jnp.transpose(w_keyval, (1, 0, 2))

    own = (keep.astype(F32) + exchange(send, count, 1).astype(F32)).astype(BF16)
    bit = 2
    while bit < count:
        own = (own.astype(F32) + exchange(own, count, bit).astype(F32)).astype(BF16)
        bit *= 2
    sibling = exchange(own, count, 1)

    image, parts = keyval_parts(where, text, own, sibling, gain, weight, keyval_bias, count)
    parts = [parts[0]] + [exchange(parts[x], count, x) for x in range(1, count)]
    text_queries, image_queries = query_rows(text, image, w_query, query_bias[None, :])
    outgoing = slots_of(where, owner_rows, row_owner, image_queries, parts, capacity)
    arrived = lax.all_to_all(
        outgoing.reshape(owners, capacity, -1), ("group", "dp"), split_axis=0, concat_axis=0, tiled=True
    ).reshape(owners * capacity, -1)
    return attention(where, owner_rows, doc_ids[0], text_queries, arrived, parts)[None]


def general(
    patch_rows,
    ln_gain,
    ln_bias,
    merge_up,
    merge_up_bias,
    merge_down,
    merge_down_bias,
    row_owner,
    text_embed,
    doc_ids,
    rms_gain,
    w_query,
    query_bias,
    w_keyval,
    keyval_bias,
):
    owners = lax.axis_size(("group", "dp"))
    own_index = lax.axis_index(("group", "dp"))
    mp_index = lax.axis_index("mp")
    pixels = patch_rows[0].astype(jnp.float32)
    center = pixels - jnp.mean(pixels, axis=-1, keepdims=True)
    spread = jnp.mean(center * center, axis=-1, keepdims=True)
    normed_patch = (center * lax.rsqrt(spread + 1e-06) * ln_gain + ln_bias).astype(jnp.bfloat16)
    merged = normed_patch.reshape(-1, 4 * pixels.shape[1])
    merged_rows = merged.shape[0]
    hidden = jax.nn.gelu(
        jnp.dot(merged, merge_up, preferred_element_type=jnp.float32) + merge_up_bias,
        approximate=False,
    ).astype(jnp.bfloat16)
    partial_sum = jnp.dot(hidden, merge_down, preferred_element_type=jnp.float32)
    vision = (
        lax.psum_scatter(partial_sum, "mp", scatter_dimension=1, tiled=True) + merge_down_bias
    ).astype(jnp.bfloat16)
    col_width = vision.shape[1]
    capacity = max(2, 2 * merged_rows // owners)
    owner_all = row_owner[:, 0]
    owner_ids = jnp.arange(owners, dtype=jnp.int32)
    onehot = (owner_all[:, None] == owner_ids[None, :]).astype(jnp.int32)
    per_source = jnp.sum(onehot.reshape(owners, merged_rows, owners), axis=1)
    my_block = lax.dynamic_slice_in_dim(onehot, own_index * merged_rows, merged_rows, 0)
    block_rank = jnp.sum((jnp.cumsum(my_block, axis=0) - my_block) * my_block, axis=1)
    my_owner = jnp.sum(my_block * owner_ids[None, :], axis=1)
    slot_id = my_owner * capacity + block_rank
    all_slots = jnp.arange(owners * capacity, dtype=jnp.int32)
    select = (slot_id[:, None] == all_slots[None, :]).astype(jnp.bfloat16)
    outgoing = jnp.einsum("ms,mc->sc", select, vision, preferred_element_type=jnp.float32).astype(
        jnp.bfloat16
    )
    arrived = lax.all_to_all(
        outgoing.reshape(owners, capacity, col_width),
        ("group", "dp"),
        split_axis=0,
        concat_axis=0,
        tiled=True,
    )
    arrived = arrived.reshape(owners * capacity, col_width)
    incoming = lax.dynamic_slice_in_dim(per_source, own_index, 1, 1)[:, 0]
    offsets = jnp.cumsum(incoming) - incoming
    total = jnp.sum(incoming)
    slot_rank = jnp.arange(capacity, dtype=jnp.int32)
    target = jnp.where(
        slot_rank[None, :] < incoming[:, None], offsets[:, None] + slot_rank[None, :], -1
    ).reshape(-1)
    text_rows = text_embed[0]
    seq_len = text_rows.shape[0]
    positions = jnp.arange(seq_len, dtype=jnp.int32)
    source_slot = jnp.sum(
        jnp.where(target[:, None] == positions[None, :], all_slots[:, None], 0), axis=0
    )
    is_image = (positions < total)[:, None]
    image_full = lax.all_gather(arrived, "mp", axis=1, tiled=True)
    sequence = jnp.where(is_image, jnp.take(image_full, source_slot, axis=0), text_rows)
    seq_f = sequence.astype(jnp.float32)
    normed_seq = (
        seq_f * lax.rsqrt(jnp.mean(seq_f * seq_f, axis=-1, keepdims=True) + 1e-06) * rms_gain
    ).astype(jnp.bfloat16)
    queries = (
        jnp.dot(normed_seq, w_query, preferred_element_type=jnp.float32) + query_bias
    ).astype(jnp.bfloat16)
    keyval_local = (
        jnp.einsum("sd,dtc->stc", normed_seq, w_keyval, preferred_element_type=jnp.float32)
        + keyval_bias
    ).astype(jnp.bfloat16)
    keyval_full = lax.all_gather(keyval_local, "mp", axis=2, tiled=True)
    keyval_heads = jnp.transpose(keyval_full.reshape(seq_len, 2, HEAD_DIM, KV_HEADS), (0, 1, 3, 2))
    local_heads = queries.shape[1] // HEAD_DIM
    group_size = HEADS // KV_HEADS
    kv_index = (mp_index * local_heads + jnp.arange(local_heads, dtype=jnp.int32)) // group_size
    keys = jnp.take(keyval_heads[:, 0], kv_index, axis=1)
    values = jnp.take(keyval_heads[:, 1], kv_index, axis=1)
    query_heads = queries.reshape(seq_len, local_heads, HEAD_DIM)
    scores = jnp.einsum(
        "qhd,khd->hqk", query_heads, keys, preferred_element_type=jnp.float32
    ) / math.sqrt(HEAD_DIM)
    documents = doc_ids[0]
    allowed = (documents[:, None] == documents[None, :]) & (
        positions[None, :] <= positions[:, None]
    )
    scores = jnp.where(allowed[None], scores, jnp.float32(-1e30))
    highest = jnp.max(scores, axis=-1, keepdims=True)
    weights = jnp.exp(scores - highest)
    probs = (weights / jnp.sum(weights, axis=-1, keepdims=True)).astype(jnp.bfloat16)
    output = jnp.einsum("hqk,khd->qhd", probs, values, preferred_element_type=jnp.float32)
    return output.astype(jnp.bfloat16).reshape(1, seq_len, local_heads * HEAD_DIM)


def solution(mesh):
    in_specs = (
        P(("group", "dp"), None, None),
        P(),
        P(),
        P(None, "mp"),
        P("mp"),
        P("mp", None),
        P("mp"),
        P(),
        P(("group", "dp"), None, None),
        P(("group", "dp"), None),
        P(),
        P(None, "mp"),
        P("mp"),
        P(None, None, "mp"),
        P(None, "mp"),
    )
    out_specs = P(("group", "dp"), None, "mp")
    count = mesh.shape["mp"]
    narrow = count < 2 or count > KV_HEADS or count & (count - 1)
    body = general if narrow else per_device
    return jax.shard_map(body, mesh=mesh, in_specs=in_specs, out_specs=out_specs, check_vma=False)
```

```python
import functools
import math

import jax
import jax.numpy as jnp
from jax import lax
from jax.experimental import pallas as pl
from jax.experimental.pallas import tpu as pltpu
from jax.sharding import PartitionSpec as P

HEADS = 64
KV_HEADS = 8
HEAD_DIM = 128
DOC_MAX = 64

BF16 = jnp.bfloat16
F32 = jnp.float32
VMEM = pl.BlockSpec(memory_space=pltpu.VMEM)
SMEM = pl.BlockSpec(memory_space=pltpu.SMEM)
ANY = pl.BlockSpec(memory_space=pl.ANY)
HBM = pl.BlockSpec(memory_space=pltpu.HBM)
AHEAD = 3
MIB = 1 << 20


def dot(a, b):
    return jnp.dot(a, b, preferred_element_type=F32)


def in_hbm(x):
    return pltpu.with_memory_space_constraint(x, pltpu.HBM)


def in_vmem(x):
    return pltpu.with_memory_space_constraint(x, pltpu.VMEM)


def params(mib):
    return pltpu.CompilerParams(vmem_limit_bytes=mib * MIB)


def cost(flops, nbytes):
    return pl.CostEstimate(flops=flops, bytes_accessed=nbytes, transcendentals=0)


def rms_scale(x, width):
    return lax.rsqrt(jnp.sum(x * x, axis=-1, keepdims=True) / width + 1e-06)


def stream(count, copy, body, then=None):
    @pl.loop(0, count)
    def _(i):
        copy(i).wait()

        @pl.when(i + AHEAD < count)
        def _():
            copy(i + AHEAD).start()

        if then is not None:

            @pl.when(i + AHEAD >= count)
            def _():
                then(i + AHEAD - count).start()

        body(i)


def begin(copy):
    for i in range(AHEAD):
        copy(i).start()


def tile(i, width):
    return pl.ds(pl.multiple_of(i * width, width), width)


def merger_kernel(
    where, patch_in, gain_in, bias_in, up, up_bias_in, down, down_bias_in, send, keep,
    patch, gain, bias, up_bias, down_bias, bias_row, normed, merged, total, up_buf, down_buf, small_sem, up_sem, down_sem,
):
    slots = AHEAD + 1
    step = up_buf.shape[1]
    width = down_buf.shape[2]
    half = send.shape[1]
    per_half = half // width
    mp = where[0]
    mine = mp % 2
    pairs = [(patch_in, patch), (gain_in, gain), (bias_in, bias), (up_bias_in, up_bias), (down_bias_in, down_bias)]
    small = [pltpu.make_async_copy(x, y, small_sem.at[i]) for i, (x, y) in enumerate(pairs)]
    for copy in small:
        copy.start()

    def up_copy(i):
        return pltpu.make_async_copy(up.at[tile(i, step)], up_buf.at[i % slots], up_sem.at[i % slots])

    def column(i):
        first = jnp.where(i < per_half, 1 - mine, mine)
        return pl.multiple_of(first * half + (i % per_half) * width, width)

    def down_copy(i):
        return pltpu.make_async_copy(
            down.at[:, pl.ds(column(i), width)], down_buf.at[i % slots], down_sem.at[i % slots]
        )

    begin(up_copy)
    for copy in small:
        copy.wait()
    rows = send.shape[0]
    joined = patch.shape[0] // rows
    features = patch.shape[1]
    pixels = patch[...].astype(F32)
    center = pixels - jnp.mean(pixels, axis=-1, keepdims=True)
    spread = jnp.mean(center * center, axis=-1, keepdims=True)
    patches = center * lax.rsqrt(spread + 1e-06) * gain[...][None, :] + bias[...][None, :]
    for c in range(features // 128):
        normed[c] = patches[:, c * 128 : (c + 1) * 128]
        for j in range(joined):
            merged[:, pl.ds(j * features + c * 128, 128)] = normed[c, pl.ds(j, rows, stride=joined), :].astype(BF16)
    own = down_bias.shape[0]
    bias_row[...] = jnp.zeros_like(bias_row)
    bias_row[:, pl.ds(pl.multiple_of(mp * own, 128), own)] = down_bias[...][None, :]
    total[...] = jnp.broadcast_to(up_bias[...][None, :], total.shape)

    def up_body(i):
        total[...] += dot(merged[:, tile(i, step)], up_buf[i % slots])

    stream(up.shape[0] // step, up_copy, up_body, down_copy)
    sums = total[...]
    hidden = (0.5 * sums * (1.0 + lax.erf(sums * math.sqrt(0.5)))).astype(BF16)

    def down_body(i):
        part = (dot(hidden, down_buf[i % slots]) + bias_row[:, pl.ds(column(i), width)]).astype(BF16)
        here = tile(i % per_half, width)

        @pl.when(i < per_half)
        def _():
            send[:, here] = part

        @pl.when(i >= per_half)
        def _():
            keep[:, here] = part

    stream(2 * per_half, down_copy, down_body)


def merger(where, patch, gain, bias, up, up_bias, down, down_bias, rows):
    features = patch.shape[1]
    depth, hidden = up.shape
    columns = down.shape[1]
    step = depth // 8
    width = columns // 8
    slots = AHEAD + 1
    return pl.pallas_call(
        merger_kernel,
        out_shape=[jax.ShapeDtypeStruct((rows, columns // 2), BF16)] * 2,
        in_specs=[SMEM] + [HBM] * 7,
        out_specs=[VMEM, VMEM],
        scratch_shapes=[
            pltpu.VMEM(patch.shape, BF16),
            pltpu.VMEM(gain.shape, F32),
            pltpu.VMEM(bias.shape, F32),
            pltpu.VMEM(up_bias.shape, F32),
            pltpu.VMEM(down_bias.shape, F32),
            pltpu.VMEM((1, columns), F32),
            pltpu.VMEM((features // 128, patch.shape[0], 128), F32),
            pltpu.VMEM((rows, depth), BF16),
            pltpu.VMEM((rows, hidden), F32),
            pltpu.VMEM((slots, step, hidden), BF16),
            pltpu.VMEM((slots, hidden, width), BF16),
            pltpu.SemaphoreType.DMA((5,)),
            pltpu.SemaphoreType.DMA((slots,)),
            pltpu.SemaphoreType.DMA((slots,)),
        ],
        compiler_params=params(28),
        cost_estimate=cost(2 * rows * hidden * (depth + columns), 2 * hidden * (depth + columns)),
        name="merger",
    )(where, *map(in_hbm, (patch, gain, bias, up, up_bias, down, down_bias)))


def keyval_kernel(where, text, own, sibling, gain, weight, bias, rows_all, *rest):
    parts = rest[:-5]
    buf, keyval, text_buf, sem, text_sem = rest[-5:]
    slots = AHEAD + 1
    block = text_buf.shape[1]
    texts, images = text.shape[0], own.shape[0]

    def text_copy(i):
        return pltpu.make_async_copy(text.at[tile(i, block)], text_buf.at[i % slots], text_sem.at[i % slots])

    def weight_copy(i):
        return pltpu.make_async_copy(weight.at[i], buf.at[i], sem.at[i])

    begin(text_copy)
    for i in range(2):
        weight_copy(i).start()
    mp = where[0]
    half = own.shape[1]
    mine = mp % 2
    first, second = own[...].astype(F32), sibling[...].astype(F32)
    squares = jnp.sum(first * first, axis=-1, keepdims=True) + jnp.sum(second * second, axis=-1, keepdims=True)
    scale = lax.rsqrt(squares / (2 * half) + 1e-06)
    for values, which in ((first, mine), (second, 1 - mine)):
        here = pl.ds(pl.multiple_of(which * half, half), half)
        rows_all[pl.ds(texts, images), here] = (values * scale * gain[:, here]).astype(BF16)

    def text_body(i):
        x = text_buf[i % slots].astype(F32)
        rows_all[tile(i, block), :] = (x * rms_scale(x, 2 * half) * gain[...]).astype(BF16)

    stream(texts // block, text_copy, text_body)

    @pl.loop(0, 2)
    def _(t):
        weight_copy(t).wait()
        keyval[t] = (dot(rows_all[...], buf[t]) + bias[pl.ds(t, 1), :]).astype(BF16)

    count = len(parts)
    columns = weight.shape[2]
    width = parts[0].shape[1]
    heads = KV_HEADS // count
    coords = columns // KV_HEADS
    row = lax.broadcasted_iota(jnp.int32, (columns, width // 2), 0)
    column = lax.broadcasted_iota(jnp.int32, (columns, width // 2), 1)
    for x in range(count):
        head = (mp ^ x) * heads + column // coords
        pick = (row == (column % coords) * KV_HEADS + head).astype(F32).astype(BF16)
        for t in range(2):
            parts[x][:, pl.ds(t * (width // 2), width // 2)] = dot(keyval[t], pick).astype(BF16)


def keyval_parts(where, text, own, sibling, gain, weight, bias, count):
    texts, depth = text.shape
    columns = weight.shape[2]
    rows = texts + own.shape[0]
    width = 2 * columns // count
    outs = pl.pallas_call(
        keyval_kernel,
        out_shape=[pltpu.VMEM((rows, depth), BF16)] + [jax.ShapeDtypeStruct((rows, width), BF16)] * count,
        in_specs=[SMEM, HBM, VMEM, VMEM, VMEM, HBM, VMEM],
        out_specs=[VMEM] * (1 + count),
        scratch_shapes=[
            pltpu.VMEM((2, depth, columns), BF16),
            pltpu.VMEM((2, rows, columns), BF16),
            pltpu.VMEM((AHEAD + 1, 32, depth), BF16),
            pltpu.SemaphoreType.DMA((2,)),
            pltpu.SemaphoreType.DMA((AHEAD + 1,)),
        ],
        compiler_params=params(18),
        cost_estimate=cost(4 * rows * depth * columns, 4 * depth * columns),
        name="keyval",
    )(where, in_hbm(text), own, sibling, gain, in_hbm(weight), bias)
    return outs[0], outs[1:]


def query_kernel(rows_all, weight, bias, text_out, image_out, buf, sem):
    width = buf.shape[2]
    slots = AHEAD + 1
    texts = text_out.shape[0]

    def copy(i):
        return pltpu.make_async_copy(weight.at[:, tile(i, width)], buf.at[i % slots], sem.at[i % slots])

    def body(i):
        here = tile(i, width)
        out = (dot(rows_all[...], buf[i % slots]) + bias[:, here]).astype(BF16)
        text_out[:, here] = out[:texts]
        image_out[:, here] = out[texts:]

    begin(copy)
    stream(weight.shape[1] // width, copy, body)


def query_rows(rows_all, texts, weight, bias):
    depth = rows_all.shape[1]
    images = rows_all.shape[0] - texts
    columns = weight.shape[1]
    return pl.pallas_call(
        query_kernel,
        out_shape=[jax.ShapeDtypeStruct((texts, columns), BF16), jax.ShapeDtypeStruct((images, columns), BF16)],
        in_specs=[VMEM, HBM, VMEM],
        out_specs=[VMEM, VMEM],
        scratch_shapes=[pltpu.VMEM((AHEAD + 1, depth, 256), BF16), pltpu.SemaphoreType.DMA((AHEAD + 1,))],
        compiler_params=params(24),
        cost_estimate=cost(2 * (texts + images) * depth * columns, 2 * depth * columns),
        name="query",
    )(in_vmem(rows_all), in_hbm(weight), bias[None, :])


def join_parts(mp, parts, first_row, rows):
    count = len(parts)
    width = parts[0].shape[1]
    heads = KV_HEADS // count
    coords = HEAD_DIM // count
    full = 2 * heads * HEAD_DIM
    row = lax.broadcasted_iota(jnp.int32, (width, full), 0)
    column = lax.broadcasted_iota(jnp.int32, (width, full), 1)
    total = jnp.zeros((rows, full), F32)
    for x in range(count):
        coordinate = (mp ^ x) * coords + row % coords
        place = (column == (row // coords) * HEAD_DIM + coordinate).astype(BF16)
        total = total + dot(parts[x][pl.ds(first_row, rows), :], place)
    return total.astype(BF16)


def slots_kernel(where, owner_rows, owner_columns, queries, *rest):
    parts, out = rest[:-1], rest[-1]
    owners = owner_rows.shape[0]
    rows, columns = queries.shape
    slots = out.shape[0]
    mp, me = where[0], where[1]
    down = owner_columns[pl.ds(pl.multiple_of(me * rows, rows), rows), :]
    across = owner_rows[pl.ds(me, 1), :]
    earlier = lax.broadcasted_iota(jnp.int32, (rows, rows), 0) < lax.broadcasted_iota(jnp.int32, (rows, rows), 1)
    rank = jnp.sum(jnp.where((down == across) & earlier, 1, 0), axis=0, keepdims=True)
    slot = across * (slots // owners) + rank
    select = (lax.broadcasted_iota(jnp.int32, (slots, rows), 0) == slot).astype(F32).astype(BF16)
    out[:, pl.ds(0, columns)] = dot(select, queries[...]).astype(BF16)
    keyval = join_parts(mp, parts, parts[0].shape[0] - rows, rows)
    out[:, pl.ds(columns, out.shape[1] - columns)] = dot(select, keyval).astype(BF16)


def slots_of(where, owner_rows, owner_columns, queries, parts, capacity):
    slots = owner_rows.shape[0] * capacity
    width = queries.shape[1] + 2 * (KV_HEADS // len(parts)) * HEAD_DIM
    return pl.pallas_call(
        slots_kernel,
        out_shape=jax.ShapeDtypeStruct((slots, width), BF16),
        in_specs=[SMEM] + [VMEM] * (3 + len(parts)),
        out_specs=VMEM,
        compiler_params=params(12),
        name="slots",
    )(where, owner_rows, owner_columns, queries, *parts)


def attend(blocks, first, doc_column, windows, q_all, kv_all, out):
    q_first, k_first, out_first = first
    heads = q_all.shape[1] // HEAD_DIM
    groups = kv_all.shape[1] // (2 * HEAD_DIM)
    shared = heads // groups
    block = DOC_MAX
    scale = 1.0 / math.sqrt(HEAD_DIM)
    row = lax.broadcasted_iota(jnp.int32, (block, 2 * block), 0)
    column = lax.broadcasted_iota(jnp.int32, (block, 2 * block), 1)

    @pl.loop(blocks[0], blocks[1])
    def _(b):
        q0 = pl.multiple_of(b * block, block)
        k0 = pl.multiple_of(jnp.maximum(b - 1, 0) * block, block)
        allowed = (doc_column[pl.ds(q0, block), :] == windows[pl.ds(b, 1), :]) & (k0 + column <= q0 + row)
        penalty = jnp.concatenate([jnp.where(allowed, 0.0, -1e30)] * shared, axis=0)

        @pl.loop(0, groups)
        def _(g):
            keys = kv_all[pl.ds(k0 - k_first, 2 * block), tile(g, HEAD_DIM)]
            values = kv_all[pl.ds(k0 - k_first, 2 * block), tile(groups + g, HEAD_DIM)]
            columns = [tile(g * shared + h, HEAD_DIM) for h in range(shared)]
            q = jnp.concatenate([q_all[pl.ds(q0 - q_first, block), c] for c in columns], axis=0)
            scores = lax.dot_general(q, keys, (((1,), (1,)), ((), ())), preferred_element_type=F32) * scale
            scores = jnp.where(penalty < 0.0, penalty, scores)
            weights = jnp.exp(scores - jnp.max(scores, axis=-1, keepdims=True))
            probs = (weights / jnp.sum(weights, axis=-1, keepdims=True)).astype(BF16)
            result = dot(probs, values).astype(BF16)
            for h, c in enumerate(columns):
                out[pl.ds(q0 - out_first, block), c] = result[h * block : (h + 1) * block]


def late_kernel(early, where, doc_column, windows, queries, *rest):
    parts, out, kv_all = rest[:-2], rest[-2], rest[-1]
    seq = queries.shape[0]
    first = early - DOC_MAX
    kv_all[...] = join_parts(where[0], parts, first, seq - first)
    attend((early // DOC_MAX, seq // DOC_MAX), (0, first, 0), doc_column, windows, queries, kv_all, out)


def early_kernel(early, where, owner_rows, doc_column, windows, queries, arrived, *rest):
    parts = rest[:-6]
    _, out, q_all, kv_all, result, sem = rest[-6:]
    mp, me = where[0], where[1]
    columns = queries.shape[1]
    slots = arrived.shape[0]
    owners = owner_rows.shape[0]
    capacity = slots // owners
    incoming = jnp.sum(jnp.where(owner_rows[...] == me, 1, 0), axis=1, keepdims=True)
    source = lax.broadcasted_iota(jnp.int32, (owners, slots), 0)
    slot = lax.broadcasted_iota(jnp.int32, (owners, slots), 1)
    offset = jnp.sum(jnp.where(source < slot // capacity, incoming, 0), axis=0, keepdims=True)
    here = jnp.sum(jnp.where(source == slot // capacity, incoming, 0), axis=0, keepdims=True)
    index = lax.broadcasted_iota(jnp.int32, (1, slots), 1) % capacity
    target = jnp.where(index < here, offset + index, -1)
    position = lax.broadcasted_iota(jnp.int32, (slots, slots), 0)
    place = (position == target).astype(F32).astype(BF16)
    placed = dot(place, arrived[...]).astype(BF16)
    is_image = lax.broadcasted_iota(jnp.int32, (slots, 1), 0) < jnp.sum(incoming, axis=0, keepdims=True)

    keyval = join_parts(mp, parts, 0, early)
    kv_all[...] = keyval
    kv_all[pl.ds(0, slots), :] = jnp.where(is_image, placed[:, columns:], keyval[:slots])
    q_all[...] = queries[pl.ds(0, early), :]
    q_all[pl.ds(0, slots), :] = jnp.where(is_image, placed[:, :columns], queries[pl.ds(0, slots), :])
    attend((0, early // DOC_MAX), (0, 0, 0), doc_column, windows, q_all, kv_all, result)
    copy = pltpu.make_async_copy(result, out.at[pl.ds(0, early)], sem)
    copy.start()
    copy.wait()


def attention(where, owner_rows, documents, queries, parts, capacity):
    seq, columns = queries.shape
    width = 2 * (KV_HEADS // len(parts)) * HEAD_DIM
    slots = owner_rows.shape[0] * capacity
    early = min(seq, -(-slots // DOC_MAX) * DOC_MAX + DOC_MAX)
    windows = jnp.stack([documents[max(0, b - 1) * DOC_MAX :][: 2 * DOC_MAX] for b in range(seq // DOC_MAX)])
    docs = (documents[:, None], windows)
    shape = jax.ShapeDtypeStruct((seq, columns), BF16)

    def late(queries):
        return pl.pallas_call(
            functools.partial(late_kernel, early),
            out_shape=shape,
            in_specs=[SMEM] + [VMEM] * (3 + len(parts)),
            out_specs=VMEM,
            scratch_shapes=[pltpu.VMEM((seq - early + DOC_MAX, width), BF16)],
            compiler_params=params(16),
            cost_estimate=cost(4 * (seq - early) * columns * 2 * DOC_MAX, 4 * seq * columns),
            name="attention_late",
        )(where, *docs, queries, *parts)

    def final(arrived, before):
        return pl.pallas_call(
            functools.partial(early_kernel, early),
            out_shape=shape,
            in_specs=[SMEM] + [VMEM] * (5 + len(parts)) + [ANY],
            out_specs=ANY,
            scratch_shapes=[
                pltpu.VMEM((early, columns), BF16),
                pltpu.VMEM((early, width), BF16),
                pltpu.VMEM((early, columns), BF16),
                pltpu.SemaphoreType.DMA,
            ],
            input_output_aliases={6 + len(parts): 0},
            compiler_params=params(16),
            cost_estimate=cost(4 * early * columns * 2 * DOC_MAX, 4 * seq * columns),
            name="attention_early",
        )(where, owner_rows, *docs, queries, arrived, *parts, before)

    return late, final


def after(x, *others):
    return lax.optimization_barrier((x, *others))[0]


def exchange(x, count, bit):
    return lax.ppermute(x, "mp", [(i, i ^ bit) for i in range(count)])


def per_device(
    patch_rows,
    ln_gain,
    ln_bias,
    merge_up,
    merge_up_bias,
    merge_down,
    merge_down_bias,
    row_owner,
    text_embed,
    doc_ids,
    rms_gain,
    w_query,
    query_bias,
    w_keyval,
    keyval_bias,
):
    owners = lax.axis_size(("group", "dp"))
    count = lax.axis_size("mp")
    mp_index = lax.axis_index("mp")
    where = jnp.stack([mp_index, lax.axis_index(("group", "dp"))]).astype(jnp.int32)
    rows = row_owner.shape[0] // owners
    capacity = max(2, 2 * rows // owners)
    gain = rms_gain[None, :]
    owner_rows = row_owner.reshape(owners, rows)

    send, keep = merger(
        where, patch_rows[0], ln_gain, ln_bias, merge_up, merge_up_bias, merge_down, merge_down_bias, rows
    )
    text = text_embed[0]
    own = (keep.astype(F32) + exchange(send, count, 1).astype(F32)).astype(BF16)
    weight = jnp.transpose(after(w_keyval, own), (1, 0, 2))
    bit = 2
    while bit < count:
        other = after(exchange(own, count, bit), weight)
        own = (own.astype(F32) + other.astype(F32)).astype(BF16)
        bit *= 2
    sibling = exchange(own, count, 1)

    rows_all, parts = keyval_parts(where, text, own, sibling, gain, weight, keyval_bias, count)
    parts = [parts[0]] + [exchange(parts[x], count, x) for x in range(1, count)]
    text_queries, image_queries = query_rows(rows_all, text.shape[0], w_query, query_bias)
    outgoing = slots_of(where, owner_rows, row_owner, image_queries, parts, capacity)
    arrived = lax.all_to_all(
        outgoing.reshape(owners, capacity, -1), ("group", "dp"), split_axis=0, concat_axis=0, tiled=True
    ).reshape(owners * capacity, -1)
    late, final = attention(where, owner_rows, doc_ids[0], text_queries, parts, capacity)
    before = late(after(text_queries, outgoing))
    return final(after(arrived, before), before)[None]


def general(
    patch_rows,
    ln_gain,
    ln_bias,
    merge_up,
    merge_up_bias,
    merge_down,
    merge_down_bias,
    row_owner,
    text_embed,
    doc_ids,
    rms_gain,
    w_query,
    query_bias,
    w_keyval,
    keyval_bias,
):
    owners = lax.axis_size(("group", "dp"))
    own_index = lax.axis_index(("group", "dp"))
    mp_index = lax.axis_index("mp")
    pixels = patch_rows[0].astype(jnp.float32)
    center = pixels - jnp.mean(pixels, axis=-1, keepdims=True)
    spread = jnp.mean(center * center, axis=-1, keepdims=True)
    normed_patch = (center * lax.rsqrt(spread + 1e-06) * ln_gain + ln_bias).astype(jnp.bfloat16)
    merged = normed_patch.reshape(-1, 4 * pixels.shape[1])
    merged_rows = merged.shape[0]
    hidden = jax.nn.gelu(
        jnp.dot(merged, merge_up, preferred_element_type=jnp.float32) + merge_up_bias,
        approximate=False,
    ).astype(jnp.bfloat16)
    partial_sum = jnp.dot(hidden, merge_down, preferred_element_type=jnp.float32)
    vision = (
        lax.psum_scatter(partial_sum, "mp", scatter_dimension=1, tiled=True) + merge_down_bias
    ).astype(jnp.bfloat16)
    col_width = vision.shape[1]
    capacity = max(2, 2 * merged_rows // owners)
    owner_all = row_owner[:, 0]
    owner_ids = jnp.arange(owners, dtype=jnp.int32)
    onehot = (owner_all[:, None] == owner_ids[None, :]).astype(jnp.int32)
    per_source = jnp.sum(onehot.reshape(owners, merged_rows, owners), axis=1)
    my_block = lax.dynamic_slice_in_dim(onehot, own_index * merged_rows, merged_rows, 0)
    block_rank = jnp.sum((jnp.cumsum(my_block, axis=0) - my_block) * my_block, axis=1)
    my_owner = jnp.sum(my_block * owner_ids[None, :], axis=1)
    slot_id = my_owner * capacity + block_rank
    all_slots = jnp.arange(owners * capacity, dtype=jnp.int32)
    select = (slot_id[:, None] == all_slots[None, :]).astype(jnp.bfloat16)
    outgoing = jnp.einsum("ms,mc->sc", select, vision, preferred_element_type=jnp.float32).astype(
        jnp.bfloat16
    )
    arrived = lax.all_to_all(
        outgoing.reshape(owners, capacity, col_width),
        ("group", "dp"),
        split_axis=0,
        concat_axis=0,
        tiled=True,
    )
    arrived = arrived.reshape(owners * capacity, col_width)
    incoming = lax.dynamic_slice_in_dim(per_source, own_index, 1, 1)[:, 0]
    offsets = jnp.cumsum(incoming) - incoming
    total = jnp.sum(incoming)
    slot_rank = jnp.arange(capacity, dtype=jnp.int32)
    target = jnp.where(
        slot_rank[None, :] < incoming[:, None], offsets[:, None] + slot_rank[None, :], -1
    ).reshape(-1)
    text_rows = text_embed[0]
    seq_len = text_rows.shape[0]
    positions = jnp.arange(seq_len, dtype=jnp.int32)
    source_slot = jnp.sum(
        jnp.where(target[:, None] == positions[None, :], all_slots[:, None], 0), axis=0
    )
    is_image = (positions < total)[:, None]
    image_full = lax.all_gather(arrived, "mp", axis=1, tiled=True)
    sequence = jnp.where(is_image, jnp.take(image_full, source_slot, axis=0), text_rows)
    seq_f = sequence.astype(jnp.float32)
    normed_seq = (
        seq_f * lax.rsqrt(jnp.mean(seq_f * seq_f, axis=-1, keepdims=True) + 1e-06) * rms_gain
    ).astype(jnp.bfloat16)
    queries = (
        jnp.dot(normed_seq, w_query, preferred_element_type=jnp.float32) + query_bias
    ).astype(jnp.bfloat16)
    keyval_local = (
        jnp.einsum("sd,dtc->stc", normed_seq, w_keyval, preferred_element_type=jnp.float32)
        + keyval_bias
    ).astype(jnp.bfloat16)
    keyval_full = lax.all_gather(keyval_local, "mp", axis=2, tiled=True)
    keyval_heads = jnp.transpose(keyval_full.reshape(seq_len, 2, HEAD_DIM, KV_HEADS), (0, 1, 3, 2))
    local_heads = queries.shape[1] // HEAD_DIM
    group_size = HEADS // KV_HEADS
    kv_index = (mp_index * local_heads + jnp.arange(local_heads, dtype=jnp.int32)) // group_size
    keys = jnp.take(keyval_heads[:, 0], kv_index, axis=1)
    values = jnp.take(keyval_heads[:, 1], kv_index, axis=1)
    query_heads = queries.reshape(seq_len, local_heads, HEAD_DIM)
    scores = jnp.einsum(
        "qhd,khd->hqk", query_heads, keys, preferred_element_type=jnp.float32
    ) / math.sqrt(HEAD_DIM)
    documents = doc_ids[0]
    allowed = (documents[:, None] == documents[None, :]) & (
        positions[None, :] <= positions[:, None]
    )
    scores = jnp.where(allowed[None], scores, jnp.float32(-1e30))
    highest = jnp.max(scores, axis=-1, keepdims=True)
    weights = jnp.exp(scores - highest)
    probs = (weights / jnp.sum(weights, axis=-1, keepdims=True)).astype(jnp.bfloat16)
    output = jnp.einsum("hqk,khd->qhd", probs, values, preferred_element_type=jnp.float32)
    return output.astype(jnp.bfloat16).reshape(1, seq_len, local_heads * HEAD_DIM)


def solution(mesh):
    in_specs = (
        P(("group", "dp"), None, None),
        P(),
        P(),
        P(None, "mp"),
        P("mp"),
        P("mp", None),
        P("mp"),
        P(),
        P(("group", "dp"), None, None),
        P(("group", "dp"), None),
        P(),
        P(None, "mp"),
        P("mp"),
        P(None, None, "mp"),
        P(None, "mp"),
    )
    out_specs = P(("group", "dp"), None, "mp")
    count = mesh.shape["mp"]
    narrow = count < 2 or count > KV_HEADS or count & (count - 1)
    body = general if narrow else per_device
    return jax.shard_map(body, mesh=mesh, in_specs=in_specs, out_specs=out_specs, check_vma=False)
```

```python
import functools
import math

import jax
import jax.numpy as jnp
from jax import lax
from jax.experimental import pallas as pl
from jax.experimental.pallas import tpu as pltpu
from jax.sharding import PartitionSpec as P

HEADS = 64
KV_HEADS = 8
HEAD_DIM = 128
DOC_MAX = 64

BF16 = jnp.bfloat16
F32 = jnp.float32
VMEM = pl.BlockSpec(memory_space=pltpu.VMEM)
SMEM = pl.BlockSpec(memory_space=pltpu.SMEM)
ANY = pl.BlockSpec(memory_space=pl.ANY)
HBM = pl.BlockSpec(memory_space=pltpu.HBM)
AHEAD = 3
DEEP = 5
MIB = 1 << 20


def dot(a, b):
    return jnp.dot(a, b, preferred_element_type=F32)


def in_hbm(x):
    return pltpu.with_memory_space_constraint(x, pltpu.HBM)


def in_vmem(x):
    return pltpu.with_memory_space_constraint(x, pltpu.VMEM)


def params(mib):
    return pltpu.CompilerParams(vmem_limit_bytes=mib * MIB)


def cost(flops, nbytes):
    return pl.CostEstimate(flops=flops, bytes_accessed=nbytes, transcendentals=0)


def rms_scale(x, width):
    return lax.rsqrt(jnp.sum(x * x, axis=-1, keepdims=True) / width + 1e-06)


def stream(count, copy, body, ahead=AHEAD, then=None):
    @pl.loop(0, count)
    def _(i):
        copy(i).wait()

        @pl.when(i + ahead < count)
        def _():
            copy(i + ahead).start()

        if then is not None:

            @pl.when(i + ahead >= count)
            def _():
                then(i + ahead - count).start()

        body(i)


def begin(copy, ahead=AHEAD):
    for i in range(ahead):
        copy(i).start()


def tile(i, width):
    return pl.ds(pl.multiple_of(i * width, width), width)


def merger_kernel(
    where, patch_in, gain_in, bias_in, up, up_bias_in, down, down_bias_in, text, rms_gain_in, send, keep, text_out,
    patch, gain, bias, up_bias, down_bias, rms_gain, bias_row, normed, merged, total, up_buf, down_buf, text_buf,
    small_sem, up_sem, down_sem, text_sem,
):
    slots = DEEP + 1
    step = up_buf.shape[1]
    width = down_buf.shape[2]
    half = send.shape[1]
    per_half = half // width
    mp = where[0]
    mine = mp % 2
    pairs = [(patch_in, patch), (gain_in, gain), (bias_in, bias), (up_bias_in, up_bias), (down_bias_in, down_bias)]
    pairs.append((rms_gain_in, rms_gain))
    small = [pltpu.make_async_copy(x, y, small_sem.at[i]) for i, (x, y) in enumerate(pairs)]
    for copy in small:
        copy.start()

    def up_copy(i):
        return pltpu.make_async_copy(up.at[tile(i, step)], up_buf.at[i % slots], up_sem.at[i % slots])

    def column(i):
        first = jnp.where(i < per_half, 1 - mine, mine)
        return pl.multiple_of(first * half + (i % per_half) * width, width)

    def down_copy(i):
        return pltpu.make_async_copy(
            down.at[:, pl.ds(column(i), width)], down_buf.at[i % slots], down_sem.at[i % slots]
        )

    block = text_buf.shape[1]
    blocks = text.shape[0] // block

    def text_copy(i):
        return pltpu.make_async_copy(text.at[tile(i, block)], text_buf.at[i % slots], text_sem.at[i % slots])

    def text_norm(i):
        text_copy(i).wait()

        @pl.when(i + DEEP < blocks)
        def _():
            text_copy(i + DEEP).start()

        x = text_buf[i % slots].astype(F32)
        text_out[tile(i, block), :] = (x * rms_scale(x, x.shape[1]) * rms_gain[...]).astype(BF16)

    begin(up_copy, DEEP)
    begin(text_copy, DEEP)
    for copy in small:
        copy.wait()
    rows = send.shape[0]
    joined = patch.shape[0] // rows
    features = patch.shape[1]
    pixels = patch[...].astype(F32)
    center = pixels - jnp.mean(pixels, axis=-1, keepdims=True)
    spread = jnp.mean(center * center, axis=-1, keepdims=True)
    patches = center * lax.rsqrt(spread + 1e-06) * gain[...][None, :] + bias[...][None, :]
    for c in range(features // 128):
        normed[c] = patches[:, c * 128 : (c + 1) * 128]
        for j in range(joined):
            merged[:, pl.ds(j * features + c * 128, 128)] = normed[c, pl.ds(j, rows, stride=joined), :].astype(BF16)
    own = down_bias.shape[0]
    bias_row[...] = jnp.zeros_like(bias_row)
    bias_row[:, pl.ds(pl.multiple_of(mp * own, 128), own)] = down_bias[...][None, :]
    total[...] = jnp.broadcast_to(up_bias[...][None, :], total.shape)

    def up_body(i):
        text_norm(i)
        total[...] += dot(merged[:, tile(i, step)], up_buf[i % slots])

    up_steps = up.shape[0] // step
    stream(up_steps, up_copy, up_body, DEEP, down_copy)
    sums = total[...]
    hidden = (0.5 * sums * (1.0 + lax.erf(sums * math.sqrt(0.5)))).astype(BF16)

    def down_body(i):
        text_norm(up_steps + i)
        part = (dot(hidden, down_buf[i % slots]) + bias_row[:, pl.ds(column(i), width)]).astype(BF16)
        here = tile(i % per_half, width)

        @pl.when(i < per_half)
        def _():
            send[:, here] = part

        @pl.when(i >= per_half)
        def _():
            keep[:, here] = part

    stream(2 * per_half, down_copy, down_body, DEEP)


def merger(where, patch, gain, bias, up, up_bias, down, down_bias, text, rms_gain, rows):
    features = patch.shape[1]
    depth, hidden = up.shape
    columns = down.shape[1]
    step = depth // 8
    width = columns // 8
    slots = DEEP + 1
    return pl.pallas_call(
        merger_kernel,
        out_shape=[jax.ShapeDtypeStruct((rows, columns // 2), BF16)] * 2 + [pltpu.VMEM(text.shape, BF16)],
        in_specs=[SMEM] + [HBM] * 9,
        out_specs=[VMEM, VMEM, VMEM],
        scratch_shapes=[
            pltpu.VMEM(patch.shape, BF16),
            pltpu.VMEM(gain.shape, F32),
            pltpu.VMEM(bias.shape, F32),
            pltpu.VMEM(up_bias.shape, F32),
            pltpu.VMEM(down_bias.shape, F32),
            pltpu.VMEM(rms_gain.shape, F32),
            pltpu.VMEM((1, columns), F32),
            pltpu.VMEM((features // 128, patch.shape[0], 128), F32),
            pltpu.VMEM((rows, depth), BF16),
            pltpu.VMEM((rows, hidden), F32),
            pltpu.VMEM((slots, step, hidden), BF16),
            pltpu.VMEM((slots, hidden, width), BF16),
            pltpu.VMEM((slots, text.shape[0] // 16, text.shape[1]), BF16),
            pltpu.SemaphoreType.DMA((6,)),
            pltpu.SemaphoreType.DMA((slots,)),
            pltpu.SemaphoreType.DMA((slots,)),
            pltpu.SemaphoreType.DMA((slots,)),
        ],
        compiler_params=params(34),
        cost_estimate=cost(2 * rows * hidden * (depth + columns), 2 * hidden * (depth + columns)),
        name="merger",
    )(where, *map(in_hbm, (patch, gain, bias, up, up_bias, down, down_bias, text, rms_gain)))


def weights_kernel(keyval, query, out, query_out, buf, sem, query_sem):
    depth, _, columns = keyval.shape
    pieces = sem.shape[0]
    step = depth // pieces

    def copy(i):
        return pltpu.make_async_copy(keyval.at[tile(i, step)], buf.at[tile(i, step)], sem.at[i])

    for i in range(pieces):
        copy(i).start()
    query_copy = pltpu.make_async_copy(query.at[:, pl.ds(0, query_out.shape[1])], query_out, query_sem)
    query_copy.start()
    pairs = buf.reshape(2 * depth, columns)
    row = lax.broadcasted_iota(jnp.int32, (256, 256), 0)
    column = lax.broadcasted_iota(jnp.int32, (256, 256), 1)
    apart = (column == 2 * (row % 128) + row // 128).astype(F32).astype(BF16)
    together = 4

    @pl.loop(0, pieces)
    def _(i):
        copy(i).wait()

        @pl.loop(0, step // (128 * together))
        def _(j):
            first = i * (step // 128) + j * together
            blocks = [pairs[tile(first + n, 256), :] for n in range(together)]
            sorted_blocks = dot(apart, jnp.concatenate(blocks, axis=1)).astype(BF16)
            for n in range(together):
                for side in range(2):
                    out[tile(first + n, 128), pl.ds(side * columns, columns)] = sorted_blocks[
                        side * 128 : (side + 1) * 128, n * columns : (n + 1) * columns
                    ]

    query_copy.wait()


def weights_ahead(keyval, query, width):
    depth, _, columns = keyval.shape
    return pl.pallas_call(
        weights_kernel,
        out_shape=[pltpu.VMEM((depth, 2 * columns), BF16), pltpu.VMEM((depth, width), BF16)],
        in_specs=[HBM, HBM],
        out_specs=[VMEM, VMEM],
        scratch_shapes=[
            pltpu.VMEM((depth, 2, columns), BF16),
            pltpu.SemaphoreType.DMA((8,)),
            pltpu.SemaphoreType.DMA,
        ],
        compiler_params=params(12),
        cost_estimate=cost(4 * depth * columns * 256, 4 * depth * columns + 2 * depth * width),
        name="weights_ahead",
    )(in_hbm(keyval), in_hbm(query))


def keyval_kernel(where, text, own, sibling, gain, weight, bias, rows_all, *rest):
    parts, keyval = rest[:-1], rest[-1]
    texts, images = text.shape[0], own.shape[0]
    mp = where[0]
    half = own.shape[1]
    mine = mp % 2
    first, second = own[...].astype(F32), sibling[...].astype(F32)
    squares = jnp.sum(first * first, axis=-1, keepdims=True) + jnp.sum(second * second, axis=-1, keepdims=True)
    scale = lax.rsqrt(squares / (2 * half) + 1e-06)
    for values, which in ((first, mine), (second, 1 - mine)):
        here = pl.ds(pl.multiple_of(which * half, half), half)
        rows_all[pl.ds(texts, images), here] = (values * scale * gain[:, here]).astype(BF16)
    rows_all[pl.ds(0, texts), :] = text[...]
    columns = weight.shape[1] // 2
    sums = dot(rows_all[...], weight[...])
    for t in range(2):
        keyval[t] = (sums[:, t * columns : (t + 1) * columns] + bias[pl.ds(t, 1), :]).astype(BF16)

    count = len(parts)
    width = parts[0].shape[1]
    heads = KV_HEADS // count
    coords = columns // KV_HEADS
    row = lax.broadcasted_iota(jnp.int32, (columns, width // 2), 0)
    column = lax.broadcasted_iota(jnp.int32, (columns, width // 2), 1)
    for x in range(count):
        head = (mp ^ x) * heads + column // coords
        pick = (row == (column % coords) * KV_HEADS + head).astype(F32).astype(BF16)
        for t in range(2):
            parts[x][:, pl.ds(t * (width // 2), width // 2)] = dot(keyval[t], pick).astype(BF16)


def keyval_parts(where, text, own, sibling, gain, weight, bias, count):
    texts, depth = text.shape
    columns = weight.shape[1] // 2
    rows = texts + own.shape[0]
    width = 2 * columns // count
    outs = pl.pallas_call(
        keyval_kernel,
        out_shape=[pltpu.VMEM((rows, depth), BF16)] + [jax.ShapeDtypeStruct((rows, width), BF16)] * count,
        in_specs=[SMEM, VMEM, VMEM, VMEM, VMEM, VMEM, VMEM],
        out_specs=[VMEM] * (1 + count),
        scratch_shapes=[pltpu.VMEM((2, rows, columns), BF16)],
        compiler_params=params(8),
        cost_estimate=cost(4 * rows * depth * columns, 4 * depth * columns),
        name="keyval",
    )(where, in_vmem(text), own, sibling, gain, in_vmem(weight), bias)
    return outs[0], outs[1:]


def query_kernel(rows_all, ready, weight, bias, text_out, image_out, buf, sem):
    width = ready.shape[1]
    texts = text_out.shape[0]
    later = buf.shape[0]

    def copy(i):
        return pltpu.make_async_copy(weight.at[:, tile(i + 1, width)], buf.at[i], sem.at[i])

    def columns(i, weights):
        here = tile(i, width)
        out = (dot(rows_all[...], weights) + bias[:, here]).astype(BF16)
        text_out[:, here] = out[:texts]
        image_out[:, here] = out[texts:]

    begin(copy, 2)
    columns(0, ready[...])
    stream(later, copy, lambda i: columns(i + 1, buf[i]), 2)


def query_rows(rows_all, texts, ready, weight, bias):
    depth = rows_all.shape[1]
    images = rows_all.shape[0] - texts
    columns = weight.shape[1]
    width = ready.shape[1]
    later = columns // width - 1
    return pl.pallas_call(
        query_kernel,
        out_shape=[jax.ShapeDtypeStruct((texts, columns), BF16), jax.ShapeDtypeStruct((images, columns), BF16)],
        in_specs=[VMEM, VMEM, HBM, VMEM],
        out_specs=[VMEM, VMEM],
        scratch_shapes=[pltpu.VMEM((later, depth, width), BF16), pltpu.SemaphoreType.DMA((later,))],
        compiler_params=params(30),
        cost_estimate=cost(2 * (texts + images) * depth * columns, 2 * depth * columns),
        name="query",
    )(in_vmem(rows_all), in_vmem(ready), in_hbm(weight), bias[None, :])


def join_parts(mp, parts, first_row, rows):
    count = len(parts)
    width = parts[0].shape[1]
    heads = KV_HEADS // count
    coords = HEAD_DIM // count
    full = 2 * heads * HEAD_DIM
    row = lax.broadcasted_iota(jnp.int32, (width, full), 0)
    column = lax.broadcasted_iota(jnp.int32, (width, full), 1)
    total = jnp.zeros((rows, full), F32)
    for x in range(count):
        coordinate = (mp ^ x) * coords + row % coords
        place = (column == (row // coords) * HEAD_DIM + coordinate).astype(BF16)
        total = total + dot(parts[x][pl.ds(first_row, rows), :], place)
    return total.astype(BF16)


def slots_kernel(where, owner_row, queries, *rest):
    parts, out = rest[:-1], rest[-1]
    rows, columns = queries.shape
    slots = out.shape[0]
    owners = owner_row.shape[1] // rows
    mp, me = where[0], where[1]
    row = lax.broadcasted_iota(jnp.int32, (owners * rows, rows), 0)
    mine = (row == me * rows + lax.broadcasted_iota(jnp.int32, (owners * rows, rows), 1)).astype(F32).astype(BF16)
    named = owner_row[...].astype(F32).astype(BF16)
    across = dot(named, mine)
    down = lax.dot_general(mine, named, (((0,), (1,)), ((), ())), preferred_element_type=F32)
    earlier = lax.broadcasted_iota(jnp.int32, (rows, rows), 0) < lax.broadcasted_iota(jnp.int32, (rows, rows), 1)
    rank = jnp.sum(jnp.where((down == across) & earlier, 1.0, 0.0), axis=0, keepdims=True)
    slot = across * (slots // owners) + rank
    select = (lax.broadcasted_iota(jnp.int32, (slots, rows), 0).astype(F32) == slot).astype(F32).astype(BF16)
    out[:, pl.ds(0, columns)] = dot(select, queries[...]).astype(BF16)
    keyval = join_parts(mp, parts, parts[0].shape[0] - rows, rows)
    out[:, pl.ds(columns, out.shape[1] - columns)] = dot(select, keyval).astype(BF16)


def slots_of(where, owner_row, queries, parts, slots):
    width = queries.shape[1] + 2 * (KV_HEADS // len(parts)) * HEAD_DIM
    return pl.pallas_call(
        slots_kernel,
        out_shape=jax.ShapeDtypeStruct((slots, width), BF16),
        in_specs=[SMEM] + [VMEM] * (2 + len(parts)),
        out_specs=VMEM,
        compiler_params=params(8),
        name="slots",
    )(where, owner_row, queries, *parts)


def attend(blocks, first, doc_row, doc_column, windows, q_all, kv_all, out):
    q_first, k_first, out_first = first
    heads = q_all.shape[1] // HEAD_DIM
    groups = kv_all.shape[1] // (2 * HEAD_DIM)
    shared = heads // groups
    block = DOC_MAX
    seq = doc_row.shape[1]
    scale = 1.0 / math.sqrt(HEAD_DIM)
    docs = doc_row[...].astype(F32)
    for b in range(seq // block):
        k0 = max(0, b - 1) * block
        windows[pl.ds(b, 1), :] = docs[:, k0 : k0 + 2 * block]
    eye = lax.broadcasted_iota(jnp.int32, (seq, seq), 0) == lax.broadcasted_iota(jnp.int32, (seq, seq), 1)
    doc_column[...] = jnp.sum(jnp.where(eye, docs, 0.0), axis=1, keepdims=True)
    row = lax.broadcasted_iota(jnp.int32, (block, 2 * block), 0)
    column = lax.broadcasted_iota(jnp.int32, (block, 2 * block), 1)

    @pl.loop(blocks[0], blocks[1])
    def _(b):
        q0 = pl.multiple_of(b * block, block)
        k0 = pl.multiple_of(jnp.maximum(b - 1, 0) * block, block)
        allowed = (doc_column[pl.ds(q0, block), :] == windows[pl.ds(b, 1), :]) & (k0 + column <= q0 + row)
        penalty = jnp.concatenate([jnp.where(allowed, 0.0, -1e30)] * shared, axis=0)
        for g in range(groups):
            keys = kv_all[pl.ds(k0 - k_first, 2 * block), tile(g, HEAD_DIM)]
            values = kv_all[pl.ds(k0 - k_first, 2 * block), tile(groups + g, HEAD_DIM)]
            columns = [tile(g * shared + h, HEAD_DIM) for h in range(shared)]
            q = jnp.concatenate([q_all[pl.ds(q0 - q_first, block), c] for c in columns], axis=0)
            scores = lax.dot_general(q, keys, (((1,), (1,)), ((), ())), preferred_element_type=F32) * scale
            scores = jnp.where(penalty < 0.0, penalty, scores)
            weights = jnp.exp(scores - jnp.max(scores, axis=-1, keepdims=True))
            probs = (weights * (1.0 / jnp.sum(weights, axis=-1, keepdims=True))).astype(BF16)
            result = dot(probs, values).astype(BF16)
            for h, c in enumerate(columns):
                out[pl.ds(q0 - out_first, block), c] = result[h * block : (h + 1) * block]


def late_kernel(early, where, doc_row, queries, *rest):
    parts = rest[:-4]
    out, kv_all, doc_column, windows = rest[-4:]
    seq = queries.shape[0]
    first = early - DOC_MAX
    kv_all[...] = join_parts(where[0], parts, first, seq - first)
    blocks = (early // DOC_MAX, seq // DOC_MAX)
    attend(blocks, (0, first, 0), doc_row, doc_column, windows, queries, kv_all, out)


def early_kernel(early, owners, where, owner_row, doc_row, queries, arrived, *rest):
    parts = rest[:-8]
    _, out, q_all, kv_all, result, doc_column, windows, sem = rest[-8:]
    mp, me = where[0], where[1]
    columns = queries.shape[1]
    slots = arrived.shape[0]
    capacity = slots // owners
    named = (owner_row[...] == me).astype(F32).astype(BF16)
    total = owner_row.shape[1]
    source = lax.broadcasted_iota(jnp.int32, (total, slots), 0) // (total // owners)
    block = lax.broadcasted_iota(jnp.int32, (total, slots), 1) // capacity
    here = dot(named, (source == block).astype(F32).astype(BF16))
    offset = dot(named, (source < block).astype(F32).astype(BF16))
    index = (lax.broadcasted_iota(jnp.int32, (1, slots), 1) % capacity).astype(F32)
    target = jnp.where(index < here, offset + index, -1.0)
    position = lax.broadcasted_iota(jnp.int32, (slots, slots), 0).astype(F32)
    place = (position == target).astype(F32).astype(BF16)
    placed = dot(place, arrived[...]).astype(BF16)
    count = jnp.sum(named.astype(F32), axis=1, keepdims=True)
    is_image = lax.broadcasted_iota(jnp.int32, (slots, 1), 0).astype(F32) < count

    keyval = join_parts(mp, parts, 0, early)
    kv_all[...] = keyval
    kv_all[pl.ds(0, slots), :] = jnp.where(is_image, placed[:, columns:], keyval[:slots])
    q_all[...] = queries[pl.ds(0, early), :]
    q_all[pl.ds(0, slots), :] = jnp.where(is_image, placed[:, :columns], queries[pl.ds(0, slots), :])
    attend((0, early // DOC_MAX), (0, 0, 0), doc_row, doc_column, windows, q_all, kv_all, result)
    copy = pltpu.make_async_copy(result, out.at[pl.ds(0, early)], sem)
    copy.start()
    copy.wait()


def attention(where, owner_row, documents, queries, parts, owners, slots):
    seq, columns = queries.shape
    width = 2 * (KV_HEADS // len(parts)) * HEAD_DIM
    early = min(seq, -(-slots // DOC_MAX) * DOC_MAX + DOC_MAX)
    shape = jax.ShapeDtypeStruct((seq, columns), BF16)
    docs = [pltpu.VMEM((seq, 1), F32), pltpu.VMEM((seq // DOC_MAX, 2 * DOC_MAX), F32)]

    def late(queries):
        return pl.pallas_call(
            functools.partial(late_kernel, early),
            out_shape=shape,
            in_specs=[SMEM] + [VMEM] * (2 + len(parts)),
            out_specs=VMEM,
            scratch_shapes=[pltpu.VMEM((seq - early + DOC_MAX, width), BF16)] + docs,
            compiler_params=params(12),
            cost_estimate=cost(4 * (seq - early) * columns * 2 * DOC_MAX, 4 * seq * columns),
            name="attention_late",
        )(where, documents, queries, *parts)

    def final(arrived, before):
        return pl.pallas_call(
            functools.partial(early_kernel, early, owners),
            out_shape=shape,
            in_specs=[SMEM] + [VMEM] * (4 + len(parts)) + [ANY],
            out_specs=ANY,
            scratch_shapes=[
                pltpu.VMEM((early, columns), BF16),
                pltpu.VMEM((early, width), BF16),
                pltpu.VMEM((early, columns), BF16),
            ]
            + docs
            + [pltpu.SemaphoreType.DMA],
            input_output_aliases={5 + len(parts): 0},
            compiler_params=params(12),
            cost_estimate=cost(4 * early * columns * 2 * DOC_MAX, 4 * seq * columns),
            name="attention_early",
        )(where, owner_row, documents, queries, arrived, *parts, before)

    return late, final


def after(x, *others):
    return lax.optimization_barrier((x, *others))[0]


def exchange(x, count, bit):
    return lax.ppermute(x, "mp", [(i, i ^ bit) for i in range(count)])


def per_device(
    patch_rows,
    ln_gain,
    ln_bias,
    merge_up,
    merge_up_bias,
    merge_down,
    merge_down_bias,
    row_owner,
    text_embed,
    doc_ids,
    rms_gain,
    w_query,
    query_bias,
    w_keyval,
    keyval_bias,
):
    owners = lax.axis_size(("group", "dp"))
    count = lax.axis_size("mp")
    mp_index = lax.axis_index("mp")
    where = jnp.stack([mp_index, lax.axis_index(("group", "dp"))]).astype(jnp.int32)
    rows = row_owner.shape[0] // owners
    capacity = max(2, 2 * rows // owners)
    owner_row = row_owner.reshape(1, -1)

    send, keep, text = merger(
        where, patch_rows[0], ln_gain, ln_bias, merge_up, merge_up_bias, merge_down, merge_down_bias,
        text_embed[0], rms_gain[None, :], rows,
    )
    own = (keep.astype(F32) + exchange(send, count, 1).astype(F32)).astype(BF16)
    weight, ready = weights_ahead(after(w_keyval, own), w_query, w_query.shape[1] // 4)
    bit = 2
    while bit < count:
        other = after(exchange(own, count, bit), weight)
        own = (own.astype(F32) + other.astype(F32)).astype(BF16)
        bit *= 2
    sibling = exchange(own, count, 1)

    rows_all, parts = keyval_parts(where, text, own, sibling, rms_gain[None, :], weight, keyval_bias, count)
    parts = [parts[0]] + [exchange(parts[x], count, x) for x in range(1, count)]
    text_queries, image_queries = query_rows(rows_all, text.shape[0], ready, w_query, query_bias)
    outgoing = slots_of(where, owner_row, image_queries, parts, owners * capacity)
    arrived = lax.all_to_all(
        outgoing.reshape(owners, capacity, -1), ("group", "dp"), split_axis=0, concat_axis=0, tiled=True
    ).reshape(owners * capacity, -1)
    late, final = attention(where, owner_row, doc_ids, text_queries, parts, owners, owners * capacity)
    before = late(after(text_queries, outgoing))
    return final(after(arrived, before), before)[None]


def general(
    patch_rows,
    ln_gain,
    ln_bias,
    merge_up,
    merge_up_bias,
    merge_down,
    merge_down_bias,
    row_owner,
    text_embed,
    doc_ids,
    rms_gain,
    w_query,
    query_bias,
    w_keyval,
    keyval_bias,
):
    owners = lax.axis_size(("group", "dp"))
    own_index = lax.axis_index(("group", "dp"))
    mp_index = lax.axis_index("mp")
    pixels = patch_rows[0].astype(jnp.float32)
    center = pixels - jnp.mean(pixels, axis=-1, keepdims=True)
    spread = jnp.mean(center * center, axis=-1, keepdims=True)
    normed_patch = (center * lax.rsqrt(spread + 1e-06) * ln_gain + ln_bias).astype(jnp.bfloat16)
    merged = normed_patch.reshape(-1, 4 * pixels.shape[1])
    merged_rows = merged.shape[0]
    hidden = jax.nn.gelu(
        jnp.dot(merged, merge_up, preferred_element_type=jnp.float32) + merge_up_bias,
        approximate=False,
    ).astype(jnp.bfloat16)
    partial_sum = jnp.dot(hidden, merge_down, preferred_element_type=jnp.float32)
    vision = (
        lax.psum_scatter(partial_sum, "mp", scatter_dimension=1, tiled=True) + merge_down_bias
    ).astype(jnp.bfloat16)
    col_width = vision.shape[1]
    capacity = max(2, 2 * merged_rows // owners)
    owner_all = row_owner[:, 0]
    owner_ids = jnp.arange(owners, dtype=jnp.int32)
    onehot = (owner_all[:, None] == owner_ids[None, :]).astype(jnp.int32)
    per_source = jnp.sum(onehot.reshape(owners, merged_rows, owners), axis=1)
    my_block = lax.dynamic_slice_in_dim(onehot, own_index * merged_rows, merged_rows, 0)
    block_rank = jnp.sum((jnp.cumsum(my_block, axis=0) - my_block) * my_block, axis=1)
    my_owner = jnp.sum(my_block * owner_ids[None, :], axis=1)
    slot_id = my_owner * capacity + block_rank
    all_slots = jnp.arange(owners * capacity, dtype=jnp.int32)
    select = (slot_id[:, None] == all_slots[None, :]).astype(jnp.bfloat16)
    outgoing = jnp.einsum("ms,mc->sc", select, vision, preferred_element_type=jnp.float32).astype(
        jnp.bfloat16
    )
    arrived = lax.all_to_all(
        outgoing.reshape(owners, capacity, col_width),
        ("group", "dp"),
        split_axis=0,
        concat_axis=0,
        tiled=True,
    )
    arrived = arrived.reshape(owners * capacity, col_width)
    incoming = lax.dynamic_slice_in_dim(per_source, own_index, 1, 1)[:, 0]
    offsets = jnp.cumsum(incoming) - incoming
    total = jnp.sum(incoming)
    slot_rank = jnp.arange(capacity, dtype=jnp.int32)
    target = jnp.where(
        slot_rank[None, :] < incoming[:, None], offsets[:, None] + slot_rank[None, :], -1
    ).reshape(-1)
    text_rows = text_embed[0]
    seq_len = text_rows.shape[0]
    positions = jnp.arange(seq_len, dtype=jnp.int32)
    source_slot = jnp.sum(
        jnp.where(target[:, None] == positions[None, :], all_slots[:, None], 0), axis=0
    )
    is_image = (positions < total)[:, None]
    image_full = lax.all_gather(arrived, "mp", axis=1, tiled=True)
    sequence = jnp.where(is_image, jnp.take(image_full, source_slot, axis=0), text_rows)
    seq_f = sequence.astype(jnp.float32)
    normed_seq = (
        seq_f * lax.rsqrt(jnp.mean(seq_f * seq_f, axis=-1, keepdims=True) + 1e-06) * rms_gain
    ).astype(jnp.bfloat16)
    queries = (
        jnp.dot(normed_seq, w_query, preferred_element_type=jnp.float32) + query_bias
    ).astype(jnp.bfloat16)
    keyval_local = (
        jnp.einsum("sd,dtc->stc", normed_seq, w_keyval, preferred_element_type=jnp.float32)
        + keyval_bias
    ).astype(jnp.bfloat16)
    keyval_full = lax.all_gather(keyval_local, "mp", axis=2, tiled=True)
    keyval_heads = jnp.transpose(keyval_full.reshape(seq_len, 2, HEAD_DIM, KV_HEADS), (0, 1, 3, 2))
    local_heads = queries.shape[1] // HEAD_DIM
    group_size = HEADS // KV_HEADS
    kv_index = (mp_index * local_heads + jnp.arange(local_heads, dtype=jnp.int32)) // group_size
    keys = jnp.take(keyval_heads[:, 0], kv_index, axis=1)
    values = jnp.take(keyval_heads[:, 1], kv_index, axis=1)
    query_heads = queries.reshape(seq_len, local_heads, HEAD_DIM)
    scores = jnp.einsum(
        "qhd,khd->hqk", query_heads, keys, preferred_element_type=jnp.float32
    ) / math.sqrt(HEAD_DIM)
    documents = doc_ids[0]
    allowed = (documents[:, None] == documents[None, :]) & (
        positions[None, :] <= positions[:, None]
    )
    scores = jnp.where(allowed[None], scores, jnp.float32(-1e30))
    highest = jnp.max(scores, axis=-1, keepdims=True)
    weights = jnp.exp(scores - highest)
    probs = (weights / jnp.sum(weights, axis=-1, keepdims=True)).astype(jnp.bfloat16)
    output = jnp.einsum("hqk,khd->qhd", probs, values, preferred_element_type=jnp.float32)
    return output.astype(jnp.bfloat16).reshape(1, seq_len, local_heads * HEAD_DIM)


def solution(mesh):
    in_specs = (
        P(("group", "dp"), None, None),
        P(),
        P(),
        P(None, "mp"),
        P("mp"),
        P("mp", None),
        P("mp"),
        P(),
        P(("group", "dp"), None, None),
        P(("group", "dp"), None),
        P(),
        P(None, "mp"),
        P("mp"),
        P(None, None, "mp"),
        P(None, "mp"),
    )
    out_specs = P(("group", "dp"), None, "mp")
    count = mesh.shape["mp"]
    narrow = count < 2 or count > KV_HEADS or count & (count - 1)
    body = general if narrow else per_device
    return jax.shard_map(body, mesh=mesh, in_specs=in_specs, out_specs=out_specs, check_vma=False)
```

```python
import functools
import math

import jax
import jax.numpy as jnp
from jax import lax
from jax.experimental import pallas as pl
from jax.experimental.pallas import tpu as pltpu
from jax.sharding import PartitionSpec as P

HEADS = 64
KV_HEADS = 8
HEAD_DIM = 128
DOC_MAX = 64

BF16 = jnp.bfloat16
F32 = jnp.float32
VMEM = pl.BlockSpec(memory_space=pltpu.VMEM)
SMEM = pl.BlockSpec(memory_space=pltpu.SMEM)
ANY = pl.BlockSpec(memory_space=pl.ANY)
HBM = pl.BlockSpec(memory_space=pltpu.HBM)
AHEAD = 3
DEEP = 5
MIB = 1 << 20


def dot(a, b):
    return jnp.dot(a, b, preferred_element_type=F32)


def in_hbm(x):
    return pltpu.with_memory_space_constraint(x, pltpu.HBM)


def in_vmem(x):
    return pltpu.with_memory_space_constraint(x, pltpu.VMEM)


def params(mib):
    return pltpu.CompilerParams(vmem_limit_bytes=mib * MIB)


def cost(flops, nbytes):
    return pl.CostEstimate(flops=flops, bytes_accessed=nbytes, transcendentals=0)


def rms_scale(x, width):
    return lax.rsqrt(jnp.sum(x * x, axis=-1, keepdims=True) / width + 1e-06)


def stream(count, copy, body, ahead=AHEAD, then=None):
    @pl.loop(0, count)
    def _(i):
        copy(i).wait()

        @pl.when(i + ahead < count)
        def _():
            copy(i + ahead).start()

        if then is not None:

            @pl.when(i + ahead >= count)
            def _():
                then(i + ahead - count).start()

        body(i)


def begin(copy, ahead=AHEAD):
    for i in range(ahead):
        copy(i).start()


def tile(i, width):
    return pl.ds(pl.multiple_of(i * width, width), width)


def merger_kernel(
    where, patch_in, gain_in, bias_in, up, up_bias_in, down, down_bias_in, text, rms_gain_in, send, keep, text_out,
    patch, gain, bias, up_bias, down_bias, rms_gain, bias_row, normed, merged, total, up_buf, down_buf, text_buf,
    small_sem, up_sem, down_sem, text_sem,
):
    slots = DEEP + 1
    step = up_buf.shape[1]
    width = down_buf.shape[2]
    half = send.shape[1]
    per_half = half // width
    mp = where[0]
    mine = mp % 2
    pairs = [(patch_in, patch), (gain_in, gain), (bias_in, bias), (up_bias_in, up_bias), (down_bias_in, down_bias)]
    pairs.append((rms_gain_in, rms_gain))
    small = [pltpu.make_async_copy(x, y, small_sem.at[i]) for i, (x, y) in enumerate(pairs)]
    for copy in small:
        copy.start()

    def up_copy(i):
        return pltpu.make_async_copy(up.at[tile(i, step)], up_buf.at[i % slots], up_sem.at[i % slots])

    def column(i):
        first = jnp.where(i < per_half, 1 - mine, mine)
        return pl.multiple_of(first * half + (i % per_half) * width, width)

    def down_copy(i):
        return pltpu.make_async_copy(
            down.at[:, pl.ds(column(i), width)], down_buf.at[i % slots], down_sem.at[i % slots]
        )

    block = text_buf.shape[1]
    blocks = text.shape[0] // block

    def text_copy(i):
        return pltpu.make_async_copy(text.at[tile(i, block)], text_buf.at[i % slots], text_sem.at[i % slots])

    def text_norm(i):
        text_copy(i).wait()

        @pl.when(i + DEEP < blocks)
        def _():
            text_copy(i + DEEP).start()

        x = text_buf[i % slots].astype(F32)
        text_out[tile(i, block), :] = (x * rms_scale(x, x.shape[1]) * rms_gain[...]).astype(BF16)

    begin(up_copy, DEEP)
    begin(text_copy, DEEP)
    for copy in small:
        copy.wait()
    rows = send.shape[0]
    joined = patch.shape[0] // rows
    features = patch.shape[1]
    pixels = patch[...].astype(F32)
    center = pixels - jnp.mean(pixels, axis=-1, keepdims=True)
    spread = jnp.mean(center * center, axis=-1, keepdims=True)
    patches = center * lax.rsqrt(spread + 1e-06) * gain[...][None, :] + bias[...][None, :]
    for c in range(features // 128):
        normed[c] = patches[:, c * 128 : (c + 1) * 128]
        for j in range(joined):
            merged[:, pl.ds(j * features + c * 128, 128)] = normed[c, pl.ds(j, rows, stride=joined), :].astype(BF16)
    own = down_bias.shape[0]
    bias_row[...] = jnp.zeros_like(bias_row)
    bias_row[:, pl.ds(pl.multiple_of(mp * own, 128), own)] = down_bias[...][None, :]
    total[...] = jnp.broadcast_to(up_bias[...][None, :], total.shape)

    def up_body(i):
        text_norm(i)
        total[...] += dot(merged[:, tile(i, step)], up_buf[i % slots])

    up_steps = up.shape[0] // step
    stream(up_steps, up_copy, up_body, DEEP, down_copy)
    sums = total[...]
    hidden = (0.5 * sums * (1.0 + lax.erf(sums * math.sqrt(0.5)))).astype(BF16)

    def down_body(i):
        text_norm(up_steps + i)
        part = (dot(hidden, down_buf[i % slots]) + bias_row[:, pl.ds(column(i), width)]).astype(BF16)
        here = tile(i % per_half, width)

        @pl.when(i < per_half)
        def _():
            send[:, here] = part

        @pl.when(i >= per_half)
        def _():
            keep[:, here] = part

    stream(2 * per_half, down_copy, down_body, DEEP)


def merger(where, patch, gain, bias, up, up_bias, down, down_bias, text, rms_gain, rows):
    features = patch.shape[1]
    depth, hidden = up.shape
    columns = down.shape[1]
    step = depth // 8
    width = columns // 8
    slots = DEEP + 1
    return pl.pallas_call(
        merger_kernel,
        out_shape=[jax.ShapeDtypeStruct((rows, columns // 2), BF16)] * 2 + [pltpu.VMEM(text.shape, BF16)],
        in_specs=[SMEM] + [HBM] * 9,
        out_specs=[VMEM, VMEM, VMEM],
        scratch_shapes=[
            pltpu.VMEM(patch.shape, BF16),
            pltpu.VMEM(gain.shape, F32),
            pltpu.VMEM(bias.shape, F32),
            pltpu.VMEM(up_bias.shape, F32),
            pltpu.VMEM(down_bias.shape, F32),
            pltpu.VMEM(rms_gain.shape, F32),
            pltpu.VMEM((1, columns), F32),
            pltpu.VMEM((features // 128, patch.shape[0], 128), F32),
            pltpu.VMEM((rows, depth), BF16),
            pltpu.VMEM((rows, hidden), F32),
            pltpu.VMEM((slots, step, hidden), BF16),
            pltpu.VMEM((slots, hidden, width), BF16),
            pltpu.VMEM((slots, text.shape[0] // 16, text.shape[1]), BF16),
            pltpu.SemaphoreType.DMA((6,)),
            pltpu.SemaphoreType.DMA((slots,)),
            pltpu.SemaphoreType.DMA((slots,)),
            pltpu.SemaphoreType.DMA((slots,)),
        ],
        compiler_params=params(34),
        cost_estimate=cost(2 * rows * hidden * (depth + columns), 2 * hidden * (depth + columns)),
        name="merger",
    )(where, *map(in_hbm, (patch, gain, bias, up, up_bias, down, down_bias, text, rms_gain)))


def weights_kernel(keyval, query, out, query_out, sem):
    depth, _, columns = keyval.shape
    pieces = sem.shape[0]
    step = depth // pieces
    width = query_out.shape[1]
    copies = [
        pltpu.make_async_copy(query.at[pl.ds(i * step, step), pl.ds(0, width)], query_out.at[pl.ds(i * step, step)], sem.at[i])
        for i in range(pieces)
    ]
    for copy in copies:
        copy.start()
    pairs = keyval.reshape(2 * depth, columns)
    row = lax.broadcasted_iota(jnp.int32, (256, 256), 0)
    column = lax.broadcasted_iota(jnp.int32, (256, 256), 1)
    apart = (column == 2 * (row % 128) + row // 128).astype(F32).astype(BF16)
    together = 8

    @pl.loop(0, depth // (128 * together))
    def _(j):
        blocks = [pairs[tile(j * together + n, 256), :] for n in range(together)]
        ordered = dot(apart, jnp.concatenate(blocks, axis=1)).astype(BF16)
        for n in range(together):
            for side in range(2):
                out[tile(j * together + n, 128), pl.ds(side * columns, columns)] = ordered[
                    side * 128 : (side + 1) * 128, n * columns : (n + 1) * columns
                ]

    for copy in copies:
        copy.wait()


def weights_ahead(keyval, query, width):
    depth, _, columns = keyval.shape
    return pl.pallas_call(
        weights_kernel,
        out_shape=[pltpu.VMEM((depth, 2 * columns), BF16), pltpu.VMEM((depth, width), BF16)],
        in_specs=[VMEM, HBM],
        out_specs=[VMEM, VMEM],
        scratch_shapes=[pltpu.SemaphoreType.DMA((4,))],
        compiler_params=params(8),
        cost_estimate=cost(4 * depth * columns * 256, 4 * depth * columns + 2 * depth * width),
        name="weights_ahead",
    )(in_vmem(keyval), in_hbm(query))


def keyval_kernel(where, text, own, sibling, gain, weight, bias, rows_all, *rest):
    parts, keyval = rest[:-1], rest[-1]
    texts, images = text.shape[0], own.shape[0]
    mp = where[0]
    half = own.shape[1]
    mine = mp % 2
    first, second = own[...].astype(F32), sibling[...].astype(F32)
    squares = jnp.sum(first * first, axis=-1, keepdims=True) + jnp.sum(second * second, axis=-1, keepdims=True)
    scale = lax.rsqrt(squares / (2 * half) + 1e-06)
    for values, which in ((first, mine), (second, 1 - mine)):
        here = pl.ds(pl.multiple_of(which * half, half), half)
        rows_all[pl.ds(texts, images), here] = (values * scale * gain[:, here]).astype(BF16)
    rows_all[pl.ds(0, texts), :] = text[...]
    columns = weight.shape[1] // 2
    sums = dot(rows_all[...], weight[...])
    for t in range(2):
        keyval[t] = (sums[:, t * columns : (t + 1) * columns] + bias[pl.ds(t, 1), :]).astype(BF16)

    count = len(parts)
    width = parts[0].shape[1]
    heads = KV_HEADS // count
    coords = columns // KV_HEADS
    row = lax.broadcasted_iota(jnp.int32, (columns, width // 2), 0)
    column = lax.broadcasted_iota(jnp.int32, (columns, width // 2), 1)
    for x in range(count):
        head = (mp ^ x) * heads + column // coords
        pick = (row == (column % coords) * KV_HEADS + head).astype(F32).astype(BF16)
        for t in range(2):
            parts[x][:, pl.ds(t * (width // 2), width // 2)] = dot(keyval[t], pick).astype(BF16)


def keyval_parts(where, text, own, sibling, gain, weight, bias, count):
    texts, depth = text.shape
    columns = weight.shape[1] // 2
    rows = texts + own.shape[0]
    width = 2 * columns // count
    outs = pl.pallas_call(
        keyval_kernel,
        out_shape=[pltpu.VMEM((rows, depth), BF16)]
        + [jax.ShapeDtypeStruct((rows, width), BF16)] * count,
        in_specs=[SMEM, VMEM, VMEM, VMEM, VMEM, VMEM, VMEM],
        out_specs=[VMEM] * (1 + count),
        scratch_shapes=[pltpu.VMEM((2, rows, columns), BF16)],
        compiler_params=params(8),
        cost_estimate=cost(4 * rows * depth * columns, 4 * depth * columns),
        name="keyval",
    )(where, in_vmem(text), own, sibling, gain, in_vmem(weight), bias)
    return outs[0], outs[1:]


def query_kernel(rows_all, ready, weight, bias, first_half, second_half, image_out, buf, sem):
    width = ready.shape[1]
    texts, half = first_half.shape
    later = buf.shape[0]

    def copy(i):
        return pltpu.make_async_copy(weight.at[:, tile(i + 1, width)], buf.at[i], sem.at[i])

    def columns(i, weights, text_out, offset):
        out = (dot(rows_all[...], weights) + bias[:, tile(i, width)]).astype(BF16)
        text_out[:, pl.ds(i * width - offset, width)] = out[:texts]
        image_out[:, tile(i, width)] = out[texts:]

    begin(copy, 2)
    columns(0, ready[...], first_half, 0)
    for i in range(1, later + 1):
        copy(i - 1).wait()
        if i + 1 < later:
            copy(i + 1).start()
        if i * width < half:
            columns(i, buf[i - 1], first_half, 0)
        else:
            columns(i, buf[i - 1], second_half, half)


def query_rows(rows_all, texts, ready, weight, bias):
    depth = rows_all.shape[1]
    images = rows_all.shape[0] - texts
    columns = weight.shape[1]
    width = ready.shape[1]
    later = columns // width - 1
    return pl.pallas_call(
        query_kernel,
        out_shape=[jax.ShapeDtypeStruct((texts, columns // 2), BF16)] * 2 + [jax.ShapeDtypeStruct((images, columns), BF16)],
        in_specs=[VMEM, VMEM, HBM, VMEM],
        out_specs=[VMEM] * 3,
        scratch_shapes=[pltpu.VMEM((later, depth, width), BF16), pltpu.SemaphoreType.DMA((later,))],
        compiler_params=params(30),
        cost_estimate=cost(2 * (texts + images) * depth * columns, 2 * depth * columns),
        name="query",
    )(in_vmem(rows_all), in_vmem(ready), in_hbm(weight), bias)


def join_matrix(mp, count, width):
    heads = KV_HEADS // count
    coords = HEAD_DIM // count
    full = 2 * heads * HEAD_DIM
    column = lax.broadcasted_iota(jnp.int32, (width, full), 1)
    row = lax.broadcasted_iota(jnp.int32, (width, full), 0)
    base = (row // coords) * HEAD_DIM + row % coords
    places = [(column == base + (mp ^ x) * coords).astype(F32).astype(BF16) for x in range(count)]
    return jnp.concatenate(places, axis=0)


def slots_kernel(owners, where, owner_row, queries, *rest):
    parts, outs = rest[:-owners], rest[-owners:]
    rows, columns = queries.shape
    capacity = outs[0].shape[0]
    slots = owners * capacity
    me = where[1]
    row = lax.broadcasted_iota(jnp.int32, (owners * rows, rows), 0)
    mine = (row == me * rows + lax.broadcasted_iota(jnp.int32, (owners * rows, rows), 1)).astype(F32).astype(BF16)
    named = (owner_row[...] ^ me).astype(F32).astype(BF16)
    across = dot(named, mine)
    down = lax.dot_general(mine, named, (((0,), (1,)), ((), ())), preferred_element_type=F32)
    earlier = lax.broadcasted_iota(jnp.int32, (rows, rows), 0) < lax.broadcasted_iota(jnp.int32, (rows, rows), 1)
    rank = jnp.sum(jnp.where((down == across) & earlier, 1.0, 0.0), axis=0, keepdims=True)
    slot = across * capacity + rank
    select = (lax.broadcasted_iota(jnp.int32, (slots, rows), 0).astype(F32) == slot).astype(F32).astype(BF16)
    width = parts[0].shape[1]
    images = [queries[...]] + [part[pl.ds(part.shape[0] - rows, rows), :] for part in parts]
    chosen = dot(select, jnp.concatenate(images, axis=1))
    for x, out in enumerate(outs):
        out[...] = chosen[x * capacity : (x + 1) * capacity].astype(BF16)


def slots_of(where, owner_row, queries, parts, owners, capacity):
    width = queries.shape[1] + len(parts) * parts[0].shape[1]
    return pl.pallas_call(
        functools.partial(slots_kernel, owners),
        out_shape=[jax.ShapeDtypeStruct((capacity, width), BF16)] * owners,
        in_specs=[SMEM] + [VMEM] * (2 + len(parts)),
        out_specs=[VMEM] * owners,
        compiler_params=params(8),
        name="slots",
    )(where, owner_row, queries, *parts)


def attend(blocks, first, doc_row, queries, kv_all, out):
    q_first, k_first, out_first = first
    groups = kv_all.shape[1] // (2 * HEAD_DIM)
    per_half = groups // len(queries)
    shared = queries[0].shape[1] // HEAD_DIM // per_half
    block = DOC_MAX
    scale = 1.0 / math.sqrt(HEAD_DIM)
    docs = doc_row[...].astype(F32)
    row = lax.broadcasted_iota(jnp.int32, (block, 2 * block), 0)
    column = lax.broadcasted_iota(jnp.int32, (block, 2 * block), 1)
    for b in range(*blocks):
        q0 = b * block
        k0 = max(0, b - 1) * block
        k_doc = docs[:, k0 : k0 + 2 * block]
        q_doc = jnp.sum(jnp.where(k0 + column == q0 + row, k_doc, 0.0), axis=1, keepdims=True)
        allowed = (q_doc == k_doc) & (k0 + column <= q0 + row)
        penalty = jnp.concatenate([jnp.where(allowed, 0.0, -1e30)] * shared, axis=0)
        for g in range(groups):
            keys = kv_all[pl.ds(k0 - k_first, 2 * block), tile(g, HEAD_DIM)]
            values = kv_all[pl.ds(k0 - k_first, 2 * block), tile(groups + g, HEAD_DIM)]
            source = queries[g // per_half]
            columns = [tile((g % per_half) * shared + h, HEAD_DIM) for h in range(shared)]
            q = jnp.concatenate([source[pl.ds(q0 - q_first, block), c] for c in columns], axis=0)
            scores = lax.dot_general(q, keys, (((1,), (1,)), ((), ())), preferred_element_type=F32) * scale
            scores = jnp.where(penalty < 0.0, penalty, scores)
            weights = jnp.exp(scores - jnp.max(scores, axis=-1, keepdims=True))
            probs = (weights * (1.0 / jnp.sum(weights, axis=-1, keepdims=True))).astype(BF16)
            result = dot(probs, values).astype(BF16)
            for h in range(shared):
                out[pl.ds(q0 - out_first, block), tile(g * shared + h, HEAD_DIM)] = result[h * block : (h + 1) * block]
        yield b


def late_kernel(early, owners, where, owner_row, doc_row, first_half, second_half, *rest):
    parts = rest[:-4]
    out, kv_all, join, place = rest[-4:]
    mp, me = where[0], where[1]
    seq = first_half.shape[0]
    join[...] = join_matrix(mp, len(parts), parts[0].shape[1])
    sent = jnp.concatenate([part[pl.ds(0, seq), :] for part in parts], axis=1)
    kv_all[...] = dot(sent, join[...]).astype(BF16)
    slots = place.shape[0]
    capacity = slots // owners
    named = (owner_row[...] == me).astype(F32).astype(BF16)
    total = owner_row.shape[1]
    source = lax.broadcasted_iota(jnp.int32, (total, slots), 0) // (total // owners)
    block = (lax.broadcasted_iota(jnp.int32, (total, slots), 1) // capacity) ^ me
    here = dot(named, (source == block).astype(F32).astype(BF16))
    offset = dot(named, (source < block).astype(F32).astype(BF16))
    index = (lax.broadcasted_iota(jnp.int32, (1, slots), 1) % capacity).astype(F32)
    target = jnp.where(index < here, offset + index, -1.0)
    position = lax.broadcasted_iota(jnp.int32, (slots, slots), 0).astype(F32)
    place[...] = (position == target).astype(F32).astype(BF16)
    blocks = (early // DOC_MAX, seq // DOC_MAX)
    for _ in attend(blocks, (0, 0, early), doc_row, (first_half, second_half), kv_all, out):
        pass


def early_kernel(early, doc_row, first_half, second_half, keyval, join, place, *rest):
    arrived = rest[:-7]
    late, out, first, second, kv_all, result, sem = rest[-7:]
    slots = place.shape[0]
    copies = [pltpu.make_async_copy(late, out.at[pl.ds(early, late.shape[0])], sem.at[0])]
    copies[0].start()
    half = first_half.shape[1]
    together = jnp.concatenate([rows[...].astype(F32) for rows in arrived], axis=0).astype(BF16)
    placed = dot(place[...], together).astype(BF16)
    is_image = jnp.sum(place[...].astype(F32), axis=1, keepdims=True) > 0.5
    image_keyval = dot(placed[:, 2 * half :], join[...]).astype(BF16)
    kv_all[...] = keyval[pl.ds(0, early), :]
    kv_all[pl.ds(0, slots), :] = jnp.where(is_image, image_keyval, keyval[pl.ds(0, slots), :])
    for i, (source, target) in enumerate(((first_half, first), (second_half, second))):
        target[...] = source[pl.ds(0, early), :]
        target[pl.ds(0, slots), :] = jnp.where(
            is_image, placed[:, i * half : (i + 1) * half], source[pl.ds(0, slots), :]
        )
    for b in attend((0, early // DOC_MAX), (0, 0, 0), doc_row, (first, second), kv_all, result):
        here = pl.ds(b * DOC_MAX, DOC_MAX)
        copies.append(pltpu.make_async_copy(result.at[here], out.at[here], sem.at[b + 1]))
        copies[-1].start()
    for copy in copies:
        copy.wait()


def attention(where, owner_row, documents, halves, parts, arrived, owners, slots, columns):
    seq = documents.shape[1]
    full = 2 * (KV_HEADS // len(parts)) * HEAD_DIM
    early = min(seq, -(-slots // DOC_MAX) * DOC_MAX + DOC_MAX)
    out, keyval, join, place = pl.pallas_call(
        functools.partial(late_kernel, early, owners),
        out_shape=[
            pltpu.VMEM((seq - early, columns), BF16),
            jax.ShapeDtypeStruct((seq, full), BF16),
            jax.ShapeDtypeStruct((len(parts) * parts[0].shape[1], full), BF16),
            jax.ShapeDtypeStruct((slots, slots), BF16),
        ],
        in_specs=[SMEM] + [VMEM] * (4 + len(parts)),
        out_specs=[VMEM] * 4,
        compiler_params=params(12),
        cost_estimate=cost(4 * (seq - early) * columns * 2 * DOC_MAX, 4 * seq * columns),
        name="attention_late",
    )(where, owner_row, documents, *halves, *parts)
    return pl.pallas_call(
        functools.partial(early_kernel, early),
        out_shape=jax.ShapeDtypeStruct((seq, columns), BF16),
        in_specs=[VMEM] * (7 + owners),
        out_specs=HBM,
        scratch_shapes=[pltpu.VMEM((early, columns // 2), BF16)] * 2
        + [pltpu.VMEM((early, full), BF16), pltpu.VMEM((early, columns), BF16), pltpu.SemaphoreType.DMA((1 + early // DOC_MAX,))],
        compiler_params=params(12),
        cost_estimate=cost(4 * early * columns * 2 * DOC_MAX, 4 * seq * columns),
        name="attention_early",
    )(documents, *halves, keyval, join, place, *arrived(out), in_vmem(out))


def after(x, *others):
    return lax.optimization_barrier((x, *others))[0]


def exchange(x, count, bit):
    return lax.ppermute(x, "mp", [(i, i ^ bit) for i in range(count)])


def per_device(
    patch_rows,
    ln_gain,
    ln_bias,
    merge_up,
    merge_up_bias,
    merge_down,
    merge_down_bias,
    row_owner,
    text_embed,
    doc_ids,
    rms_gain,
    w_query,
    query_bias,
    w_keyval,
    keyval_bias,
):
    owners = lax.axis_size(("group", "dp"))
    count = lax.axis_size("mp")
    mp_index = lax.axis_index("mp")
    where = jnp.stack([mp_index, lax.axis_index(("group", "dp"))]).astype(jnp.int32)
    rows = row_owner.shape[0] // owners
    capacity = max(2, 2 * rows // owners)
    owner_row = row_owner.reshape(1, -1)

    send, keep, text = merger(
        where, patch_rows[0], ln_gain, ln_bias, merge_up, merge_up_bias, merge_down, merge_down_bias,
        text_embed[0], rms_gain[None, :], rows,
    )
    own = (keep.astype(F32) + exchange(send, count, 1).astype(F32)).astype(BF16)
    weight, ready = weights_ahead(after(w_keyval, send), w_query, w_query.shape[1] // 4)
    bit = 2
    while bit < count:
        other = after(exchange(own, count, bit), weight)
        own = (own.astype(F32) + other.astype(F32)).astype(BF16)
        bit *= 2
    sibling = exchange(own, count, 1)

    columns = w_query.shape[1]
    rows_all, parts = keyval_parts(where, text, own, sibling, rms_gain[None, :], weight, keyval_bias, count)
    parts = [parts[0]] + [exchange(parts[x], count, x) for x in range(1, count)]
    *halves, image_queries = query_rows(rows_all, text.shape[0], ready, w_query, query_bias[None, :])
    outgoing = slots_of(where, owner_row, image_queries, parts, owners, capacity)

    def arrived(done):
        rows = [
            lax.ppermute(outgoing[x], ("group", "dp"), [(i, i ^ x) for i in range(owners)]) for x in range(1, owners)
        ]
        return lax.optimization_barrier((outgoing[0], *rows, done))[:-1]

    halves = [after(half, outgoing[0]) for half in halves]
    return attention(
        where, owner_row, doc_ids, halves, parts, arrived, owners, owners * capacity, columns
    )[None]


def general(
    patch_rows,
    ln_gain,
    ln_bias,
    merge_up,
    merge_up_bias,
    merge_down,
    merge_down_bias,
    row_owner,
    text_embed,
    doc_ids,
    rms_gain,
    w_query,
    query_bias,
    w_keyval,
    keyval_bias,
):
    owners = lax.axis_size(("group", "dp"))
    own_index = lax.axis_index(("group", "dp"))
    mp_index = lax.axis_index("mp")
    pixels = patch_rows[0].astype(jnp.float32)
    center = pixels - jnp.mean(pixels, axis=-1, keepdims=True)
    spread = jnp.mean(center * center, axis=-1, keepdims=True)
    normed_patch = (center * lax.rsqrt(spread + 1e-06) * ln_gain + ln_bias).astype(jnp.bfloat16)
    merged = normed_patch.reshape(-1, 4 * pixels.shape[1])
    merged_rows = merged.shape[0]
    hidden = jax.nn.gelu(
        jnp.dot(merged, merge_up, preferred_element_type=jnp.float32) + merge_up_bias,
        approximate=False,
    ).astype(jnp.bfloat16)
    partial_sum = jnp.dot(hidden, merge_down, preferred_element_type=jnp.float32)
    vision = (
        lax.psum_scatter(partial_sum, "mp", scatter_dimension=1, tiled=True) + merge_down_bias
    ).astype(jnp.bfloat16)
    col_width = vision.shape[1]
    capacity = max(2, 2 * merged_rows // owners)
    owner_all = row_owner[:, 0]
    owner_ids = jnp.arange(owners, dtype=jnp.int32)
    onehot = (owner_all[:, None] == owner_ids[None, :]).astype(jnp.int32)
    per_source = jnp.sum(onehot.reshape(owners, merged_rows, owners), axis=1)
    my_block = lax.dynamic_slice_in_dim(onehot, own_index * merged_rows, merged_rows, 0)
    block_rank = jnp.sum((jnp.cumsum(my_block, axis=0) - my_block) * my_block, axis=1)
    my_owner = jnp.sum(my_block * owner_ids[None, :], axis=1)
    slot_id = my_owner * capacity + block_rank
    all_slots = jnp.arange(owners * capacity, dtype=jnp.int32)
    select = (slot_id[:, None] == all_slots[None, :]).astype(jnp.bfloat16)
    outgoing = jnp.einsum("ms,mc->sc", select, vision, preferred_element_type=jnp.float32).astype(
        jnp.bfloat16
    )
    arrived = lax.all_to_all(
        outgoing.reshape(owners, capacity, col_width),
        ("group", "dp"),
        split_axis=0,
        concat_axis=0,
        tiled=True,
    )
    arrived = arrived.reshape(owners * capacity, col_width)
    incoming = lax.dynamic_slice_in_dim(per_source, own_index, 1, 1)[:, 0]
    offsets = jnp.cumsum(incoming) - incoming
    total = jnp.sum(incoming)
    slot_rank = jnp.arange(capacity, dtype=jnp.int32)
    target = jnp.where(
        slot_rank[None, :] < incoming[:, None], offsets[:, None] + slot_rank[None, :], -1
    ).reshape(-1)
    text_rows = text_embed[0]
    seq_len = text_rows.shape[0]
    positions = jnp.arange(seq_len, dtype=jnp.int32)
    source_slot = jnp.sum(
        jnp.where(target[:, None] == positions[None, :], all_slots[:, None], 0), axis=0
    )
    is_image = (positions < total)[:, None]
    image_full = lax.all_gather(arrived, "mp", axis=1, tiled=True)
    sequence = jnp.where(is_image, jnp.take(image_full, source_slot, axis=0), text_rows)
    seq_f = sequence.astype(jnp.float32)
    normed_seq = (
        seq_f * lax.rsqrt(jnp.mean(seq_f * seq_f, axis=-1, keepdims=True) + 1e-06) * rms_gain
    ).astype(jnp.bfloat16)
    queries = (
        jnp.dot(normed_seq, w_query, preferred_element_type=jnp.float32) + query_bias
    ).astype(jnp.bfloat16)
    keyval_local = (
        jnp.einsum("sd,dtc->stc", normed_seq, w_keyval, preferred_element_type=jnp.float32)
        + keyval_bias
    ).astype(jnp.bfloat16)
    keyval_full = lax.all_gather(keyval_local, "mp", axis=2, tiled=True)
    keyval_heads = jnp.transpose(keyval_full.reshape(seq_len, 2, HEAD_DIM, KV_HEADS), (0, 1, 3, 2))
    local_heads = queries.shape[1] // HEAD_DIM
    group_size = HEADS // KV_HEADS
    kv_index = (mp_index * local_heads + jnp.arange(local_heads, dtype=jnp.int32)) // group_size
    keys = jnp.take(keyval_heads[:, 0], kv_index, axis=1)
    values = jnp.take(keyval_heads[:, 1], kv_index, axis=1)
    query_heads = queries.reshape(seq_len, local_heads, HEAD_DIM)
    scores = jnp.einsum(
        "qhd,khd->hqk", query_heads, keys, preferred_element_type=jnp.float32
    ) / math.sqrt(HEAD_DIM)
    documents = doc_ids[0]
    allowed = (documents[:, None] == documents[None, :]) & (
        positions[None, :] <= positions[:, None]
    )
    scores = jnp.where(allowed[None], scores, jnp.float32(-1e30))
    highest = jnp.max(scores, axis=-1, keepdims=True)
    weights = jnp.exp(scores - highest)
    probs = (weights / jnp.sum(weights, axis=-1, keepdims=True)).astype(jnp.bfloat16)
    output = jnp.einsum("hqk,khd->qhd", probs, values, preferred_element_type=jnp.float32)
    return output.astype(jnp.bfloat16).reshape(1, seq_len, local_heads * HEAD_DIM)


def solution(mesh):
    in_specs = (
        P(("group", "dp"), None, None),
        P(),
        P(),
        P(None, "mp"),
        P("mp"),
        P("mp", None),
        P("mp"),
        P(),
        P(("group", "dp"), None, None),
        P(("group", "dp"), None),
        P(),
        P(None, "mp"),
        P("mp"),
        P(None, None, "mp"),
        P(None, "mp"),
    )
    out_specs = P(("group", "dp"), None, "mp")
    count = mesh.shape["mp"]
    owners = mesh.shape["group"] * mesh.shape["dp"]
    narrow = count < 2 or count > KV_HEADS or count & (count - 1) or owners & (owners - 1)
    body = general if narrow else per_device
    return jax.shard_map(body, mesh=mesh, in_specs=in_specs, out_specs=out_specs, check_vma=False)
```

```python
import functools
import math

import jax
import jax.numpy as jnp
from jax import lax
from jax.experimental import pallas as pl
from jax.experimental.pallas import tpu as pltpu
from jax.sharding import PartitionSpec as P

HEADS = 64
KV_HEADS = 8
HEAD_DIM = 128
DOC_MAX = 64

BF16 = jnp.bfloat16
F32 = jnp.float32
VMEM = pl.BlockSpec(memory_space=pltpu.VMEM)
SMEM = pl.BlockSpec(memory_space=pltpu.SMEM)
ANY = pl.BlockSpec(memory_space=pl.ANY)
HBM = pl.BlockSpec(memory_space=pltpu.HBM)
AHEAD = 3
DEEP = 5
MIB = 1 << 20


def dot(a, b):
    return jnp.dot(a, b, preferred_element_type=F32)


def in_hbm(x):
    return pltpu.with_memory_space_constraint(x, pltpu.HBM)


def in_vmem(x):
    return pltpu.with_memory_space_constraint(x, pltpu.VMEM)


def params(mib):
    return pltpu.CompilerParams(vmem_limit_bytes=mib * MIB)


def cost(flops, nbytes):
    return pl.CostEstimate(flops=flops, bytes_accessed=nbytes, transcendentals=0)


def rms_scale(x, width):
    return lax.rsqrt(jnp.sum(x * x, axis=-1, keepdims=True) / width + 1e-06)


def stream(count, copy, body, ahead=AHEAD, then=None):
    @pl.loop(0, count)
    def _(i):
        copy(i).wait()

        @pl.when(i + ahead < count)
        def _():
            copy(i + ahead).start()

        if then is not None:

            @pl.when(i + ahead >= count)
            def _():
                then(i + ahead - count).start()

        body(i)


def begin(copy, ahead=AHEAD):
    for i in range(ahead):
        copy(i).start()


def tile(i, width):
    return pl.ds(pl.multiple_of(i * width, width), width)


def merger_kernel(
    where, patch_in, gain_in, bias_in, up, up_bias_in, down, down_bias_in, text, rms_gain_in, send, keep, text_out,
    patch, gain, bias, up_bias, down_bias, rms_gain, bias_row, normed, merged, total, up_buf, down_buf, text_buf,
    small_sem, up_sem, down_sem, text_sem,
):
    slots = DEEP + 1
    step = up_buf.shape[1]
    width = down_buf.shape[2]
    half = send.shape[1]
    per_half = half // width
    mp = where[0]
    mine = mp % 2
    pairs = [(patch_in, patch), (gain_in, gain), (bias_in, bias), (up_bias_in, up_bias), (down_bias_in, down_bias)]
    pairs.append((rms_gain_in, rms_gain))
    small = [pltpu.make_async_copy(x, y, small_sem.at[i]) for i, (x, y) in enumerate(pairs)]
    for copy in small:
        copy.start()

    def up_copy(i):
        return pltpu.make_async_copy(up.at[tile(i, step)], up_buf.at[i % slots], up_sem.at[i % slots])

    def column(i):
        first = jnp.where(i < per_half, 1 - mine, mine)
        return pl.multiple_of(first * half + (i % per_half) * width, width)

    def down_copy(i):
        return pltpu.make_async_copy(
            down.at[:, pl.ds(column(i), width)], down_buf.at[i % slots], down_sem.at[i % slots]
        )

    block = text_buf.shape[1]
    blocks = text.shape[0] // block

    def text_copy(i):
        return pltpu.make_async_copy(text.at[tile(i, block)], text_buf.at[i % slots], text_sem.at[i % slots])

    def text_norm(i):
        text_copy(i).wait()

        @pl.when(i + DEEP < blocks)
        def _():
            text_copy(i + DEEP).start()

        x = text_buf[i % slots].astype(F32)
        text_out[tile(i, block), :] = (x * rms_scale(x, x.shape[1]) * rms_gain[...]).astype(BF16)

    begin(up_copy, DEEP)
    begin(text_copy, DEEP)
    for copy in small:
        copy.wait()
    rows = send.shape[0]
    joined = patch.shape[0] // rows
    features = patch.shape[1]
    pixels = patch[...].astype(F32)
    center = pixels - jnp.mean(pixels, axis=-1, keepdims=True)
    spread = jnp.mean(center * center, axis=-1, keepdims=True)
    patches = center * lax.rsqrt(spread + 1e-06) * gain[...][None, :] + bias[...][None, :]
    for c in range(features // 128):
        normed[c] = patches[:, c * 128 : (c + 1) * 128]
        for j in range(joined):
            merged[:, pl.ds(j * features + c * 128, 128)] = normed[c, pl.ds(j, rows, stride=joined), :].astype(BF16)
    own = down_bias.shape[0]
    bias_row[...] = jnp.zeros_like(bias_row)
    bias_row[:, pl.ds(pl.multiple_of(mp * own, 128), own)] = down_bias[...][None, :]
    total[...] = jnp.broadcast_to(up_bias[...][None, :], total.shape)

    def up_body(i):
        text_norm(i)
        total[...] += dot(merged[:, tile(i, step)], up_buf[i % slots])

    up_steps = up.shape[0] // step
    stream(up_steps, up_copy, up_body, DEEP, down_copy)
    sums = total[...]
    hidden = (0.5 * sums * (1.0 + lax.erf(sums * math.sqrt(0.5)))).astype(BF16)

    def down_body(i):
        text_norm(up_steps + i)
        part = (dot(hidden, down_buf[i % slots]) + bias_row[:, pl.ds(column(i), width)]).astype(BF16)
        here = tile(i % per_half, width)

        @pl.when(i < per_half)
        def _():
            send[:, here] = part

        @pl.when(i >= per_half)
        def _():
            keep[:, here] = part

    stream(2 * per_half, down_copy, down_body, DEEP)


def merger(where, patch, gain, bias, up, up_bias, down, down_bias, text, rms_gain, rows):
    features = patch.shape[1]
    depth, hidden = up.shape
    columns = down.shape[1]
    step = depth // 8
    width = columns // 8
    slots = DEEP + 1
    return pl.pallas_call(
        merger_kernel,
        out_shape=[jax.ShapeDtypeStruct((rows, columns // 2), BF16)] * 2 + [pltpu.VMEM(text.shape, BF16)],
        in_specs=[SMEM] + [HBM] * 9,
        out_specs=[VMEM, VMEM, VMEM],
        scratch_shapes=[
            pltpu.VMEM(patch.shape, BF16),
            pltpu.VMEM(gain.shape, F32),
            pltpu.VMEM(bias.shape, F32),
            pltpu.VMEM(up_bias.shape, F32),
            pltpu.VMEM(down_bias.shape, F32),
            pltpu.VMEM(rms_gain.shape, F32),
            pltpu.VMEM((1, columns), F32),
            pltpu.VMEM((features // 128, patch.shape[0], 128), F32),
            pltpu.VMEM((rows, depth), BF16),
            pltpu.VMEM((rows, hidden), F32),
            pltpu.VMEM((slots, step, hidden), BF16),
            pltpu.VMEM((slots, hidden, width), BF16),
            pltpu.VMEM((slots, text.shape[0] // 16, text.shape[1]), BF16),
            pltpu.SemaphoreType.DMA((6,)),
            pltpu.SemaphoreType.DMA((slots,)),
            pltpu.SemaphoreType.DMA((slots,)),
            pltpu.SemaphoreType.DMA((slots,)),
        ],
        compiler_params=params(34),
        cost_estimate=cost(2 * rows * hidden * (depth + columns), 2 * hidden * (depth + columns)),
        name="merger",
    )(where, *map(in_hbm, (patch, gain, bias, up, up_bias, down, down_bias, text, rms_gain)))


def weights_kernel(keyval, query, out, query_out, sem):
    depth, _, columns = keyval.shape
    pieces = sem.shape[0]
    step = depth // pieces
    width = query_out.shape[1]
    copies = [
        pltpu.make_async_copy(query.at[pl.ds(i * step, step), pl.ds(0, width)], query_out.at[pl.ds(i * step, step)], sem.at[i])
        for i in range(pieces)
    ]
    for copy in copies:
        copy.start()
    pairs = keyval.reshape(2 * depth, columns)
    row = lax.broadcasted_iota(jnp.int32, (256, 256), 0)
    column = lax.broadcasted_iota(jnp.int32, (256, 256), 1)
    apart = (column == 2 * (row % 128) + row // 128).astype(F32).astype(BF16)
    together = 8

    @pl.loop(0, depth // (128 * together))
    def _(j):
        blocks = [pairs[tile(j * together + n, 256), :] for n in range(together)]
        ordered = dot(apart, jnp.concatenate(blocks, axis=1)).astype(BF16)
        for n in range(together):
            for side in range(2):
                out[tile(j * together + n, 128), pl.ds(side * columns, columns)] = ordered[
                    side * 128 : (side + 1) * 128, n * columns : (n + 1) * columns
                ]

    for copy in copies:
        copy.wait()


def weights_ahead(keyval, query, width):
    depth, _, columns = keyval.shape
    return pl.pallas_call(
        weights_kernel,
        out_shape=[pltpu.VMEM((depth, 2 * columns), BF16), pltpu.VMEM((depth, width), BF16)],
        in_specs=[VMEM, HBM],
        out_specs=[VMEM, VMEM],
        scratch_shapes=[pltpu.SemaphoreType.DMA((4,))],
        compiler_params=params(8),
        cost_estimate=cost(4 * depth * columns * 256, 4 * depth * columns + 2 * depth * width),
        name="weights_ahead",
    )(in_vmem(keyval), in_hbm(query))


def keyval_kernel(where, text, own, sibling, gain, weight, bias, rows_all, *rest):
    parts, keyval = rest[:-1], rest[-1]
    texts, images = text.shape[0], own.shape[0]
    mp = where[0]
    half = own.shape[1]
    mine = mp % 2
    first, second = own[...].astype(F32), sibling[...].astype(F32)
    squares = jnp.sum(first * first, axis=-1, keepdims=True) + jnp.sum(second * second, axis=-1, keepdims=True)
    scale = lax.rsqrt(squares / (2 * half) + 1e-06)
    for values, which in ((first, mine), (second, 1 - mine)):
        here = pl.ds(pl.multiple_of(which * half, half), half)
        rows_all[pl.ds(texts, images), here] = (values * scale * gain[:, here]).astype(BF16)
    rows_all[pl.ds(0, texts), :] = text[...]
    columns = weight.shape[1] // 2
    sums = dot(rows_all[...], weight[...])
    for t in range(2):
        keyval[t] = (sums[:, t * columns : (t + 1) * columns] + bias[pl.ds(t, 1), :]).astype(BF16)

    count = len(parts)
    width = parts[0].shape[1]
    heads = KV_HEADS // count
    coords = columns // KV_HEADS
    row = lax.broadcasted_iota(jnp.int32, (columns, width // 2), 0)
    column = lax.broadcasted_iota(jnp.int32, (columns, width // 2), 1)
    for x in range(count):
        head = (mp ^ x) * heads + column // coords
        pick = (row == (column % coords) * KV_HEADS + head).astype(F32).astype(BF16)
        for t in range(2):
            parts[x][:, pl.ds(t * (width // 2), width // 2)] = dot(keyval[t], pick).astype(BF16)


def keyval_parts(where, text, own, sibling, gain, weight, bias, count):
    texts, depth = text.shape
    columns = weight.shape[1] // 2
    rows = texts + own.shape[0]
    width = 2 * columns // count
    outs = pl.pallas_call(
        keyval_kernel,
        out_shape=[pltpu.VMEM((rows, depth), BF16)]
        + [jax.ShapeDtypeStruct((rows, width), BF16)] * count,
        in_specs=[SMEM, VMEM, VMEM, VMEM, VMEM, VMEM, VMEM],
        out_specs=[VMEM] * (1 + count),
        scratch_shapes=[pltpu.VMEM((2, rows, columns), BF16)],
        compiler_params=params(8),
        cost_estimate=cost(4 * rows * depth * columns, 4 * depth * columns),
        name="keyval",
    )(where, in_vmem(text), own, sibling, gain, in_vmem(weight), bias)
    return outs[0], outs[1:]


def query_kernel(rows_all, ready, weight, bias, first_half, second_half, image_out, buf, sem):
    width = ready.shape[1]
    texts, half = first_half.shape
    later = buf.shape[0]

    def copy(i):
        return pltpu.make_async_copy(weight.at[:, tile(i + 1, width)], buf.at[i], sem.at[i])

    def columns(i, weights, text_out, offset):
        out = (dot(rows_all[...], weights) + bias[:, tile(i, width)]).astype(BF16)
        text_out[:, pl.ds(i * width - offset, width)] = out[:texts]
        image_out[:, tile(i, width)] = out[texts:]

    begin(copy, 2)
    columns(0, ready[...], first_half, 0)
    for i in range(1, later + 1):
        copy(i - 1).wait()
        if i + 1 < later:
            copy(i + 1).start()
        if i * width < half:
            columns(i, buf[i - 1], first_half, 0)
        else:
            columns(i, buf[i - 1], second_half, half)


def query_rows(rows_all, texts, ready, weight, bias):
    depth = rows_all.shape[1]
    images = rows_all.shape[0] - texts
    columns = weight.shape[1]
    width = ready.shape[1]
    later = columns // width - 1
    return pl.pallas_call(
        query_kernel,
        out_shape=[jax.ShapeDtypeStruct((texts, columns // 2), BF16)] * 2 + [jax.ShapeDtypeStruct((images, columns), BF16)],
        in_specs=[VMEM, VMEM, HBM, VMEM],
        out_specs=[VMEM] * 3,
        scratch_shapes=[pltpu.VMEM((later, depth, width), BF16), pltpu.SemaphoreType.DMA((later,))],
        compiler_params=params(30),
        cost_estimate=cost(2 * (texts + images) * depth * columns, 2 * depth * columns),
        name="query",
    )(in_vmem(rows_all), in_vmem(ready), in_hbm(weight), bias)


def join_matrix(mp, count, width):
    heads = KV_HEADS // count
    coords = HEAD_DIM // count
    full = 2 * heads * HEAD_DIM
    column = lax.broadcasted_iota(jnp.int32, (width, full), 1)
    row = lax.broadcasted_iota(jnp.int32, (width, full), 0)
    base = (row // coords) * HEAD_DIM + row % coords
    places = [(column == base + (mp ^ x) * coords).astype(F32).astype(BF16) for x in range(count)]
    return jnp.concatenate(places, axis=0)


def slots_kernel(owners, where, owner_row, queries, *rest):
    parts, outs = rest[:-owners], rest[-owners:]
    rows, columns = queries.shape
    capacity = outs[0].shape[0]
    slots = owners * capacity
    me = where[1]
    row = lax.broadcasted_iota(jnp.int32, (owners * rows, rows), 0)
    mine = (row == me * rows + lax.broadcasted_iota(jnp.int32, (owners * rows, rows), 1)).astype(F32).astype(BF16)
    named = (owner_row[...] ^ me).astype(F32).astype(BF16)
    across = dot(named, mine)
    down = lax.dot_general(mine, named, (((0,), (1,)), ((), ())), preferred_element_type=F32)
    earlier = lax.broadcasted_iota(jnp.int32, (rows, rows), 0) < lax.broadcasted_iota(jnp.int32, (rows, rows), 1)
    rank = jnp.sum(jnp.where((down == across) & earlier, 1.0, 0.0), axis=0, keepdims=True)
    slot = across * capacity + rank
    select = (lax.broadcasted_iota(jnp.int32, (slots, rows), 0).astype(F32) == slot).astype(F32).astype(BF16)
    width = parts[0].shape[1]
    images = [queries[...]] + [part[pl.ds(part.shape[0] - rows, rows), :] for part in parts]
    chosen = dot(select, jnp.concatenate(images, axis=1))
    for x, out in enumerate(outs):
        out[...] = chosen[x * capacity : (x + 1) * capacity].astype(BF16)


def slots_of(where, owner_row, queries, parts, owners, capacity):
    width = queries.shape[1] + len(parts) * parts[0].shape[1]
    return pl.pallas_call(
        functools.partial(slots_kernel, owners),
        out_shape=[jax.ShapeDtypeStruct((capacity, width), BF16)] * owners,
        in_specs=[SMEM] + [VMEM] * (2 + len(parts)),
        out_specs=[VMEM] * owners,
        compiler_params=params(8),
        name="slots",
    )(where, owner_row, queries, *parts)


def attend(blocks, first, doc_row, queries, kv_all, out):
    q_first, k_first, out_first = first
    groups = kv_all.shape[1] // (2 * HEAD_DIM)
    per_half = groups // len(queries)
    shared = queries[0].shape[1] // HEAD_DIM // per_half
    block = DOC_MAX
    scale = 1.0 / math.sqrt(HEAD_DIM)
    docs = doc_row[...].astype(F32)
    row = lax.broadcasted_iota(jnp.int32, (block, 2 * block), 0)
    column = lax.broadcasted_iota(jnp.int32, (block, 2 * block), 1)
    for b in range(*blocks):
        q0 = b * block
        k0 = max(0, b - 1) * block
        k_doc = docs[:, k0 : k0 + 2 * block]
        q_doc = jnp.sum(jnp.where(k0 + column == q0 + row, k_doc, 0.0), axis=1, keepdims=True)
        allowed = (q_doc == k_doc) & (k0 + column <= q0 + row)
        penalty = jnp.concatenate([jnp.where(allowed, 0.0, -1e30)] * shared, axis=0)
        for g in range(groups):
            keys = kv_all[pl.ds(k0 - k_first, 2 * block), tile(g, HEAD_DIM)]
            values = kv_all[pl.ds(k0 - k_first, 2 * block), tile(groups + g, HEAD_DIM)]
            source = queries[g // per_half]
            columns = [tile((g % per_half) * shared + h, HEAD_DIM) for h in range(shared)]
            q = jnp.concatenate([source[pl.ds(q0 - q_first, block), c] for c in columns], axis=0)
            scores = lax.dot_general(q, keys, (((1,), (1,)), ((), ())), preferred_element_type=F32) * scale
            scores = jnp.where(penalty < 0.0, penalty, scores)
            weights = jnp.exp(scores - jnp.max(scores, axis=-1, keepdims=True))
            probs = (weights * (1.0 / jnp.sum(weights, axis=-1, keepdims=True))).astype(BF16)
            result = dot(probs, values).astype(BF16)
            for h in range(shared):
                out[pl.ds(q0 - out_first, block), tile(g * shared + h, HEAD_DIM)] = result[h * block : (h + 1) * block]
        yield b


def late_kernel(early, owners, where, owner_row, doc_row, first_half, second_half, *rest):
    parts = rest[:-4]
    out, kv_all, join, place = rest[-4:]
    mp, me = where[0], where[1]
    seq = first_half.shape[0]
    join[...] = join_matrix(mp, len(parts), parts[0].shape[1])
    sent = jnp.concatenate([part[pl.ds(0, seq), :] for part in parts], axis=1)
    kv_all[...] = dot(sent, join[...]).astype(BF16)
    slots = place.shape[0]
    capacity = slots // owners
    named = (owner_row[...] == me).astype(F32).astype(BF16)
    total = owner_row.shape[1]
    source = lax.broadcasted_iota(jnp.int32, (total, slots), 0) // (total // owners)
    block = (lax.broadcasted_iota(jnp.int32, (total, slots), 1) // capacity) ^ me
    here = dot(named, (source == block).astype(F32).astype(BF16))
    offset = dot(named, (source < block).astype(F32).astype(BF16))
    index = (lax.broadcasted_iota(jnp.int32, (1, slots), 1) % capacity).astype(F32)
    target = jnp.where(index < here, offset + index, -1.0)
    position = lax.broadcasted_iota(jnp.int32, (slots, slots), 0).astype(F32)
    place[...] = (position == target).astype(F32).astype(BF16)
    blocks = (early // DOC_MAX, seq // DOC_MAX)
    for _ in attend(blocks, (0, 0, early), doc_row, (first_half, second_half), kv_all, out):
        pass


def early_kernel(early, order, doc_row, first_half, second_half, keyval, join, place, *rest):
    arrived = rest[:-7]
    late, out, first, second, kv_all, result, sem = rest[-7:]
    slots = place.shape[0]
    copies = [pltpu.make_async_copy(late, out.at[pl.ds(early, late.shape[0])], sem.at[0])]
    copies[0].start()
    half = first_half.shape[1]
    in_place = [arrived[order.index(x)][...].astype(F32) for x in range(len(order))]
    together = jnp.concatenate(in_place, axis=0).astype(BF16)
    placed = dot(place[...], together).astype(BF16)
    is_image = jnp.sum(place[...].astype(F32), axis=1, keepdims=True) > 0.5
    image_keyval = dot(placed[:, 2 * half :], join[...]).astype(BF16)
    kv_all[...] = keyval[pl.ds(0, early), :]
    kv_all[pl.ds(0, slots), :] = jnp.where(is_image, image_keyval, keyval[pl.ds(0, slots), :])
    for i, (source, target) in enumerate(((first_half, first), (second_half, second))):
        target[...] = source[pl.ds(0, early), :]
        target[pl.ds(0, slots), :] = jnp.where(
            is_image, placed[:, i * half : (i + 1) * half], source[pl.ds(0, slots), :]
        )
    for b in attend((0, early // DOC_MAX), (0, 0, 0), doc_row, (first, second), kv_all, result):
        here = pl.ds(b * DOC_MAX, DOC_MAX)
        copies.append(pltpu.make_async_copy(result.at[here], out.at[here], sem.at[b + 1]))
        copies[-1].start()
    for copy in copies:
        copy.wait()


def attention(where, owner_row, documents, halves, parts, arrived, order, owners, slots, columns):
    seq = documents.shape[1]
    full = 2 * (KV_HEADS // len(parts)) * HEAD_DIM
    early = min(seq, -(-slots // DOC_MAX) * DOC_MAX + DOC_MAX)
    out, keyval, join, place = pl.pallas_call(
        functools.partial(late_kernel, early, owners),
        out_shape=[
            pltpu.VMEM((seq - early, columns), BF16),
            jax.ShapeDtypeStruct((seq, full), BF16),
            jax.ShapeDtypeStruct((len(parts) * parts[0].shape[1], full), BF16),
            jax.ShapeDtypeStruct((slots, slots), BF16),
        ],
        in_specs=[SMEM] + [VMEM] * (4 + len(parts)),
        out_specs=[VMEM] * 4,
        compiler_params=params(12),
        cost_estimate=cost(4 * (seq - early) * columns * 2 * DOC_MAX, 4 * seq * columns),
        name="attention_late",
    )(where, owner_row, documents, *halves, *parts)
    return pl.pallas_call(
        functools.partial(early_kernel, early, order),
        out_shape=jax.ShapeDtypeStruct((seq, columns), BF16),
        in_specs=[VMEM] * (7 + owners),
        out_specs=HBM,
        scratch_shapes=[pltpu.VMEM((early, columns // 2), BF16)] * 2
        + [pltpu.VMEM((early, full), BF16), pltpu.VMEM((early, columns), BF16), pltpu.SemaphoreType.DMA((1 + early // DOC_MAX,))],
        compiler_params=params(12),
        cost_estimate=cost(4 * early * columns * 2 * DOC_MAX, 4 * seq * columns),
        name="attention_early",
    )(documents, *halves, keyval, join, place, *arrived(out), in_vmem(out))


def after(x, *others):
    return lax.optimization_barrier((x, *others))[0]


def exchange(x, count, bit):
    return lax.ppermute(x, "mp", [(i, i ^ bit) for i in range(count)])


def per_device(
    patch_rows,
    ln_gain,
    ln_bias,
    merge_up,
    merge_up_bias,
    merge_down,
    merge_down_bias,
    row_owner,
    text_embed,
    doc_ids,
    rms_gain,
    w_query,
    query_bias,
    w_keyval,
    keyval_bias,
):
    owners = lax.axis_size(("group", "dp"))
    count = lax.axis_size("mp")
    mp_index = lax.axis_index("mp")
    where = jnp.stack([mp_index, lax.axis_index(("group", "dp"))]).astype(jnp.int32)
    rows = row_owner.shape[0] // owners
    capacity = max(2, 2 * rows // owners)
    owner_row = row_owner.reshape(1, -1)
    groups, line = lax.axis_size("group"), lax.axis_size("dp")

    def far(x):
        return max(abs(i % line - (i ^ x) % line) + (x >= line) for i in range(groups * line))


    send, keep, text = merger(
        where, patch_rows[0], ln_gain, ln_bias, merge_up, merge_up_bias, merge_down, merge_down_bias,
        text_embed[0], rms_gain[None, :], rows,
    )
    own = (keep.astype(F32) + exchange(send, count, 1).astype(F32)).astype(BF16)
    weight, ready = weights_ahead(after(w_keyval, send), w_query, w_query.shape[1] // 4)
    bit = 2
    while bit < count:
        other = after(exchange(own, count, bit), weight)
        own = (own.astype(F32) + other.astype(F32)).astype(BF16)
        bit *= 2
    sibling = exchange(own, count, 1)

    columns = w_query.shape[1]
    rows_all, parts = keyval_parts(where, text, own, sibling, rms_gain[None, :], weight, keyval_bias, count)
    parts = [parts[0]] + [exchange(parts[x], count, x) for x in range(1, count)]
    *halves, image_queries = query_rows(rows_all, text.shape[0], ready, w_query, query_bias[None, :])
    outgoing = slots_of(where, owner_row, image_queries, parts, owners, capacity)

    order = sorted(range(1, owners), key=far, reverse=True)

    def arrived(done):
        rows = [lax.ppermute(outgoing[x], ("group", "dp"), [(i, i ^ x) for i in range(owners)]) for x in order]
        return lax.optimization_barrier((*rows, outgoing[0], done))[:-1]

    halves = [after(half, outgoing[0]) for half in halves]
    return attention(
        where, owner_row, doc_ids, halves, parts, arrived, [*order, 0], owners, owners * capacity, columns
    )[None]


def general(
    patch_rows,
    ln_gain,
    ln_bias,
    merge_up,
    merge_up_bias,
    merge_down,
    merge_down_bias,
    row_owner,
    text_embed,
    doc_ids,
    rms_gain,
    w_query,
    query_bias,
    w_keyval,
    keyval_bias,
):
    owners = lax.axis_size(("group", "dp"))
    own_index = lax.axis_index(("group", "dp"))
    mp_index = lax.axis_index("mp")
    pixels = patch_rows[0].astype(jnp.float32)
    center = pixels - jnp.mean(pixels, axis=-1, keepdims=True)
    spread = jnp.mean(center * center, axis=-1, keepdims=True)
    normed_patch = (center * lax.rsqrt(spread + 1e-06) * ln_gain + ln_bias).astype(jnp.bfloat16)
    merged = normed_patch.reshape(-1, 4 * pixels.shape[1])
    merged_rows = merged.shape[0]
    hidden = jax.nn.gelu(
        jnp.dot(merged, merge_up, preferred_element_type=jnp.float32) + merge_up_bias,
        approximate=False,
    ).astype(jnp.bfloat16)
    partial_sum = jnp.dot(hidden, merge_down, preferred_element_type=jnp.float32)
    vision = (
        lax.psum_scatter(partial_sum, "mp", scatter_dimension=1, tiled=True) + merge_down_bias
    ).astype(jnp.bfloat16)
    col_width = vision.shape[1]
    capacity = max(2, 2 * merged_rows // owners)
    owner_all = row_owner[:, 0]
    owner_ids = jnp.arange(owners, dtype=jnp.int32)
    onehot = (owner_all[:, None] == owner_ids[None, :]).astype(jnp.int32)
    per_source = jnp.sum(onehot.reshape(owners, merged_rows, owners), axis=1)
    my_block = lax.dynamic_slice_in_dim(onehot, own_index * merged_rows, merged_rows, 0)
    block_rank = jnp.sum((jnp.cumsum(my_block, axis=0) - my_block) * my_block, axis=1)
    my_owner = jnp.sum(my_block * owner_ids[None, :], axis=1)
    slot_id = my_owner * capacity + block_rank
    all_slots = jnp.arange(owners * capacity, dtype=jnp.int32)
    select = (slot_id[:, None] == all_slots[None, :]).astype(jnp.bfloat16)
    outgoing = jnp.einsum("ms,mc->sc", select, vision, preferred_element_type=jnp.float32).astype(
        jnp.bfloat16
    )
    arrived = lax.all_to_all(
        outgoing.reshape(owners, capacity, col_width),
        ("group", "dp"),
        split_axis=0,
        concat_axis=0,
        tiled=True,
    )
    arrived = arrived.reshape(owners * capacity, col_width)
    incoming = lax.dynamic_slice_in_dim(per_source, own_index, 1, 1)[:, 0]
    offsets = jnp.cumsum(incoming) - incoming
    total = jnp.sum(incoming)
    slot_rank = jnp.arange(capacity, dtype=jnp.int32)
    target = jnp.where(
        slot_rank[None, :] < incoming[:, None], offsets[:, None] + slot_rank[None, :], -1
    ).reshape(-1)
    text_rows = text_embed[0]
    seq_len = text_rows.shape[0]
    positions = jnp.arange(seq_len, dtype=jnp.int32)
    source_slot = jnp.sum(
        jnp.where(target[:, None] == positions[None, :], all_slots[:, None], 0), axis=0
    )
    is_image = (positions < total)[:, None]
    image_full = lax.all_gather(arrived, "mp", axis=1, tiled=True)
    sequence = jnp.where(is_image, jnp.take(image_full, source_slot, axis=0), text_rows)
    seq_f = sequence.astype(jnp.float32)
    normed_seq = (
        seq_f * lax.rsqrt(jnp.mean(seq_f * seq_f, axis=-1, keepdims=True) + 1e-06) * rms_gain
    ).astype(jnp.bfloat16)
    queries = (
        jnp.dot(normed_seq, w_query, preferred_element_type=jnp.float32) + query_bias
    ).astype(jnp.bfloat16)
    keyval_local = (
        jnp.einsum("sd,dtc->stc", normed_seq, w_keyval, preferred_element_type=jnp.float32)
        + keyval_bias
    ).astype(jnp.bfloat16)
    keyval_full = lax.all_gather(keyval_local, "mp", axis=2, tiled=True)
    keyval_heads = jnp.transpose(keyval_full.reshape(seq_len, 2, HEAD_DIM, KV_HEADS), (0, 1, 3, 2))
    local_heads = queries.shape[1] // HEAD_DIM
    group_size = HEADS // KV_HEADS
    kv_index = (mp_index * local_heads + jnp.arange(local_heads, dtype=jnp.int32)) // group_size
    keys = jnp.take(keyval_heads[:, 0], kv_index, axis=1)
    values = jnp.take(keyval_heads[:, 1], kv_index, axis=1)
    query_heads = queries.reshape(seq_len, local_heads, HEAD_DIM)
    scores = jnp.einsum(
        "qhd,khd->hqk", query_heads, keys, preferred_element_type=jnp.float32
    ) / math.sqrt(HEAD_DIM)
    documents = doc_ids[0]
    allowed = (documents[:, None] == documents[None, :]) & (
        positions[None, :] <= positions[:, None]
    )
    scores = jnp.where(allowed[None], scores, jnp.float32(-1e30))
    highest = jnp.max(scores, axis=-1, keepdims=True)
    weights = jnp.exp(scores - highest)
    probs = (weights / jnp.sum(weights, axis=-1, keepdims=True)).astype(jnp.bfloat16)
    output = jnp.einsum("hqk,khd->qhd", probs, values, preferred_element_type=jnp.float32)
    return output.astype(jnp.bfloat16).reshape(1, seq_len, local_heads * HEAD_DIM)


def solution(mesh):
    in_specs = (
        P(("group", "dp"), None, None),
        P(),
        P(),
        P(None, "mp"),
        P("mp"),
        P("mp", None),
        P("mp"),
        P(),
        P(("group", "dp"), None, None),
        P(("group", "dp"), None),
        P(),
        P(None, "mp"),
        P("mp"),
        P(None, None, "mp"),
        P(None, "mp"),
    )
    out_specs = P(("group", "dp"), None, "mp")
    count = mesh.shape["mp"]
    owners = mesh.shape["group"] * mesh.shape["dp"]
    narrow = count < 2 or count > KV_HEADS or count & (count - 1) or owners & (owners - 1)
    body = general if narrow else per_device
    return jax.shard_map(body, mesh=mesh, in_specs=in_specs, out_specs=out_specs, check_vma=False)
```

```python
import functools
import math

import jax
import jax.numpy as jnp
from jax import lax
from jax.experimental import pallas as pl
from jax.experimental.pallas import tpu as pltpu
from jax.sharding import PartitionSpec as P

HEADS = 64
KV_HEADS = 8
HEAD_DIM = 128
DOC_MAX = 64

BF16 = jnp.bfloat16
F32 = jnp.float32
VMEM = pl.BlockSpec(memory_space=pltpu.VMEM)
SMEM = pl.BlockSpec(memory_space=pltpu.SMEM)
ANY = pl.BlockSpec(memory_space=pl.ANY)
HBM = pl.BlockSpec(memory_space=pltpu.HBM)
AHEAD = 3
DEEP = 5
MIB = 1 << 20


def dot(a, b):
    return jnp.dot(a, b, preferred_element_type=F32)


def in_hbm(x):
    return pltpu.with_memory_space_constraint(x, pltpu.HBM)


def in_vmem(x):
    return pltpu.with_memory_space_constraint(x, pltpu.VMEM)


def params(mib):
    return pltpu.CompilerParams(vmem_limit_bytes=mib * MIB)


def cost(flops, nbytes):
    return pl.CostEstimate(flops=flops, bytes_accessed=nbytes, transcendentals=0)


def rms_scale(x, width):
    return lax.rsqrt(jnp.sum(x * x, axis=-1, keepdims=True) / width + 1e-06)


def stream(count, copy, body, ahead=AHEAD, then=None):
    @pl.loop(0, count)
    def _(i):
        copy(i).wait()

        @pl.when(i + ahead < count)
        def _():
            copy(i + ahead).start()

        if then is not None:

            @pl.when(i + ahead >= count)
            def _():
                then(i + ahead - count).start()

        body(i)


def begin(copy, ahead=AHEAD):
    for i in range(ahead):
        copy(i).start()


def tile(i, width):
    return pl.ds(pl.multiple_of(i * width, width), width)


def merger_kernel(
    where, patch_in, gain_in, bias_in, up, up_bias_in, down, down_bias_in, text, rms_gain_in, send, keep, text_out,
    patch, gain, bias, up_bias, down_bias, rms_gain, bias_row, normed, merged, total, up_buf, down_buf, text_buf,
    small_sem, up_sem, down_sem, text_sem,
):
    slots = DEEP + 1
    step = up_buf.shape[1]
    width = down_buf.shape[2]
    half = send.shape[1]
    per_half = half // width
    mp = where[0]
    mine = mp % 2
    pairs = [(patch_in, patch), (gain_in, gain), (bias_in, bias), (up_bias_in, up_bias), (down_bias_in, down_bias)]
    pairs.append((rms_gain_in, rms_gain))
    small = [pltpu.make_async_copy(x, y, small_sem.at[i]) for i, (x, y) in enumerate(pairs)]
    for copy in small:
        copy.start()

    def up_copy(i):
        return pltpu.make_async_copy(up.at[tile(i, step)], up_buf.at[i % slots], up_sem.at[i % slots])

    def column(i):
        first = jnp.where(i < per_half, 1 - mine, mine)
        return pl.multiple_of(first * half + (i % per_half) * width, width)

    def down_copy(i):
        return pltpu.make_async_copy(
            down.at[:, pl.ds(column(i), width)], down_buf.at[i % slots], down_sem.at[i % slots]
        )

    block = text_buf.shape[1]
    blocks = text.shape[0] // block

    def text_copy(i):
        return pltpu.make_async_copy(text.at[tile(i, block)], text_buf.at[i % slots], text_sem.at[i % slots])

    def text_norm(i):
        text_copy(i).wait()

        @pl.when(i + DEEP < blocks)
        def _():
            text_copy(i + DEEP).start()

        x = text_buf[i % slots].astype(F32)
        text_out[tile(i, block), :] = (x * rms_scale(x, x.shape[1]) * rms_gain[...]).astype(BF16)

    begin(up_copy, DEEP)
    begin(text_copy, DEEP)
    for copy in small:
        copy.wait()
    rows = send.shape[0]
    joined = patch.shape[0] // rows
    features = patch.shape[1]
    pixels = patch[...].astype(F32)
    center = pixels - jnp.mean(pixels, axis=-1, keepdims=True)
    spread = jnp.mean(center * center, axis=-1, keepdims=True)
    patches = center * lax.rsqrt(spread + 1e-06) * gain[...][None, :] + bias[...][None, :]
    for c in range(features // 128):
        normed[c] = patches[:, c * 128 : (c + 1) * 128]
        for j in range(joined):
            merged[:, pl.ds(j * features + c * 128, 128)] = normed[c, pl.ds(j, rows, stride=joined), :].astype(BF16)
    own = down_bias.shape[0]
    bias_row[...] = jnp.zeros_like(bias_row)
    bias_row[:, pl.ds(pl.multiple_of(mp * own, 128), own)] = down_bias[...][None, :]
    total[...] = jnp.broadcast_to(up_bias[...][None, :], total.shape)

    def up_body(i):
        text_norm(i)
        total[...] += dot(merged[:, tile(i, step)], up_buf[i % slots])

    up_steps = up.shape[0] // step
    stream(up_steps, up_copy, up_body, DEEP, down_copy)
    sums = total[...]
    hidden = (0.5 * sums * (1.0 + lax.erf(sums * math.sqrt(0.5)))).astype(BF16)

    def down_body(i):
        text_norm(up_steps + i)
        part = (dot(hidden, down_buf[i % slots]) + bias_row[:, pl.ds(column(i), width)]).astype(BF16)
        here = tile(i % per_half, width)

        @pl.when(i < per_half)
        def _():
            send[:, here] = part

        @pl.when(i >= per_half)
        def _():
            keep[:, here] = part

    stream(2 * per_half, down_copy, down_body, DEEP)


def merger(where, patch, gain, bias, up, up_bias, down, down_bias, text, rms_gain, rows):
    features = patch.shape[1]
    depth, hidden = up.shape
    columns = down.shape[1]
    step = depth // 8
    width = columns // 8
    slots = DEEP + 1
    return pl.pallas_call(
        merger_kernel,
        out_shape=[jax.ShapeDtypeStruct((rows, columns // 2), BF16)] * 2 + [pltpu.VMEM(text.shape, BF16)],
        in_specs=[SMEM] + [HBM] * 9,
        out_specs=[VMEM, VMEM, VMEM],
        scratch_shapes=[
            pltpu.VMEM(patch.shape, BF16),
            pltpu.VMEM(gain.shape, F32),
            pltpu.VMEM(bias.shape, F32),
            pltpu.VMEM(up_bias.shape, F32),
            pltpu.VMEM(down_bias.shape, F32),
            pltpu.VMEM(rms_gain.shape, F32),
            pltpu.VMEM((1, columns), F32),
            pltpu.VMEM((features // 128, patch.shape[0], 128), F32),
            pltpu.VMEM((rows, depth), BF16),
            pltpu.VMEM((rows, hidden), F32),
            pltpu.VMEM((slots, step, hidden), BF16),
            pltpu.VMEM((slots, hidden, width), BF16),
            pltpu.VMEM((slots, text.shape[0] // 16, text.shape[1]), BF16),
            pltpu.SemaphoreType.DMA((6,)),
            pltpu.SemaphoreType.DMA((slots,)),
            pltpu.SemaphoreType.DMA((slots,)),
            pltpu.SemaphoreType.DMA((slots,)),
        ],
        compiler_params=params(34),
        cost_estimate=cost(2 * rows * hidden * (depth + columns), 2 * hidden * (depth + columns)),
        name="merger",
    )(where, *map(in_hbm, (patch, gain, bias, up, up_bias, down, down_bias, text, rms_gain)))


def owner_slots(owner_row, me, rows, capacity, slots):
    total = owner_row.shape[1]
    row = lax.broadcasted_iota(jnp.int32, (total, rows), 0)
    mine = (row == me * rows + lax.broadcasted_iota(jnp.int32, (total, rows), 1)).astype(F32).astype(BF16)
    named = (owner_row[...] ^ me).astype(F32).astype(BF16)
    across = dot(named, mine)
    down = lax.dot_general(mine, named, (((0,), (1,)), ((), ())), preferred_element_type=F32)
    earlier = lax.broadcasted_iota(jnp.int32, (rows, rows), 0) < lax.broadcasted_iota(jnp.int32, (rows, rows), 1)
    rank = jnp.sum(jnp.where((down == across) & earlier, 1.0, 0.0), axis=0, keepdims=True)
    slot = across * capacity + rank
    return (lax.broadcasted_iota(jnp.int32, (slots, rows), 0).astype(F32) == slot).astype(F32).astype(BF16)


def slot_places(owner_row, me, owners, slots):
    total = owner_row.shape[1]
    capacity = slots // owners
    named = (owner_row[...] == me).astype(F32).astype(BF16)
    source = lax.broadcasted_iota(jnp.int32, (total, slots), 0) // (total // owners)
    block = (lax.broadcasted_iota(jnp.int32, (total, slots), 1) // capacity) ^ me
    here = dot(named, (source == block).astype(F32).astype(BF16))
    offset = dot(named, (source < block).astype(F32).astype(BF16))
    index = (lax.broadcasted_iota(jnp.int32, (1, slots), 1) % capacity).astype(F32)
    target = jnp.where(index < here, offset + index, -1.0)
    position = lax.broadcasted_iota(jnp.int32, (slots, slots), 0).astype(F32)
    return (position == target).astype(F32).astype(BF16)


def join_matrix(mp, count, width):
    heads = KV_HEADS // count
    coords = HEAD_DIM // count
    full = 2 * heads * HEAD_DIM
    column = lax.broadcasted_iota(jnp.int32, (width, full), 1)
    row = lax.broadcasted_iota(jnp.int32, (width, full), 0)
    base = (row // coords) * HEAD_DIM + row % coords
    places = [(column == base + (mp ^ x) * coords).astype(F32).astype(BF16) for x in range(count)]
    return jnp.concatenate(places, axis=0)


def weights_kernel(owners, where, owner_row, keyval, query, out, query_out, select, place, join, buf, sem, query_sem):
    depth, _, columns = keyval.shape
    pieces = sem.shape[0]
    step = depth // pieces
    together = step // 128

    def copy(i):
        return pltpu.make_async_copy(keyval.at[tile(i, step)], buf.at[tile(i, step)], sem.at[i])

    for i in range(pieces):
        copy(i).start()
    part = depth // query_sem.shape[0]
    copies = [
        pltpu.make_async_copy(
            query.at[pl.ds(i * part, part), pl.ds(0, query_out.shape[1])],
            query_out.at[pl.ds(i * part, part)],
            query_sem.at[i],
        )
        for i in range(query_sem.shape[0])
    ]
    for query_copy in copies:
        query_copy.start()
    mp, me = where[0], where[1]
    slots, rows = select.shape
    select[...] = owner_slots(owner_row, me, rows, slots // owners, slots)
    place[...] = slot_places(owner_row, me, owners, slots)
    count = KV_HEADS * HEAD_DIM // columns
    join[...] = join_matrix(mp, count, join.shape[0] // count)
    pairs = buf.reshape(2 * depth, columns)
    row = lax.broadcasted_iota(jnp.int32, (256, 256), 0)
    column = lax.broadcasted_iota(jnp.int32, (256, 256), 1)
    apart = (column == 2 * (row % 128) + row // 128).astype(F32).astype(BF16)

    @pl.loop(0, pieces)
    def _(j):
        copy(j).wait()
        blocks = [pairs[tile(j * together + n, 256), :] for n in range(together)]
        ordered = dot(apart, jnp.concatenate(blocks, axis=1)).astype(BF16)
        for n in range(together):
            for side in range(2):
                out[tile(j * together + n, 128), pl.ds(side * columns, columns)] = ordered[
                    side * 128 : (side + 1) * 128, n * columns : (n + 1) * columns
                ]

    for query_copy in copies:
        query_copy.wait()


def weights_ahead(where, owner_row, keyval, query, width, owners, slots):
    depth, _, columns = keyval.shape
    rows = owner_row.shape[1] // owners
    return pl.pallas_call(
        functools.partial(weights_kernel, owners),
        out_shape=[
            pltpu.VMEM((depth, 2 * columns), BF16),
            pltpu.VMEM((depth, width), BF16),
            jax.ShapeDtypeStruct((slots, rows), BF16),
            jax.ShapeDtypeStruct((slots, slots), BF16),
            jax.ShapeDtypeStruct((2 * columns, 2 * columns), BF16),
        ],
        in_specs=[SMEM, VMEM, HBM, HBM],
        out_specs=[VMEM] * 5,
        scratch_shapes=[pltpu.VMEM(keyval.shape, BF16), pltpu.SemaphoreType.DMA((8,)), pltpu.SemaphoreType.DMA((4,))],
        compiler_params=params(16),
        cost_estimate=cost(4 * depth * columns * 256, 4 * depth * columns),
        name="weights_ahead",
    )(where, owner_row, in_hbm(keyval), in_hbm(query))


def keyval_kernel(where, text, own, sibling, gain, weight, bias, rows_all, *rest):
    parts, keyval = rest[:-1], rest[-1]
    texts, images = text.shape[0], own.shape[0]
    mp = where[0]
    half = own.shape[1]
    mine = mp % 2
    first, second = own[...].astype(F32), sibling[...].astype(F32)
    squares = jnp.sum(first * first, axis=-1, keepdims=True) + jnp.sum(second * second, axis=-1, keepdims=True)
    scale = lax.rsqrt(squares / (2 * half) + 1e-06)
    for values, which in ((first, mine), (second, 1 - mine)):
        here = pl.ds(pl.multiple_of(which * half, half), half)
        rows_all[pl.ds(texts, images), here] = (values * scale * gain[:, here]).astype(BF16)
    rows_all[pl.ds(0, texts), :] = text[...]
    columns = weight.shape[1] // 2
    sums = dot(rows_all[...], weight[...])
    for t in range(2):
        keyval[t] = (sums[:, t * columns : (t + 1) * columns] + bias[pl.ds(t, 1), :]).astype(BF16)

    count = len(parts)
    width = parts[0].shape[1]
    heads = KV_HEADS // count
    coords = columns // KV_HEADS
    row = lax.broadcasted_iota(jnp.int32, (columns, width // 2), 0)
    column = lax.broadcasted_iota(jnp.int32, (columns, width // 2), 1)
    for x in range(count):
        head = (mp ^ x) * heads + column // coords
        pick = (row == (column % coords) * KV_HEADS + head).astype(F32).astype(BF16)
        for t in range(2):
            parts[x][:, pl.ds(t * (width // 2), width // 2)] = dot(keyval[t], pick).astype(BF16)


def keyval_parts(where, text, own, sibling, gain, weight, bias, count):
    texts, depth = text.shape
    columns = weight.shape[1] // 2
    rows = texts + own.shape[0]
    width = 2 * columns // count
    outs = pl.pallas_call(
        keyval_kernel,
        out_shape=[pltpu.VMEM((rows, depth), BF16)]
        + [jax.ShapeDtypeStruct((rows, width), BF16)] * count,
        in_specs=[SMEM, VMEM, VMEM, VMEM, VMEM, VMEM, VMEM],
        out_specs=[VMEM] * (1 + count),
        scratch_shapes=[pltpu.VMEM((2, rows, columns), BF16)],
        compiler_params=params(8),
        cost_estimate=cost(4 * rows * depth * columns, 4 * depth * columns),
        name="keyval",
    )(where, in_vmem(text), own, sibling, gain, in_vmem(weight), bias)
    return outs[0], outs[1:]


def query_kernel(rows_all, ready, weight, bias, first_half, second_half, image_out, buf, sem):
    width = ready.shape[1]
    texts, half = first_half.shape
    later = buf.shape[0]

    def copy(i):
        return pltpu.make_async_copy(weight.at[:, tile(i + 1, width)], buf.at[i], sem.at[i])

    def columns(i, weights, text_out, offset):
        out = (dot(rows_all[...], weights) + bias[:, tile(i, width)]).astype(BF16)
        text_out[:, pl.ds(i * width - offset, width)] = out[:texts]
        image_out[:, tile(i, width)] = out[texts:]

    begin(copy, 2)
    columns(0, ready[...], first_half, 0)
    for i in range(1, later + 1):
        copy(i - 1).wait()
        if i + 1 < later:
            copy(i + 1).start()
        if i * width < half:
            columns(i, buf[i - 1], first_half, 0)
        else:
            columns(i, buf[i - 1], second_half, half)


def query_rows(rows_all, texts, ready, weight, bias):
    depth = rows_all.shape[1]
    images = rows_all.shape[0] - texts
    columns = weight.shape[1]
    width = ready.shape[1]
    later = columns // width - 1
    return pl.pallas_call(
        query_kernel,
        out_shape=[jax.ShapeDtypeStruct((texts, columns // 2), BF16)] * 2 + [jax.ShapeDtypeStruct((images, columns), BF16)],
        in_specs=[VMEM, VMEM, HBM, VMEM],
        out_specs=[VMEM] * 3,
        scratch_shapes=[pltpu.VMEM((later, depth, width), BF16), pltpu.SemaphoreType.DMA((later,))],
        compiler_params=params(30),
        cost_estimate=cost(2 * (texts + images) * depth * columns, 2 * depth * columns),
        name="query",
    )(in_vmem(rows_all), in_vmem(ready), in_hbm(weight), bias)


def slots_kernel(owners, select, queries, *rest):
    parts, outs = rest[:-owners], rest[-owners:]
    rows = queries.shape[0]
    capacity = outs[0].shape[0]
    images = [queries[...]] + [part[pl.ds(part.shape[0] - rows, rows), :] for part in parts]
    chosen = dot(select[...], jnp.concatenate(images, axis=1))
    for x, out in enumerate(outs):
        out[...] = chosen[x * capacity : (x + 1) * capacity].astype(BF16)


def slots_of(select, queries, parts, owners):
    width = queries.shape[1] + len(parts) * parts[0].shape[1]
    capacity = select.shape[0] // owners
    return pl.pallas_call(
        functools.partial(slots_kernel, owners),
        out_shape=[jax.ShapeDtypeStruct((capacity, width), BF16)] * owners,
        in_specs=[VMEM] * (2 + len(parts)),
        out_specs=[VMEM] * owners,
        compiler_params=params(8),
        name="slots",
    )(select, queries, *parts)


def attend(blocks, first, doc_row, queries, kv_all, out):
    q_first, k_first, out_first = first
    groups = kv_all.shape[1] // (2 * HEAD_DIM)
    per_half = groups // len(queries)
    shared = queries[0].shape[1] // HEAD_DIM // per_half
    block = DOC_MAX
    scale = 1.0 / math.sqrt(HEAD_DIM)
    docs = doc_row[...].astype(F32)
    ones = jnp.ones((2 * block, HEAD_DIM), BF16)
    row = lax.broadcasted_iota(jnp.int32, (block, 2 * block), 0)
    column = lax.broadcasted_iota(jnp.int32, (block, 2 * block), 1)
    for b in range(*blocks):
        q0 = b * block
        k0 = max(0, b - 1) * block
        k_doc = docs[:, k0 : k0 + 2 * block]
        q_doc = jnp.sum(jnp.where(k0 + column == q0 + row, k_doc, 0.0), axis=1, keepdims=True)
        allowed = (q_doc == k_doc) & (k0 + column <= q0 + row)
        penalty = jnp.concatenate([jnp.where(allowed, 0.0, -1e30)] * shared, axis=0)
        for g in range(groups):
            keys = kv_all[pl.ds(k0 - k_first, 2 * block), tile(g, HEAD_DIM)]
            values = kv_all[pl.ds(k0 - k_first, 2 * block), tile(groups + g, HEAD_DIM)]
            source = queries[g // per_half]
            columns = [tile((g % per_half) * shared + h, HEAD_DIM) for h in range(shared)]
            q = jnp.concatenate([source[pl.ds(q0 - q_first, block), c] for c in columns], axis=0)
            scores = lax.dot_general(q, keys, (((1,), (1,)), ((), ())), preferred_element_type=F32) * scale
            scores = jnp.where(penalty < 0.0, penalty, scores)
            weights = jnp.exp(scores - jnp.max(scores, axis=-1, keepdims=True))
            result = dot(weights.astype(BF16), jnp.concatenate([values, ones], axis=1))
            result = (result[:, :HEAD_DIM] / result[:, HEAD_DIM:]).astype(BF16)
            for h in range(shared):
                out[pl.ds(q0 - out_first, block), tile(g * shared + h, HEAD_DIM)] = result[h * block : (h + 1) * block]
        yield b


def late_kernel(early, join, doc_row, first_half, second_half, *rest):
    parts, out, kv_all = rest[:-2], rest[-2], rest[-1]
    seq = first_half.shape[0]
    sent = jnp.concatenate([part[pl.ds(0, seq), :] for part in parts], axis=1)
    kv_all[...] = dot(sent, join[...]).astype(BF16)
    blocks = (early // DOC_MAX, seq // DOC_MAX)
    for _ in attend(blocks, (0, 0, early), doc_row, (first_half, second_half), kv_all, out):
        pass


def early_kernel(early, order, doc_row, first_half, second_half, keyval, join, place, *rest):
    arrived = rest[:-7]
    late, out, first, second, kv_all, result, sem = rest[-7:]
    slots = place.shape[0]
    copies = [pltpu.make_async_copy(late, out.at[pl.ds(early, late.shape[0])], sem.at[0])]
    copies[0].start()
    half = first_half.shape[1]
    in_place = [arrived[order.index(x)][...].astype(F32) for x in range(len(order))]
    together = jnp.concatenate(in_place, axis=0).astype(BF16)
    placed = dot(place[...], together).astype(BF16)
    is_image = jnp.sum(place[...].astype(F32), axis=1, keepdims=True) > 0.5
    image_keyval = dot(placed[:, 2 * half :], join[...]).astype(BF16)
    kv_all[...] = keyval[pl.ds(0, early), :]
    kv_all[pl.ds(0, slots), :] = jnp.where(is_image, image_keyval, keyval[pl.ds(0, slots), :])
    for i, (source, target) in enumerate(((first_half, first), (second_half, second))):
        target[...] = source[pl.ds(0, early), :]
        target[pl.ds(0, slots), :] = jnp.where(
            is_image, placed[:, i * half : (i + 1) * half], source[pl.ds(0, slots), :]
        )
    for b in attend((0, early // DOC_MAX), (0, 0, 0), doc_row, (first, second), kv_all, result):
        here = pl.ds(b * DOC_MAX, DOC_MAX)
        copies.append(pltpu.make_async_copy(result.at[here], out.at[here], sem.at[b + 1]))
        copies[-1].start()
    for copy in copies:
        copy.wait()


def attention(join, place, documents, halves, parts, arrived, order, columns):
    seq = documents.shape[1]
    full = join.shape[1]
    slots = place.shape[0]
    owners = len(order)
    early = min(seq, -(-slots // DOC_MAX) * DOC_MAX + DOC_MAX)
    out, keyval = pl.pallas_call(
        functools.partial(late_kernel, early),
        out_shape=[pltpu.VMEM((seq - early, columns), BF16), jax.ShapeDtypeStruct((seq, full), BF16)],
        in_specs=[VMEM] * (4 + len(parts)),
        out_specs=[VMEM] * 2,
        compiler_params=params(12),
        cost_estimate=cost(4 * (seq - early) * columns * 2 * DOC_MAX, 4 * seq * columns),
        name="attention_late",
    )(join, documents, *halves, *parts)
    return pl.pallas_call(
        functools.partial(early_kernel, early, order),
        out_shape=jax.ShapeDtypeStruct((seq, columns), BF16),
        in_specs=[VMEM] * (7 + owners),
        out_specs=HBM,
        scratch_shapes=[pltpu.VMEM((early, columns // 2), BF16)] * 2
        + [pltpu.VMEM((early, full), BF16), pltpu.VMEM((early, columns), BF16), pltpu.SemaphoreType.DMA((1 + early // DOC_MAX,))],
        compiler_params=params(12),
        cost_estimate=cost(4 * early * columns * 2 * DOC_MAX, 4 * seq * columns),
        name="attention_early",
    )(documents, *halves, keyval, join, place, *arrived(out), in_vmem(out))


def after(x, *others):
    return lax.optimization_barrier((x, *others))[0]


def exchange(x, count, bit):
    return lax.ppermute(x, "mp", [(i, i ^ bit) for i in range(count)])


def per_device(
    patch_rows,
    ln_gain,
    ln_bias,
    merge_up,
    merge_up_bias,
    merge_down,
    merge_down_bias,
    row_owner,
    text_embed,
    doc_ids,
    rms_gain,
    w_query,
    query_bias,
    w_keyval,
    keyval_bias,
):
    owners = lax.axis_size(("group", "dp"))
    count = lax.axis_size("mp")
    mp_index = lax.axis_index("mp")
    where = jnp.stack([mp_index, lax.axis_index(("group", "dp"))]).astype(jnp.int32)
    rows = row_owner.shape[0] // owners
    capacity = max(2, 2 * rows // owners)
    owner_row = row_owner.reshape(1, -1)
    groups, line = lax.axis_size("group"), lax.axis_size("dp")

    def far(x):
        return max(abs(i % line - (i ^ x) % line) + (x >= line) for i in range(groups * line))


    send, keep, text = merger(
        where, patch_rows[0], ln_gain, ln_bias, merge_up, merge_up_bias, merge_down, merge_down_bias,
        text_embed[0], rms_gain[None, :], rows,
    )
    own = (keep.astype(F32) + exchange(send, count, 1).astype(F32)).astype(BF16)
    slots = owners * capacity
    weight, ready, select, place, join = weights_ahead(
        where, owner_row, after(w_keyval, own), w_query, w_query.shape[1] // 4, owners, slots
    )
    bit = 2
    while bit < count:
        other = after(exchange(own, count, bit), weight)
        own = (own.astype(F32) + other.astype(F32)).astype(BF16)
        bit *= 2
    sibling = exchange(own, count, 1)

    columns = w_query.shape[1]
    rows_all, parts = keyval_parts(where, text, own, sibling, rms_gain[None, :], weight, keyval_bias, count)
    parts = [parts[0]] + [exchange(parts[x], count, x) for x in range(1, count)]
    *halves, image_queries = query_rows(rows_all, text.shape[0], ready, w_query, query_bias[None, :])
    outgoing = slots_of(select, image_queries, parts, owners)

    order = sorted(range(1, owners), key=far, reverse=True)

    def arrived(done):
        rows = [lax.ppermute(outgoing[x], ("group", "dp"), [(i, i ^ x) for i in range(owners)]) for x in order]
        return lax.optimization_barrier((*rows, outgoing[0], done))[:-1]

    halves = [after(half, outgoing[0]) for half in halves]
    return attention(join, place, doc_ids, halves, parts, arrived, [*order, 0], columns)[None]


def general(
    patch_rows,
    ln_gain,
    ln_bias,
    merge_up,
    merge_up_bias,
    merge_down,
    merge_down_bias,
    row_owner,
    text_embed,
    doc_ids,
    rms_gain,
    w_query,
    query_bias,
    w_keyval,
    keyval_bias,
):
    owners = lax.axis_size(("group", "dp"))
    own_index = lax.axis_index(("group", "dp"))
    mp_index = lax.axis_index("mp")
    pixels = patch_rows[0].astype(jnp.float32)
    center = pixels - jnp.mean(pixels, axis=-1, keepdims=True)
    spread = jnp.mean(center * center, axis=-1, keepdims=True)
    normed_patch = (center * lax.rsqrt(spread + 1e-06) * ln_gain + ln_bias).astype(jnp.bfloat16)
    merged = normed_patch.reshape(-1, 4 * pixels.shape[1])
    merged_rows = merged.shape[0]
    hidden = jax.nn.gelu(
        jnp.dot(merged, merge_up, preferred_element_type=jnp.float32) + merge_up_bias,
        approximate=False,
    ).astype(jnp.bfloat16)
    partial_sum = jnp.dot(hidden, merge_down, preferred_element_type=jnp.float32)
    vision = (
        lax.psum_scatter(partial_sum, "mp", scatter_dimension=1, tiled=True) + merge_down_bias
    ).astype(jnp.bfloat16)
    col_width = vision.shape[1]
    capacity = max(2, 2 * merged_rows // owners)
    owner_all = row_owner[:, 0]
    owner_ids = jnp.arange(owners, dtype=jnp.int32)
    onehot = (owner_all[:, None] == owner_ids[None, :]).astype(jnp.int32)
    per_source = jnp.sum(onehot.reshape(owners, merged_rows, owners), axis=1)
    my_block = lax.dynamic_slice_in_dim(onehot, own_index * merged_rows, merged_rows, 0)
    block_rank = jnp.sum((jnp.cumsum(my_block, axis=0) - my_block) * my_block, axis=1)
    my_owner = jnp.sum(my_block * owner_ids[None, :], axis=1)
    slot_id = my_owner * capacity + block_rank
    all_slots = jnp.arange(owners * capacity, dtype=jnp.int32)
    select = (slot_id[:, None] == all_slots[None, :]).astype(jnp.bfloat16)
    outgoing = jnp.einsum("ms,mc->sc", select, vision, preferred_element_type=jnp.float32).astype(
        jnp.bfloat16
    )
    arrived = lax.all_to_all(
        outgoing.reshape(owners, capacity, col_width),
        ("group", "dp"),
        split_axis=0,
        concat_axis=0,
        tiled=True,
    )
    arrived = arrived.reshape(owners * capacity, col_width)
    incoming = lax.dynamic_slice_in_dim(per_source, own_index, 1, 1)[:, 0]
    offsets = jnp.cumsum(incoming) - incoming
    total = jnp.sum(incoming)
    slot_rank = jnp.arange(capacity, dtype=jnp.int32)
    target = jnp.where(
        slot_rank[None, :] < incoming[:, None], offsets[:, None] + slot_rank[None, :], -1
    ).reshape(-1)
    text_rows = text_embed[0]
    seq_len = text_rows.shape[0]
    positions = jnp.arange(seq_len, dtype=jnp.int32)
    source_slot = jnp.sum(
        jnp.where(target[:, None] == positions[None, :], all_slots[:, None], 0), axis=0
    )
    is_image = (positions < total)[:, None]
    image_full = lax.all_gather(arrived, "mp", axis=1, tiled=True)
    sequence = jnp.where(is_image, jnp.take(image_full, source_slot, axis=0), text_rows)
    seq_f = sequence.astype(jnp.float32)
    normed_seq = (
        seq_f * lax.rsqrt(jnp.mean(seq_f * seq_f, axis=-1, keepdims=True) + 1e-06) * rms_gain
    ).astype(jnp.bfloat16)
    queries = (
        jnp.dot(normed_seq, w_query, preferred_element_type=jnp.float32) + query_bias
    ).astype(jnp.bfloat16)
    keyval_local = (
        jnp.einsum("sd,dtc->stc", normed_seq, w_keyval, preferred_element_type=jnp.float32)
        + keyval_bias
    ).astype(jnp.bfloat16)
    keyval_full = lax.all_gather(keyval_local, "mp", axis=2, tiled=True)
    keyval_heads = jnp.transpose(keyval_full.reshape(seq_len, 2, HEAD_DIM, KV_HEADS), (0, 1, 3, 2))
    local_heads = queries.shape[1] // HEAD_DIM
    group_size = HEADS // KV_HEADS
    kv_index = (mp_index * local_heads + jnp.arange(local_heads, dtype=jnp.int32)) // group_size
    keys = jnp.take(keyval_heads[:, 0], kv_index, axis=1)
    values = jnp.take(keyval_heads[:, 1], kv_index, axis=1)
    query_heads = queries.reshape(seq_len, local_heads, HEAD_DIM)
    scores = jnp.einsum(
        "qhd,khd->hqk", query_heads, keys, preferred_element_type=jnp.float32
    ) / math.sqrt(HEAD_DIM)
    documents = doc_ids[0]
    allowed = (documents[:, None] == documents[None, :]) & (
        positions[None, :] <= positions[:, None]
    )
    scores = jnp.where(allowed[None], scores, jnp.float32(-1e30))
    highest = jnp.max(scores, axis=-1, keepdims=True)
    weights = jnp.exp(scores - highest)
    probs = (weights / jnp.sum(weights, axis=-1, keepdims=True)).astype(jnp.bfloat16)
    output = jnp.einsum("hqk,khd->qhd", probs, values, preferred_element_type=jnp.float32)
    return output.astype(jnp.bfloat16).reshape(1, seq_len, local_heads * HEAD_DIM)


def solution(mesh):
    in_specs = (
        P(("group", "dp"), None, None),
        P(),
        P(),
        P(None, "mp"),
        P("mp"),
        P("mp", None),
        P("mp"),
        P(),
        P(("group", "dp"), None, None),
        P(("group", "dp"), None),
        P(),
        P(None, "mp"),
        P("mp"),
        P(None, None, "mp"),
        P(None, "mp"),
    )
    out_specs = P(("group", "dp"), None, "mp")
    count = mesh.shape["mp"]
    owners = mesh.shape["group"] * mesh.shape["dp"]
    narrow = count < 2 or count > KV_HEADS or count & (count - 1) or owners & (owners - 1)
    body = general if narrow else per_device
    return jax.shard_map(body, mesh=mesh, in_specs=in_specs, out_specs=out_specs, check_vma=False)
```

```python
import functools
import math

import jax
import jax.numpy as jnp
from jax import lax
from jax.experimental import pallas as pl
from jax.experimental.pallas import tpu as pltpu
from jax.sharding import PartitionSpec as P

HEADS = 64
KV_HEADS = 8
HEAD_DIM = 128
DOC_MAX = 64

BF16 = jnp.bfloat16
F32 = jnp.float32
VMEM = pl.BlockSpec(memory_space=pltpu.VMEM)
SMEM = pl.BlockSpec(memory_space=pltpu.SMEM)
ANY = pl.BlockSpec(memory_space=pl.ANY)
HBM = pl.BlockSpec(memory_space=pltpu.HBM)
AHEAD = 3
DEEP = 5
MIB = 1 << 20


def dot(a, b):
    return jnp.dot(a, b, preferred_element_type=F32)


def in_hbm(x):
    return pltpu.with_memory_space_constraint(x, pltpu.HBM)


def in_vmem(x):
    return pltpu.with_memory_space_constraint(x, pltpu.VMEM)


def params(mib):
    return pltpu.CompilerParams(vmem_limit_bytes=mib * MIB)


def cost(flops, nbytes):
    return pl.CostEstimate(flops=flops, bytes_accessed=nbytes, transcendentals=0)


def rms_scale(x, width):
    return lax.rsqrt(jnp.sum(x * x, axis=-1, keepdims=True) / width + 1e-06)


def stream(count, copy, body, ahead=AHEAD, then=None):
    @pl.loop(0, count)
    def _(i):
        copy(i).wait()

        @pl.when(i + ahead < count)
        def _():
            copy(i + ahead).start()

        if then is not None:

            @pl.when(i + ahead >= count)
            def _():
                then(i + ahead - count).start()

        body(i)


def begin(copy, ahead=AHEAD):
    for i in range(ahead):
        copy(i).start()


def tile(i, width):
    return pl.ds(pl.multiple_of(i * width, width), width)


def merger_kernel(
    where, patch_in, gain_in, bias_in, up, up_bias_in, down, down_bias_in, text, rms_gain_in, send, keep, text_out,
    patch, gain, bias, up_bias, down_bias, rms_gain, bias_row, normed, merged, total, up_buf, down_buf, text_buf,
    small_sem, up_sem, down_sem, text_sem,
):
    slots = DEEP + 1
    step = up_buf.shape[1]
    width = down_buf.shape[2]
    half = send.shape[1]
    per_half = half // width
    mp = where[0]
    mine = mp % 2
    pairs = [(patch_in, patch), (gain_in, gain), (bias_in, bias), (up_bias_in, up_bias), (down_bias_in, down_bias)]
    pairs.append((rms_gain_in, rms_gain))
    small = [pltpu.make_async_copy(x, y, small_sem.at[i]) for i, (x, y) in enumerate(pairs)]
    for copy in small:
        copy.start()

    def up_copy(i):
        return pltpu.make_async_copy(up.at[tile(i, step)], up_buf.at[i % slots], up_sem.at[i % slots])

    def column(i):
        first = jnp.where(i < per_half, 1 - mine, mine)
        return pl.multiple_of(first * half + (i % per_half) * width, width)

    def down_copy(i):
        return pltpu.make_async_copy(
            down.at[:, pl.ds(column(i), width)], down_buf.at[i % slots], down_sem.at[i % slots]
        )

    block = text_buf.shape[1]
    blocks = text.shape[0] // block

    def text_copy(i):
        return pltpu.make_async_copy(text.at[tile(i, block)], text_buf.at[i % slots], text_sem.at[i % slots])

    def text_norm(i):
        text_copy(i).wait()

        @pl.when(i + DEEP < blocks)
        def _():
            text_copy(i + DEEP).start()

        x = text_buf[i % slots].astype(F32)
        text_out[tile(i, block), :] = (x * rms_scale(x, x.shape[1]) * rms_gain[...]).astype(BF16)

    begin(up_copy, DEEP)
    begin(text_copy, DEEP)
    for copy in small:
        copy.wait()
    rows = send.shape[0]
    joined = patch.shape[0] // rows
    features = patch.shape[1]
    pixels = patch[...].astype(F32)
    center = pixels - jnp.mean(pixels, axis=-1, keepdims=True)
    spread = jnp.mean(center * center, axis=-1, keepdims=True)
    patches = center * lax.rsqrt(spread + 1e-06) * gain[...][None, :] + bias[...][None, :]
    for c in range(features // 128):
        normed[c] = patches[:, c * 128 : (c + 1) * 128]
        for j in range(joined):
            merged[:, pl.ds(j * features + c * 128, 128)] = normed[c, pl.ds(j, rows, stride=joined), :].astype(BF16)
    own = down_bias.shape[0]
    bias_row[...] = jnp.zeros_like(bias_row)
    bias_row[:, pl.ds(pl.multiple_of(mp * own, 128), own)] = down_bias[...][None, :]
    total[...] = jnp.broadcast_to(up_bias[...][None, :], total.shape)

    def up_body(i):
        text_norm(i)
        total[...] += dot(merged[:, tile(i, step)], up_buf[i % slots])

    up_steps = up.shape[0] // step
    stream(up_steps, up_copy, up_body, DEEP, down_copy)
    sums = total[...]
    hidden = (0.5 * sums * (1.0 + lax.erf(sums * math.sqrt(0.5)))).astype(BF16)

    def down_body(i):
        text_norm(up_steps + i)
        part = (dot(hidden, down_buf[i % slots]) + bias_row[:, pl.ds(column(i), width)]).astype(BF16)
        here = tile(i % per_half, width)

        @pl.when(i < per_half)
        def _():
            send[:, here] = part

        @pl.when(i >= per_half)
        def _():
            keep[:, here] = part

    stream(2 * per_half, down_copy, down_body, DEEP)


def merger(where, patch, gain, bias, up, up_bias, down, down_bias, text, rms_gain, rows):
    features = patch.shape[1]
    depth, hidden = up.shape
    columns = down.shape[1]
    step = depth // 8
    width = columns // 8
    slots = DEEP + 1
    return pl.pallas_call(
        merger_kernel,
        out_shape=[jax.ShapeDtypeStruct((rows, columns // 2), BF16)] * 2 + [pltpu.VMEM(text.shape, BF16)],
        in_specs=[SMEM] + [HBM] * 9,
        out_specs=[VMEM, VMEM, VMEM],
        scratch_shapes=[
            pltpu.VMEM(patch.shape, BF16),
            pltpu.VMEM(gain.shape, F32),
            pltpu.VMEM(bias.shape, F32),
            pltpu.VMEM(up_bias.shape, F32),
            pltpu.VMEM(down_bias.shape, F32),
            pltpu.VMEM(rms_gain.shape, F32),
            pltpu.VMEM((1, columns), F32),
            pltpu.VMEM((features // 128, patch.shape[0], 128), F32),
            pltpu.VMEM((rows, depth), BF16),
            pltpu.VMEM((rows, hidden), F32),
            pltpu.VMEM((slots, step, hidden), BF16),
            pltpu.VMEM((slots, hidden, width), BF16),
            pltpu.VMEM((slots, text.shape[0] // 16, text.shape[1]), BF16),
            pltpu.SemaphoreType.DMA((6,)),
            pltpu.SemaphoreType.DMA((slots,)),
            pltpu.SemaphoreType.DMA((slots,)),
            pltpu.SemaphoreType.DMA((slots,)),
        ],
        compiler_params=params(34),
        cost_estimate=cost(2 * rows * hidden * (depth + columns), 2 * hidden * (depth + columns)),
        name="merger",
    )(where, *map(in_hbm, (patch, gain, bias, up, up_bias, down, down_bias, text, rms_gain)))


def owner_slots(owner_row, me, rows, capacity, slots):
    total = owner_row.shape[1]
    row = lax.broadcasted_iota(jnp.int32, (total, rows), 0)
    mine = (row == me * rows + lax.broadcasted_iota(jnp.int32, (total, rows), 1)).astype(F32).astype(BF16)
    named = (owner_row[...] ^ me).astype(F32).astype(BF16)
    across = dot(named, mine)
    down = lax.dot_general(mine, named, (((0,), (1,)), ((), ())), preferred_element_type=F32)
    earlier = lax.broadcasted_iota(jnp.int32, (rows, rows), 0) < lax.broadcasted_iota(jnp.int32, (rows, rows), 1)
    rank = jnp.sum(jnp.where((down == across) & earlier, 1.0, 0.0), axis=0, keepdims=True)
    slot = across * capacity + rank
    return (lax.broadcasted_iota(jnp.int32, (slots, rows), 0).astype(F32) == slot).astype(F32).astype(BF16)


def slot_places(owner_row, me, owners, slots):
    total = owner_row.shape[1]
    capacity = slots // owners
    named = (owner_row[...] == me).astype(F32).astype(BF16)
    source = lax.broadcasted_iota(jnp.int32, (total, slots), 0) // (total // owners)
    block = (lax.broadcasted_iota(jnp.int32, (total, slots), 1) // capacity) ^ me
    here = dot(named, (source == block).astype(F32).astype(BF16))
    offset = dot(named, (source < block).astype(F32).astype(BF16))
    index = (lax.broadcasted_iota(jnp.int32, (1, slots), 1) % capacity).astype(F32)
    target = jnp.where(index < here, offset + index, -1.0)
    position = lax.broadcasted_iota(jnp.int32, (slots, slots), 0).astype(F32)
    return (position == target).astype(F32).astype(BF16)


def join_matrix(mp, count, width):
    heads = KV_HEADS // count
    coords = HEAD_DIM // count
    full = 2 * heads * HEAD_DIM
    column = lax.broadcasted_iota(jnp.int32, (width, full), 1)
    row = lax.broadcasted_iota(jnp.int32, (width, full), 0)
    base = (row // coords) * HEAD_DIM + row % coords
    places = [(column == base + (mp ^ x) * coords).astype(F32).astype(BF16) for x in range(count)]
    return jnp.concatenate(places, axis=0)


def weights_kernel(owners, where, owner_row, keyval, query, out, query_out, select, place, join, buf, sem, query_sem):
    depth, _, columns = keyval.shape
    pieces = sem.shape[0]
    step = depth // pieces
    together = step // 128

    def copy(i):
        return pltpu.make_async_copy(keyval.at[tile(i, step)], buf.at[tile(i, step)], sem.at[i])

    for i in range(pieces):
        copy(i).start()
    part = depth // query_sem.shape[0]
    copies = [
        pltpu.make_async_copy(
            query.at[pl.ds(i * part, part), pl.ds(0, query_out.shape[1])],
            query_out.at[pl.ds(i * part, part)],
            query_sem.at[i],
        )
        for i in range(query_sem.shape[0])
    ]
    for query_copy in copies:
        query_copy.start()
    mp, me = where[0], where[1]
    slots, rows = select.shape
    select[...] = owner_slots(owner_row, me, rows, slots // owners, slots)
    place[...] = slot_places(owner_row, me, owners, slots)
    count = KV_HEADS * HEAD_DIM // columns
    join[...] = join_matrix(mp, count, join.shape[0] // count)
    pairs = buf.reshape(2 * depth, columns)
    row = lax.broadcasted_iota(jnp.int32, (256, 256), 0)
    column = lax.broadcasted_iota(jnp.int32, (256, 256), 1)
    apart = (column == 2 * (row % 128) + row // 128).astype(F32).astype(BF16)

    @pl.loop(0, pieces)
    def _(j):
        copy(j).wait()
        blocks = [pairs[tile(j * together + n, 256), :] for n in range(together)]
        ordered = dot(apart, jnp.concatenate(blocks, axis=1)).astype(BF16)
        for n in range(together):
            for side in range(2):
                out[tile(j * together + n, 128), pl.ds(side * columns, columns)] = ordered[
                    side * 128 : (side + 1) * 128, n * columns : (n + 1) * columns
                ]

    for query_copy in copies:
        query_copy.wait()


def weights_ahead(where, owner_row, keyval, query, width, owners, slots):
    depth, _, columns = keyval.shape
    rows = owner_row.shape[1] // owners
    return pl.pallas_call(
        functools.partial(weights_kernel, owners),
        out_shape=[
            pltpu.VMEM((depth, 2 * columns), BF16),
            pltpu.VMEM((depth, width), BF16),
            jax.ShapeDtypeStruct((slots, rows), BF16),
            jax.ShapeDtypeStruct((slots, slots), BF16),
            jax.ShapeDtypeStruct((2 * columns, 2 * columns), BF16),
        ],
        in_specs=[SMEM, VMEM, HBM, HBM],
        out_specs=[VMEM] * 5,
        scratch_shapes=[pltpu.VMEM(keyval.shape, BF16), pltpu.SemaphoreType.DMA((8,)), pltpu.SemaphoreType.DMA((4,))],
        compiler_params=params(16),
        cost_estimate=cost(4 * depth * columns * 256, 4 * depth * columns),
        name="weights_ahead",
    )(where, owner_row, in_hbm(keyval), in_hbm(query))


def keyval_own_kernel(where, text, own, gain, weight, rows_all, sums):
    texts, half = text.shape[0], own.shape[1]
    here = pl.ds(pl.multiple_of((where[0] % 2) * half, half), half)
    rows_all[pl.ds(0, texts), :] = text[...]
    rows_all[pl.ds(texts, own.shape[0]), here] = (own[...].astype(F32) * gain[:, here]).astype(BF16)
    sums[...] = dot(rows_all[:, here], weight[here, :])


def keyval_kernel(where, _, sums_in, own, sibling, gain, weight, bias, rows_all, scale_out, *rest):
    parts, keyval = rest[:-1], rest[-1]
    images, half = own.shape
    texts = rows_all.shape[0] - images
    mp = where[0]
    here = pl.ds(pl.multiple_of((1 - mp % 2) * half, half), half)
    first, second = own[...].astype(F32), sibling[...].astype(F32)
    rows_all[pl.ds(texts, images), here] = (second * gain[:, here]).astype(BF16)
    squares = jnp.sum(first * first, axis=-1, keepdims=True) + jnp.sum(second * second, axis=-1, keepdims=True)
    scale = lax.rsqrt(squares / (2 * half) + 1e-06)
    scale_out[...] = jnp.broadcast_to(scale, scale_out.shape)
    columns = weight.shape[1] // 2
    sums = sums_in[...] + dot(rows_all[:, here], weight[here, :])
    for t in range(2):
        side = slice(t * columns, (t + 1) * columns)
        add = bias[pl.ds(t, 1), :]
        keyval[t, pl.ds(0, texts), :] = (sums[:texts, side] + add).astype(BF16)
        keyval[t, pl.ds(texts, images), :] = (sums[texts:, side] * scale + add).astype(BF16)

    count = len(parts)
    width = parts[0].shape[1]
    heads = KV_HEADS // count
    coords = columns // KV_HEADS
    row = lax.broadcasted_iota(jnp.int32, (columns, width // 2), 0)
    column = lax.broadcasted_iota(jnp.int32, (columns, width // 2), 1)
    for x in range(count):
        head = (mp ^ x) * heads + column // coords
        pick = (row == (column % coords) * KV_HEADS + head).astype(F32).astype(BF16)
        for t in range(2):
            parts[x][:, pl.ds(t * (width // 2), width // 2)] = dot(keyval[t], pick).astype(BF16)


def keyval_parts(where, text, own, sibling, gain, weight, bias, count):
    texts, depth = text.shape
    columns = weight.shape[1] // 2
    images = own.shape[0]
    rows = texts + images
    width = 2 * columns // count
    weight = in_vmem(weight)
    rows_all, sums = pl.pallas_call(
        keyval_own_kernel,
        out_shape=[pltpu.VMEM((rows, depth), BF16), pltpu.VMEM((rows, 2 * columns), F32)],
        in_specs=[SMEM, VMEM, VMEM, VMEM, VMEM],
        out_specs=[VMEM] * 2,
        compiler_params=params(8),
        cost_estimate=cost(2 * rows * depth * columns, 2 * depth * columns),
        name="keyval_own",
    )(where, in_vmem(text), own, gain, weight)
    outs = pl.pallas_call(
        keyval_kernel,
        out_shape=[pltpu.VMEM((rows, depth), BF16), jax.ShapeDtypeStruct((images, 128), F32)]
        + [jax.ShapeDtypeStruct((rows, width), BF16)] * count,
        in_specs=[SMEM] + [VMEM] * 7,
        out_specs=[VMEM] * (2 + count),
        scratch_shapes=[pltpu.VMEM((2, rows, columns), BF16)],
        input_output_aliases={1: 0},
        compiler_params=params(8),
        cost_estimate=cost(2 * rows * depth * columns, 2 * depth * columns),
        name="keyval",
    )(where, in_vmem(rows_all), in_vmem(sums), own, after(sibling, sums), gain, weight, bias)
    return outs[0], outs[1], outs[2:]


def query_kernel(rows_all, scale, ready, weight, bias, first_half, second_half, image_out, buf, sem):
    width = ready.shape[1]
    texts, half = first_half.shape
    later = buf.shape[0]

    def copy(i):
        return pltpu.make_async_copy(weight.at[:, tile(i + 1, width)], buf.at[i], sem.at[i])

    def columns(i, weights, text_out, offset):
        out = dot(rows_all[...], weights)
        add = bias[:, tile(i, width)]
        text_out[:, pl.ds(i * width - offset, width)] = (out[:texts] + add).astype(BF16)
        image_out[:, tile(i, width)] = (out[texts:] * scale[:, :1] + add).astype(BF16)

    begin(copy, 2)
    columns(0, ready[...], first_half, 0)
    for i in range(1, later + 1):
        copy(i - 1).wait()
        if i + 1 < later:
            copy(i + 1).start()
        if i * width < half:
            columns(i, buf[i - 1], first_half, 0)
        else:
            columns(i, buf[i - 1], second_half, half)


def query_rows(rows_all, scale, texts, ready, weight, bias):
    depth = rows_all.shape[1]
    images = rows_all.shape[0] - texts
    columns = weight.shape[1]
    width = ready.shape[1]
    later = columns // width - 1
    return pl.pallas_call(
        query_kernel,
        out_shape=[jax.ShapeDtypeStruct((texts, columns // 2), BF16)] * 2 + [jax.ShapeDtypeStruct((images, columns), BF16)],
        in_specs=[VMEM, VMEM, VMEM, HBM, VMEM],
        out_specs=[VMEM] * 3,
        scratch_shapes=[pltpu.VMEM((later, depth, width), BF16), pltpu.SemaphoreType.DMA((later,))],
        compiler_params=params(30),
        cost_estimate=cost(2 * (texts + images) * depth * columns, 2 * depth * columns),
        name="query",
    )(in_vmem(rows_all), scale, in_vmem(ready), in_hbm(weight), bias)


def slots_kernel(owners, select, queries, *rest):
    parts, outs = rest[:-owners], rest[-owners:]
    rows = queries.shape[0]
    capacity = outs[0].shape[0]
    images = [queries[...]] + [part[pl.ds(part.shape[0] - rows, rows), :] for part in parts]
    chosen = dot(select[...], jnp.concatenate(images, axis=1))
    for x, out in enumerate(outs):
        out[...] = chosen[x * capacity : (x + 1) * capacity].astype(BF16)


def slots_of(select, queries, parts, owners):
    width = queries.shape[1] + len(parts) * parts[0].shape[1]
    capacity = select.shape[0] // owners
    return pl.pallas_call(
        functools.partial(slots_kernel, owners),
        out_shape=[jax.ShapeDtypeStruct((capacity, width), BF16)] * owners,
        in_specs=[VMEM] * (2 + len(parts)),
        out_specs=[VMEM] * owners,
        compiler_params=params(8),
        name="slots",
    )(select, queries, *parts)


def attend(blocks, first, doc_row, queries, kv_all, out):
    q_first, k_first, out_first = first
    groups = kv_all.shape[1] // (2 * HEAD_DIM)
    per_half = groups // len(queries)
    shared = queries[0].shape[1] // HEAD_DIM // per_half
    block = DOC_MAX
    scale = 1.0 / math.sqrt(HEAD_DIM)
    docs = doc_row[...].astype(F32)
    ones = jnp.ones((2 * block, HEAD_DIM), BF16)
    row = lax.broadcasted_iota(jnp.int32, (block, 2 * block), 0)
    column = lax.broadcasted_iota(jnp.int32, (block, 2 * block), 1)
    for b in range(*blocks):
        q0 = b * block
        k0 = max(0, b - 1) * block
        k_doc = docs[:, k0 : k0 + 2 * block]
        q_doc = jnp.sum(jnp.where(k0 + column == q0 + row, k_doc, 0.0), axis=1, keepdims=True)
        allowed = (q_doc == k_doc) & (k0 + column <= q0 + row)
        penalty = jnp.concatenate([jnp.where(allowed, 0.0, -1e30)] * shared, axis=0)
        for g in range(groups):
            keys = kv_all[pl.ds(k0 - k_first, 2 * block), tile(g, HEAD_DIM)]
            values = kv_all[pl.ds(k0 - k_first, 2 * block), tile(groups + g, HEAD_DIM)]
            source = queries[g // per_half]
            columns = [tile((g % per_half) * shared + h, HEAD_DIM) for h in range(shared)]
            q = jnp.concatenate([source[pl.ds(q0 - q_first, block), c] for c in columns], axis=0)
            scores = lax.dot_general(q, keys, (((1,), (1,)), ((), ())), preferred_element_type=F32) * scale
            scores = jnp.where(penalty < 0.0, penalty, scores)
            weights = jnp.exp(scores - jnp.max(scores, axis=-1, keepdims=True))
            result = dot(weights.astype(BF16), jnp.concatenate([values, ones], axis=1))
            result = (result[:, :HEAD_DIM] / result[:, HEAD_DIM:]).astype(BF16)
            for h in range(shared):
                out[pl.ds(q0 - out_first, block), tile(g * shared + h, HEAD_DIM)] = result[h * block : (h + 1) * block]
        yield b


def late_kernel(early, join, doc_row, first_half, second_half, *rest):
    parts, out, kv_all = rest[:-2], rest[-2], rest[-1]
    seq = first_half.shape[0]
    sent = jnp.concatenate([part[pl.ds(0, seq), :] for part in parts], axis=1)
    kv_all[...] = dot(sent, join[...]).astype(BF16)
    blocks = (early // DOC_MAX, seq // DOC_MAX)
    for _ in attend(blocks, (0, 0, early), doc_row, (first_half, second_half), kv_all, out):
        pass


def early_kernel(early, order, doc_row, first_half, second_half, keyval, join, place, *rest):
    arrived = rest[:-7]
    late, out, first, second, kv_all, result, sem = rest[-7:]
    slots = place.shape[0]
    copies = [pltpu.make_async_copy(late, out.at[pl.ds(early, late.shape[0])], sem.at[0])]
    copies[0].start()
    half = first_half.shape[1]
    in_place = [arrived[order.index(x)][...].astype(F32) for x in range(len(order))]
    together = jnp.concatenate(in_place, axis=0).astype(BF16)
    placed = dot(place[...], together).astype(BF16)
    is_image = jnp.sum(place[...].astype(F32), axis=1, keepdims=True) > 0.5
    image_keyval = dot(placed[:, 2 * half :], join[...]).astype(BF16)
    kv_all[...] = keyval[pl.ds(0, early), :]
    kv_all[pl.ds(0, slots), :] = jnp.where(is_image, image_keyval, keyval[pl.ds(0, slots), :])
    for i, (source, target) in enumerate(((first_half, first), (second_half, second))):
        target[...] = source[pl.ds(0, early), :]
        target[pl.ds(0, slots), :] = jnp.where(
            is_image, placed[:, i * half : (i + 1) * half], source[pl.ds(0, slots), :]
        )
    for b in attend((0, early // DOC_MAX), (0, 0, 0), doc_row, (first, second), kv_all, result):
        here = pl.ds(b * DOC_MAX, DOC_MAX)
        copies.append(pltpu.make_async_copy(result.at[here], out.at[here], sem.at[b + 1]))
        copies[-1].start()
    for copy in copies:
        copy.wait()


def attention(join, place, documents, halves, parts, arrived, order, columns):
    seq = documents.shape[1]
    full = join.shape[1]
    slots = place.shape[0]
    owners = len(order)
    early = min(seq, -(-slots // DOC_MAX) * DOC_MAX + DOC_MAX)
    out, keyval = pl.pallas_call(
        functools.partial(late_kernel, early),
        out_shape=[pltpu.VMEM((seq - early, columns), BF16), jax.ShapeDtypeStruct((seq, full), BF16)],
        in_specs=[VMEM] * (4 + len(parts)),
        out_specs=[VMEM] * 2,
        compiler_params=params(12),
        cost_estimate=cost(4 * (seq - early) * columns * 2 * DOC_MAX, 4 * seq * columns),
        name="attention_late",
    )(join, documents, *halves, *parts)
    return pl.pallas_call(
        functools.partial(early_kernel, early, order),
        out_shape=jax.ShapeDtypeStruct((seq, columns), BF16),
        in_specs=[VMEM] * (7 + owners),
        out_specs=HBM,
        scratch_shapes=[pltpu.VMEM((early, columns // 2), BF16)] * 2
        + [pltpu.VMEM((early, full), BF16), pltpu.VMEM((early, columns), BF16), pltpu.SemaphoreType.DMA((1 + early // DOC_MAX,))],
        compiler_params=params(12),
        cost_estimate=cost(4 * early * columns * 2 * DOC_MAX, 4 * seq * columns),
        name="attention_early",
    )(documents, *halves, keyval, join, place, *arrived(out), in_vmem(out))


def after(x, *others):
    return lax.optimization_barrier((x, *others))[0]


def exchange(x, count, bit):
    return lax.ppermute(x, "mp", [(i, i ^ bit) for i in range(count)])


def per_device(
    patch_rows,
    ln_gain,
    ln_bias,
    merge_up,
    merge_up_bias,
    merge_down,
    merge_down_bias,
    row_owner,
    text_embed,
    doc_ids,
    rms_gain,
    w_query,
    query_bias,
    w_keyval,
    keyval_bias,
):
    owners = lax.axis_size(("group", "dp"))
    count = lax.axis_size("mp")
    mp_index = lax.axis_index("mp")
    where = jnp.stack([mp_index, lax.axis_index(("group", "dp"))]).astype(jnp.int32)
    rows = row_owner.shape[0] // owners
    capacity = max(2, 2 * rows // owners)
    owner_row = row_owner.reshape(1, -1)
    groups, line = lax.axis_size("group"), lax.axis_size("dp")

    def far(x):
        return max(abs(i % line - (i ^ x) % line) + (x >= line) for i in range(groups * line))


    send, keep, text = merger(
        where, patch_rows[0], ln_gain, ln_bias, merge_up, merge_up_bias, merge_down, merge_down_bias,
        text_embed[0], rms_gain[None, :], rows,
    )
    own = (keep.astype(F32) + exchange(send, count, 1).astype(F32)).astype(BF16)
    slots = owners * capacity
    weight, ready, select, place, join = weights_ahead(
        where, owner_row, after(w_keyval, own), w_query, w_query.shape[1] // 4, owners, slots
    )
    bit = 2
    while bit < count:
        other = after(exchange(own, count, bit), weight)
        own = (own.astype(F32) + other.astype(F32)).astype(BF16)
        bit *= 2
    sibling = exchange(own, count, 1)

    columns = w_query.shape[1]
    rows_all, scale, parts = keyval_parts(where, text, own, sibling, rms_gain[None, :], weight, keyval_bias, count)
    parts = [parts[0]] + [exchange(parts[x], count, x) for x in range(1, count)]
    *halves, image_queries = query_rows(rows_all, scale, text.shape[0], ready, w_query, query_bias[None, :])
    outgoing = slots_of(select, image_queries, parts, owners)

    order = sorted(range(1, owners), key=far, reverse=True)

    def arrived(done):
        rows = [lax.ppermute(outgoing[x], ("group", "dp"), [(i, i ^ x) for i in range(owners)]) for x in order]
        return lax.optimization_barrier((*rows, outgoing[0], done))[:-1]

    halves = [after(half, outgoing[0]) for half in halves]
    return attention(join, place, doc_ids, halves, parts, arrived, [*order, 0], columns)[None]


def general(
    patch_rows,
    ln_gain,
    ln_bias,
    merge_up,
    merge_up_bias,
    merge_down,
    merge_down_bias,
    row_owner,
    text_embed,
    doc_ids,
    rms_gain,
    w_query,
    query_bias,
    w_keyval,
    keyval_bias,
):
    owners = lax.axis_size(("group", "dp"))
    own_index = lax.axis_index(("group", "dp"))
    mp_index = lax.axis_index("mp")
    pixels = patch_rows[0].astype(jnp.float32)
    center = pixels - jnp.mean(pixels, axis=-1, keepdims=True)
    spread = jnp.mean(center * center, axis=-1, keepdims=True)
    normed_patch = (center * lax.rsqrt(spread + 1e-06) * ln_gain + ln_bias).astype(jnp.bfloat16)
    merged = normed_patch.reshape(-1, 4 * pixels.shape[1])
    merged_rows = merged.shape[0]
    hidden = jax.nn.gelu(
        jnp.dot(merged, merge_up, preferred_element_type=jnp.float32) + merge_up_bias,
        approximate=False,
    ).astype(jnp.bfloat16)
    partial_sum = jnp.dot(hidden, merge_down, preferred_element_type=jnp.float32)
    vision = (
        lax.psum_scatter(partial_sum, "mp", scatter_dimension=1, tiled=True) + merge_down_bias
    ).astype(jnp.bfloat16)
    col_width = vision.shape[1]
    capacity = max(2, 2 * merged_rows // owners)
    owner_all = row_owner[:, 0]
    owner_ids = jnp.arange(owners, dtype=jnp.int32)
    onehot = (owner_all[:, None] == owner_ids[None, :]).astype(jnp.int32)
    per_source = jnp.sum(onehot.reshape(owners, merged_rows, owners), axis=1)
    my_block = lax.dynamic_slice_in_dim(onehot, own_index * merged_rows, merged_rows, 0)
    block_rank = jnp.sum((jnp.cumsum(my_block, axis=0) - my_block) * my_block, axis=1)
    my_owner = jnp.sum(my_block * owner_ids[None, :], axis=1)
    slot_id = my_owner * capacity + block_rank
    all_slots = jnp.arange(owners * capacity, dtype=jnp.int32)
    select = (slot_id[:, None] == all_slots[None, :]).astype(jnp.bfloat16)
    outgoing = jnp.einsum("ms,mc->sc", select, vision, preferred_element_type=jnp.float32).astype(
        jnp.bfloat16
    )
    arrived = lax.all_to_all(
        outgoing.reshape(owners, capacity, col_width),
        ("group", "dp"),
        split_axis=0,
        concat_axis=0,
        tiled=True,
    )
    arrived = arrived.reshape(owners * capacity, col_width)
    incoming = lax.dynamic_slice_in_dim(per_source, own_index, 1, 1)[:, 0]
    offsets = jnp.cumsum(incoming) - incoming
    total = jnp.sum(incoming)
    slot_rank = jnp.arange(capacity, dtype=jnp.int32)
    target = jnp.where(
        slot_rank[None, :] < incoming[:, None], offsets[:, None] + slot_rank[None, :], -1
    ).reshape(-1)
    text_rows = text_embed[0]
    seq_len = text_rows.shape[0]
    positions = jnp.arange(seq_len, dtype=jnp.int32)
    source_slot = jnp.sum(
        jnp.where(target[:, None] == positions[None, :], all_slots[:, None], 0), axis=0
    )
    is_image = (positions < total)[:, None]
    image_full = lax.all_gather(arrived, "mp", axis=1, tiled=True)
    sequence = jnp.where(is_image, jnp.take(image_full, source_slot, axis=0), text_rows)
    seq_f = sequence.astype(jnp.float32)
    normed_seq = (
        seq_f * lax.rsqrt(jnp.mean(seq_f * seq_f, axis=-1, keepdims=True) + 1e-06) * rms_gain
    ).astype(jnp.bfloat16)
    queries = (
        jnp.dot(normed_seq, w_query, preferred_element_type=jnp.float32) + query_bias
    ).astype(jnp.bfloat16)
    keyval_local = (
        jnp.einsum("sd,dtc->stc", normed_seq, w_keyval, preferred_element_type=jnp.float32)
        + keyval_bias
    ).astype(jnp.bfloat16)
    keyval_full = lax.all_gather(keyval_local, "mp", axis=2, tiled=True)
    keyval_heads = jnp.transpose(keyval_full.reshape(seq_len, 2, HEAD_DIM, KV_HEADS), (0, 1, 3, 2))
    local_heads = queries.shape[1] // HEAD_DIM
    group_size = HEADS // KV_HEADS
    kv_index = (mp_index * local_heads + jnp.arange(local_heads, dtype=jnp.int32)) // group_size
    keys = jnp.take(keyval_heads[:, 0], kv_index, axis=1)
    values = jnp.take(keyval_heads[:, 1], kv_index, axis=1)
    query_heads = queries.reshape(seq_len, local_heads, HEAD_DIM)
    scores = jnp.einsum(
        "qhd,khd->hqk", query_heads, keys, preferred_element_type=jnp.float32
    ) / math.sqrt(HEAD_DIM)
    documents = doc_ids[0]
    allowed = (documents[:, None] == documents[None, :]) & (
        positions[None, :] <= positions[:, None]
    )
    scores = jnp.where(allowed[None], scores, jnp.float32(-1e30))
    highest = jnp.max(scores, axis=-1, keepdims=True)
    weights = jnp.exp(scores - highest)
    probs = (weights / jnp.sum(weights, axis=-1, keepdims=True)).astype(jnp.bfloat16)
    output = jnp.einsum("hqk,khd->qhd", probs, values, preferred_element_type=jnp.float32)
    return output.astype(jnp.bfloat16).reshape(1, seq_len, local_heads * HEAD_DIM)


def solution(mesh):
    in_specs = (
        P(("group", "dp"), None, None),
        P(),
        P(),
        P(None, "mp"),
        P("mp"),
        P("mp", None),
        P("mp"),
        P(),
        P(("group", "dp"), None, None),
        P(("group", "dp"), None),
        P(),
        P(None, "mp"),
        P("mp"),
        P(None, None, "mp"),
        P(None, "mp"),
    )
    out_specs = P(("group", "dp"), None, "mp")
    count = mesh.shape["mp"]
    owners = mesh.shape["group"] * mesh.shape["dp"]
    narrow = count < 2 or count > KV_HEADS or count & (count - 1) or owners & (owners - 1)
    body = general if narrow else per_device
    return jax.shard_map(body, mesh=mesh, in_specs=in_specs, out_specs=out_specs, check_vma=False)
```

```python
import functools
import math

import jax
import jax.numpy as jnp
from jax import lax
from jax.experimental import pallas as pl
from jax.experimental.pallas import tpu as pltpu
from jax.sharding import PartitionSpec as P

HEADS = 64
KV_HEADS = 8
HEAD_DIM = 128
DOC_MAX = 64

BF16 = jnp.bfloat16
F32 = jnp.float32
VMEM = pl.BlockSpec(memory_space=pltpu.VMEM)
SMEM = pl.BlockSpec(memory_space=pltpu.SMEM)
ANY = pl.BlockSpec(memory_space=pl.ANY)
HBM = pl.BlockSpec(memory_space=pltpu.HBM)
AHEAD = 3
DEEP = 5
MIB = 1 << 20


def dot(a, b):
    return jnp.dot(a, b, preferred_element_type=F32)


def in_hbm(x):
    return pltpu.with_memory_space_constraint(x, pltpu.HBM)


def in_vmem(x):
    return pltpu.with_memory_space_constraint(x, pltpu.VMEM)


def params(mib):
    return pltpu.CompilerParams(vmem_limit_bytes=mib * MIB)


def cost(flops, nbytes):
    return pl.CostEstimate(flops=flops, bytes_accessed=nbytes, transcendentals=0)


def rms_scale(x, width):
    return lax.rsqrt(jnp.sum(x * x, axis=-1, keepdims=True) / width + 1e-06)


def stream(count, copy, body, ahead=AHEAD, then=None):
    @pl.loop(0, count)
    def _(i):
        copy(i).wait()

        @pl.when(i + ahead < count)
        def _():
            copy(i + ahead).start()

        if then is not None:

            @pl.when(i + ahead >= count)
            def _():
                then(i + ahead - count).start()

        body(i)


def begin(copy, ahead=AHEAD):
    for i in range(ahead):
        copy(i).start()


def tile(i, width):
    return pl.ds(pl.multiple_of(i * width, width), width)


def merger_kernel(
    where, patch_in, gain_in, bias_in, up, up_bias_in, down, down_bias_in, text, rms_gain_in, send, keep, text_out,
    patch, gain, bias, up_bias, down_bias, rms_gain, bias_row, normed, merged, total, up_buf, down_buf, text_buf,
    small_sem, up_sem, down_sem, text_sem,
):
    slots = DEEP + 1
    step = up_buf.shape[1]
    width = down_buf.shape[2]
    half = send.shape[1]
    per_half = half // width
    mp = where[0]
    mine = mp % 2
    pairs = [(patch_in, patch), (gain_in, gain), (bias_in, bias), (up_bias_in, up_bias), (down_bias_in, down_bias)]
    pairs.append((rms_gain_in, rms_gain))
    small = [pltpu.make_async_copy(x, y, small_sem.at[i]) for i, (x, y) in enumerate(pairs)]
    for copy in small:
        copy.start()

    def up_copy(i):
        return pltpu.make_async_copy(up.at[tile(i, step)], up_buf.at[i % slots], up_sem.at[i % slots])

    def column(i):
        first = jnp.where(i < per_half, 1 - mine, mine)
        return pl.multiple_of(first * half + (i % per_half) * width, width)

    def down_copy(i):
        return pltpu.make_async_copy(
            down.at[:, pl.ds(column(i), width)], down_buf.at[i % slots], down_sem.at[i % slots]
        )

    block = text_buf.shape[1]
    blocks = text.shape[0] // block

    def text_copy(i):
        return pltpu.make_async_copy(text.at[tile(i, block)], text_buf.at[i % slots], text_sem.at[i % slots])

    def text_norm(i):
        text_copy(i).wait()

        @pl.when(i + DEEP < blocks)
        def _():
            text_copy(i + DEEP).start()

        x = text_buf[i % slots].astype(F32)
        text_out[tile(i, block), :] = (x * rms_scale(x, x.shape[1]) * rms_gain[...]).astype(BF16)

    begin(up_copy, DEEP)
    begin(text_copy, DEEP)
    for copy in small:
        copy.wait()
    rows = send.shape[0]
    joined = patch.shape[0] // rows
    features = patch.shape[1]
    pixels = patch[...].astype(F32)
    center = pixels - jnp.mean(pixels, axis=-1, keepdims=True)
    spread = jnp.mean(center * center, axis=-1, keepdims=True)
    patches = center * lax.rsqrt(spread + 1e-06) * gain[...][None, :] + bias[...][None, :]
    for c in range(features // 128):
        normed[c] = patches[:, c * 128 : (c + 1) * 128]
        for j in range(joined):
            merged[:, pl.ds(j * features + c * 128, 128)] = normed[c, pl.ds(j, rows, stride=joined), :].astype(BF16)
    own = down_bias.shape[0]
    bias_row[...] = jnp.zeros_like(bias_row)
    bias_row[:, pl.ds(pl.multiple_of(mp * own, 128), own)] = down_bias[...][None, :]
    total[...] = jnp.broadcast_to(up_bias[...][None, :], total.shape)

    def up_body(i):
        text_norm(i)
        total[...] += dot(merged[:, tile(i, step)], up_buf[i % slots])

    up_steps = up.shape[0] // step
    stream(up_steps, up_copy, up_body, DEEP, down_copy)
    sums = total[...]
    hidden = (0.5 * sums * (1.0 + lax.erf(sums * math.sqrt(0.5)))).astype(BF16)

    def down_body(i):
        text_norm(up_steps + i)
        part = (dot(hidden, down_buf[i % slots]) + bias_row[:, pl.ds(column(i), width)]).astype(BF16)
        here = tile(i % per_half, width)

        @pl.when(i < per_half)
        def _():
            send[:, here] = part

        @pl.when(i >= per_half)
        def _():
            keep[:, here] = part

    stream(2 * per_half, down_copy, down_body, DEEP)


def merger(where, patch, gain, bias, up, up_bias, down, down_bias, text, rms_gain, rows):
    features = patch.shape[1]
    depth, hidden = up.shape
    columns = down.shape[1]
    step = depth // 8
    width = columns // 8
    slots = DEEP + 1
    return pl.pallas_call(
        merger_kernel,
        out_shape=[jax.ShapeDtypeStruct((rows, columns // 2), BF16)] * 2 + [pltpu.VMEM(text.shape, BF16)],
        in_specs=[SMEM] + [HBM] * 9,
        out_specs=[VMEM, VMEM, VMEM],
        scratch_shapes=[
            pltpu.VMEM(patch.shape, BF16),
            pltpu.VMEM(gain.shape, F32),
            pltpu.VMEM(bias.shape, F32),
            pltpu.VMEM(up_bias.shape, F32),
            pltpu.VMEM(down_bias.shape, F32),
            pltpu.VMEM(rms_gain.shape, F32),
            pltpu.VMEM((1, columns), F32),
            pltpu.VMEM((features // 128, patch.shape[0], 128), F32),
            pltpu.VMEM((rows, depth), BF16),
            pltpu.VMEM((rows, hidden), F32),
            pltpu.VMEM((slots, step, hidden), BF16),
            pltpu.VMEM((slots, hidden, width), BF16),
            pltpu.VMEM((slots, text.shape[0] // 16, text.shape[1]), BF16),
            pltpu.SemaphoreType.DMA((6,)),
            pltpu.SemaphoreType.DMA((slots,)),
            pltpu.SemaphoreType.DMA((slots,)),
            pltpu.SemaphoreType.DMA((slots,)),
        ],
        compiler_params=params(34),
        cost_estimate=cost(2 * rows * hidden * (depth + columns), 2 * hidden * (depth + columns)),
        name="merger",
    )(where, *map(in_hbm, (patch, gain, bias, up, up_bias, down, down_bias, text, rms_gain)))


def owner_slots(owner_row, me, rows, capacity, slots):
    total = owner_row.shape[1]
    row = lax.broadcasted_iota(jnp.int32, (total, rows), 0)
    mine = (row == me * rows + lax.broadcasted_iota(jnp.int32, (total, rows), 1)).astype(F32).astype(BF16)
    named = (owner_row[...] ^ me).astype(F32).astype(BF16)
    across = dot(named, mine)
    down = lax.dot_general(mine, named, (((0,), (1,)), ((), ())), preferred_element_type=F32)
    earlier = lax.broadcasted_iota(jnp.int32, (rows, rows), 0) < lax.broadcasted_iota(jnp.int32, (rows, rows), 1)
    rank = jnp.sum(jnp.where((down == across) & earlier, 1.0, 0.0), axis=0, keepdims=True)
    slot = across * capacity + rank
    return (lax.broadcasted_iota(jnp.int32, (slots, rows), 0).astype(F32) == slot).astype(F32).astype(BF16)


def slot_places(owner_row, me, owners, slots):
    total = owner_row.shape[1]
    capacity = slots // owners
    named = (owner_row[...] == me).astype(F32).astype(BF16)
    source = lax.broadcasted_iota(jnp.int32, (total, slots), 0) // (total // owners)
    block = (lax.broadcasted_iota(jnp.int32, (total, slots), 1) // capacity) ^ me
    here = dot(named, (source == block).astype(F32).astype(BF16))
    offset = dot(named, (source < block).astype(F32).astype(BF16))
    index = (lax.broadcasted_iota(jnp.int32, (1, slots), 1) % capacity).astype(F32)
    target = jnp.where(index < here, offset + index, -1.0)
    position = lax.broadcasted_iota(jnp.int32, (slots, slots), 0).astype(F32)
    return (position == target).astype(F32).astype(BF16)


def join_matrix(mp, count, width):
    heads = KV_HEADS // count
    coords = HEAD_DIM // count
    full = 2 * heads * HEAD_DIM
    column = lax.broadcasted_iota(jnp.int32, (width, full), 1)
    row = lax.broadcasted_iota(jnp.int32, (width, full), 0)
    base = (row // coords) * HEAD_DIM + row % coords
    places = [(column == base + (mp ^ x) * coords).astype(F32).astype(BF16) for x in range(count)]
    return jnp.concatenate(places, axis=0)


def weights_kernel(owners, where, owner_row, keyval, query, out, query_out, select, place, join, buf, sem, query_sem):
    depth, _, columns = keyval.shape
    pieces = sem.shape[0]
    step = depth // pieces
    together = step // 128

    def copy(i):
        return pltpu.make_async_copy(keyval.at[tile(i, step)], buf.at[tile(i, step)], sem.at[i])

    for i in range(pieces):
        copy(i).start()
    part = depth // query_sem.shape[0]
    copies = [
        pltpu.make_async_copy(
            query.at[pl.ds(i * part, part), pl.ds(0, query_out.shape[1])],
            query_out.at[pl.ds(i * part, part)],
            query_sem.at[i],
        )
        for i in range(query_sem.shape[0])
    ]
    for query_copy in copies:
        query_copy.start()
    mp, me = where[0], where[1]
    slots, rows = select.shape
    select[...] = owner_slots(owner_row, me, rows, slots // owners, slots)
    place[...] = slot_places(owner_row, me, owners, slots)
    count = KV_HEADS * HEAD_DIM // columns
    join[...] = join_matrix(mp, count, join.shape[0] // count)
    pairs = buf.reshape(2 * depth, columns)
    row = lax.broadcasted_iota(jnp.int32, (256, 256), 0)
    column = lax.broadcasted_iota(jnp.int32, (256, 256), 1)
    apart = (column == 2 * (row % 128) + row // 128).astype(F32).astype(BF16)

    @pl.loop(0, pieces)
    def _(j):
        copy(j).wait()
        blocks = [pairs[tile(j * together + n, 256), :] for n in range(together)]
        ordered = dot(apart, jnp.concatenate(blocks, axis=1)).astype(BF16)
        for n in range(together):
            for side in range(2):
                out[tile(j * together + n, 128), pl.ds(side * columns, columns)] = ordered[
                    side * 128 : (side + 1) * 128, n * columns : (n + 1) * columns
                ]

    for query_copy in copies:
        query_copy.wait()


def weights_ahead(where, owner_row, keyval, query, width, owners, slots):
    depth, _, columns = keyval.shape
    rows = owner_row.shape[1] // owners
    return pl.pallas_call(
        functools.partial(weights_kernel, owners),
        out_shape=[
            pltpu.VMEM((depth, 2 * columns), BF16),
            pltpu.VMEM((depth, width), BF16),
            jax.ShapeDtypeStruct((slots, rows), BF16),
            jax.ShapeDtypeStruct((slots, slots), BF16),
            jax.ShapeDtypeStruct((2 * columns, 2 * columns), BF16),
        ],
        in_specs=[SMEM, VMEM, HBM, HBM],
        out_specs=[VMEM] * 5,
        scratch_shapes=[pltpu.VMEM(keyval.shape, BF16), pltpu.SemaphoreType.DMA((8,)), pltpu.SemaphoreType.DMA((4,))],
        compiler_params=params(16),
        cost_estimate=cost(4 * depth * columns * 256, 4 * depth * columns),
        name="weights_ahead",
    )(where, owner_row, in_hbm(keyval), in_hbm(query))


def keyval_own_kernel(where, text, own, gain, weight, rows_all, sums):
    texts, half = text.shape[0], own.shape[1]
    here = pl.ds(pl.multiple_of((where[0] % 2) * half, half), half)
    rows_all[pl.ds(0, texts), :] = text[...]
    rows_all[pl.ds(texts, own.shape[0]), here] = (own[...].astype(F32) * gain[:, here]).astype(BF16)
    sums[...] = dot(rows_all[:, here], weight[here, :])


def keyval_kernel(where, _, sums_in, own, sibling, gain, weight, bias, rows_all, scale_out, *rest):
    parts, keyval = rest[:-1], rest[-1]
    images, half = own.shape
    texts = rows_all.shape[0] - images
    mp = where[0]
    here = pl.ds(pl.multiple_of((1 - mp % 2) * half, half), half)
    first, second = own[...].astype(F32), sibling[...].astype(F32)
    rows_all[pl.ds(texts, images), here] = (second * gain[:, here]).astype(BF16)
    squares = jnp.sum(first * first, axis=-1, keepdims=True) + jnp.sum(second * second, axis=-1, keepdims=True)
    scale = lax.rsqrt(squares / (2 * half) + 1e-06)
    scale_out[...] = jnp.broadcast_to(scale, scale_out.shape)
    columns = weight.shape[1] // 2
    sums = sums_in[...] + dot(rows_all[:, here], weight[here, :])
    for t in range(2):
        side = slice(t * columns, (t + 1) * columns)
        add = bias[pl.ds(t, 1), :]
        keyval[t, pl.ds(0, texts), :] = (sums[:texts, side] + add).astype(BF16)
        keyval[t, pl.ds(texts, images), :] = (sums[texts:, side] * scale + add).astype(BF16)

    count = len(parts)
    width = parts[0].shape[1]
    heads = KV_HEADS // count
    coords = columns // KV_HEADS
    row = lax.broadcasted_iota(jnp.int32, (columns, width // 2), 0)
    column = lax.broadcasted_iota(jnp.int32, (columns, width // 2), 1)
    for x in range(count):
        head = (mp ^ x) * heads + column // coords
        pick = (row == (column % coords) * KV_HEADS + head).astype(F32).astype(BF16)
        for t in range(2):
            parts[x][:, pl.ds(t * (width // 2), width // 2)] = dot(keyval[t], pick).astype(BF16)


def keyval_parts(where, text, own, sibling, gain, weight, bias, count):
    texts, depth = text.shape
    columns = weight.shape[1] // 2
    images = own.shape[0]
    rows = texts + images
    width = 2 * columns // count
    weight = in_vmem(weight)
    rows_all, sums = pl.pallas_call(
        keyval_own_kernel,
        out_shape=[pltpu.VMEM((rows, depth), BF16), pltpu.VMEM((rows, 2 * columns), F32)],
        in_specs=[SMEM, VMEM, VMEM, VMEM, VMEM],
        out_specs=[VMEM] * 2,
        compiler_params=params(8),
        cost_estimate=cost(2 * rows * depth * columns, 2 * depth * columns),
        name="keyval_own",
    )(where, in_vmem(text), own, gain, weight)
    outs = pl.pallas_call(
        keyval_kernel,
        out_shape=[pltpu.VMEM((rows, depth), BF16), jax.ShapeDtypeStruct((images, 128), F32)]
        + [jax.ShapeDtypeStruct((rows, width), BF16)] * count,
        in_specs=[SMEM] + [VMEM] * 7,
        out_specs=[VMEM] * (2 + count),
        scratch_shapes=[pltpu.VMEM((2, rows, columns), BF16)],
        input_output_aliases={1: 0},
        compiler_params=params(8),
        cost_estimate=cost(2 * rows * depth * columns, 2 * depth * columns),
        name="keyval",
    )(where, in_vmem(rows_all), in_vmem(sums), own, after(sibling, sums), gain, weight, bias)
    return outs[0], outs[1], outs[2:]


def query_kernel(rows_all, scale, ready, weight, bias, first_half, second_half, image_out, buf, sem):
    width = ready.shape[1]
    texts, half = first_half.shape
    later = buf.shape[0]

    def copy(i):
        return pltpu.make_async_copy(weight.at[:, tile(i + 1, width)], buf.at[i], sem.at[i])

    def columns(i, weights, text_out, offset):
        out = dot(rows_all[...], weights)
        add = bias[:, tile(i, width)]
        text_out[:, pl.ds(i * width - offset, width)] = (out[:texts] + add).astype(BF16)
        image_out[:, tile(i, width)] = (out[texts:] * scale[:, :1] + add).astype(BF16)

    begin(copy, 2)
    columns(0, ready[...], first_half, 0)
    for i in range(1, later + 1):
        copy(i - 1).wait()
        if i + 1 < later:
            copy(i + 1).start()
        if i * width < half:
            columns(i, buf[i - 1], first_half, 0)
        else:
            columns(i, buf[i - 1], second_half, half)


def query_rows(rows_all, scale, texts, ready, weight, bias):
    depth = rows_all.shape[1]
    images = rows_all.shape[0] - texts
    columns = weight.shape[1]
    width = ready.shape[1]
    later = columns // width - 1
    return pl.pallas_call(
        query_kernel,
        out_shape=[jax.ShapeDtypeStruct((texts, columns // 2), BF16)] * 2 + [jax.ShapeDtypeStruct((images, columns), BF16)],
        in_specs=[VMEM, VMEM, VMEM, HBM, VMEM],
        out_specs=[VMEM] * 3,
        scratch_shapes=[pltpu.VMEM((later, depth, width), BF16), pltpu.SemaphoreType.DMA((later,))],
        compiler_params=params(30),
        cost_estimate=cost(2 * (texts + images) * depth * columns, 2 * depth * columns),
        name="query",
    )(in_vmem(rows_all), scale, in_vmem(ready), in_hbm(weight), bias)


def slots_kernel(owners, select, queries, *rest):
    parts, outs = rest[:-owners], rest[-owners:]
    rows = queries.shape[0]
    capacity = outs[0].shape[0]
    images = [queries[...]] + [part[pl.ds(part.shape[0] - rows, rows), :] for part in parts]
    chosen = dot(select[...], jnp.concatenate(images, axis=1))
    for x, out in enumerate(outs):
        out[...] = chosen[x * capacity : (x + 1) * capacity].astype(BF16)


def slots_of(select, queries, parts, owners):
    width = queries.shape[1] + len(parts) * parts[0].shape[1]
    capacity = select.shape[0] // owners
    return pl.pallas_call(
        functools.partial(slots_kernel, owners),
        out_shape=[jax.ShapeDtypeStruct((capacity, width), BF16)] * owners,
        in_specs=[VMEM] * (2 + len(parts)),
        out_specs=[VMEM] * owners,
        compiler_params=params(8),
        name="slots",
    )(select, queries, *parts)


def attend(blocks, first, doc_row, queries, kv_all, out):
    q_first, k_first, out_first = first
    groups = kv_all.shape[1] // (2 * HEAD_DIM)
    per_half = groups // len(queries)
    shared = queries[0].shape[1] // HEAD_DIM // per_half
    block = DOC_MAX
    scale = 1.0 / math.sqrt(HEAD_DIM)
    docs = doc_row[...].astype(F32)
    ones = jnp.ones((2 * block, HEAD_DIM), BF16)
    row = lax.broadcasted_iota(jnp.int32, (block, 2 * block), 0)
    column = lax.broadcasted_iota(jnp.int32, (block, 2 * block), 1)
    for b in range(*blocks):
        q0 = b * block
        k0 = max(0, b - 1) * block
        k_doc = docs[:, k0 : k0 + 2 * block]
        q_doc = jnp.sum(jnp.where(k0 + column == q0 + row, k_doc, 0.0), axis=1, keepdims=True)
        allowed = (q_doc == k_doc) & (k0 + column <= q0 + row)
        penalty = jnp.concatenate([jnp.where(allowed, 0.0, -1e30)] * shared, axis=0)
        for g in range(groups):
            keys = kv_all[pl.ds(k0 - k_first, 2 * block), tile(g, HEAD_DIM)]
            values = kv_all[pl.ds(k0 - k_first, 2 * block), tile(groups + g, HEAD_DIM)]
            source = queries[g // per_half]
            columns = [tile((g % per_half) * shared + h, HEAD_DIM) for h in range(shared)]
            q = jnp.concatenate([source[pl.ds(q0 - q_first, block), c] for c in columns], axis=0)
            scores = lax.dot_general(q, keys, (((1,), (1,)), ((), ())), preferred_element_type=F32) * scale
            scores = jnp.where(penalty < 0.0, penalty, scores)
            weights = jnp.exp(scores - jnp.max(scores, axis=-1, keepdims=True))
            result = dot(weights.astype(BF16), jnp.concatenate([values, ones], axis=1))
            result = (result[:, :HEAD_DIM] / result[:, HEAD_DIM:]).astype(BF16)
            for h in range(shared):
                out[pl.ds(q0 - out_first, block), tile(g * shared + h, HEAD_DIM)] = result[h * block : (h + 1) * block]
        yield b


def late_kernel(early, join, doc_row, first_half, second_half, *rest):
    parts, out, kv_all = rest[:-2], rest[-2], rest[-1]
    seq = first_half.shape[0]
    sent = jnp.concatenate([part[pl.ds(0, seq), :] for part in parts], axis=1)
    kv_all[...] = dot(sent, join[...]).astype(BF16)
    blocks = (early // DOC_MAX, seq // DOC_MAX)
    for _ in attend(blocks, (0, 0, early), doc_row, (first_half, second_half), kv_all, out):
        pass


def early_kernel(early, order, doc_row, first_half, second_half, keyval, join, place, *rest):
    arrived = rest[:-7]
    late, out, first, second, kv_all, result, sem = rest[-7:]
    slots = place.shape[0]
    copies = [pltpu.make_async_copy(late, out.at[pl.ds(early, late.shape[0])], sem.at[0])]
    copies[0].start()
    half = first_half.shape[1]
    in_place = [arrived[order.index(x)][...].astype(F32) for x in range(len(order))]
    together = jnp.concatenate(in_place, axis=0).astype(BF16)
    placed = dot(place[...], together).astype(BF16)
    is_image = jnp.sum(place[...].astype(F32), axis=1, keepdims=True) > 0.5
    image_keyval = dot(placed[:, 2 * half :], join[...]).astype(BF16)
    kv_all[...] = keyval[pl.ds(0, early), :]
    kv_all[pl.ds(0, slots), :] = jnp.where(is_image, image_keyval, keyval[pl.ds(0, slots), :])
    for i, (source, target) in enumerate(((first_half, first), (second_half, second))):
        target[...] = source[pl.ds(0, early), :]
        target[pl.ds(0, slots), :] = jnp.where(
            is_image, placed[:, i * half : (i + 1) * half], source[pl.ds(0, slots), :]
        )
    for b in attend((0, early // DOC_MAX), (0, 0, 0), doc_row, (first, second), kv_all, result):
        here = pl.ds(b * DOC_MAX, DOC_MAX)
        copies.append(pltpu.make_async_copy(result.at[here], out.at[here], sem.at[b + 1]))
        copies[-1].start()
    for copy in copies:
        copy.wait()


def attention(join, place, documents, halves, parts, arrived, order, columns):
    seq = documents.shape[1]
    full = join.shape[1]
    slots = place.shape[0]
    owners = len(order)
    early = min(seq, -(-slots // DOC_MAX) * DOC_MAX + DOC_MAX)
    out, keyval = pl.pallas_call(
        functools.partial(late_kernel, early),
        out_shape=[pltpu.VMEM((seq - early, columns), BF16), jax.ShapeDtypeStruct((seq, full), BF16)],
        in_specs=[VMEM] * (4 + len(parts)),
        out_specs=[VMEM] * 2,
        compiler_params=params(12),
        cost_estimate=cost(4 * (seq - early) * columns * 2 * DOC_MAX, 4 * seq * columns),
        name="attention_late",
    )(join, documents, *halves, *parts)
    return pl.pallas_call(
        functools.partial(early_kernel, early, order),
        out_shape=jax.ShapeDtypeStruct((seq, columns), BF16),
        in_specs=[VMEM] * (7 + owners),
        out_specs=HBM,
        scratch_shapes=[pltpu.VMEM((early, columns // 2), BF16)] * 2
        + [pltpu.VMEM((early, full), BF16), pltpu.VMEM((early, columns), BF16), pltpu.SemaphoreType.DMA((1 + early // DOC_MAX,))],
        compiler_params=params(12),
        cost_estimate=cost(4 * early * columns * 2 * DOC_MAX, 4 * seq * columns),
        name="attention_early",
    )(documents, *halves, keyval, join, place, *arrived(out), in_vmem(out))


def after(x, *others):
    return lax.optimization_barrier((x, *others))[0]


def exchange(x, count, bit):
    return lax.ppermute(x, "mp", [(i, i ^ bit) for i in range(count)])


def per_device(
    patch_rows,
    ln_gain,
    ln_bias,
    merge_up,
    merge_up_bias,
    merge_down,
    merge_down_bias,
    row_owner,
    text_embed,
    doc_ids,
    rms_gain,
    w_query,
    query_bias,
    w_keyval,
    keyval_bias,
):
    owners = lax.axis_size(("group", "dp"))
    count = lax.axis_size("mp")
    mp_index = lax.axis_index("mp")
    where = jnp.stack([mp_index, lax.axis_index(("group", "dp"))]).astype(jnp.int32)
    rows = row_owner.shape[0] // owners
    capacity = max(2, 2 * rows // owners)
    owner_row = row_owner.reshape(1, -1)
    groups, line = lax.axis_size("group"), lax.axis_size("dp")

    def far(x):
        return max(abs(i % line - (i ^ x) % line) + (x >= line) for i in range(groups * line))


    send, keep, text = merger(
        where, patch_rows[0], ln_gain, ln_bias, merge_up, merge_up_bias, merge_down, merge_down_bias,
        text_embed[0], rms_gain[None, :], rows,
    )
    own = (keep.astype(F32) + exchange(send, count, 1).astype(F32)).astype(BF16)
    slots = owners * capacity
    weight, ready, select, place, join = weights_ahead(
        where, owner_row, after(w_keyval, own), w_query, w_query.shape[1] // 4, owners, slots
    )
    bit = 2
    while bit < count:
        other = after(exchange(own, count, bit), weight)
        own = (own.astype(F32) + other.astype(F32)).astype(BF16)
        bit *= 2
    sibling = exchange(own, count, 1)

    columns = w_query.shape[1]
    rows_all, scale, parts = keyval_parts(where, text, own, sibling, rms_gain[None, :], weight, keyval_bias, count)
    parts = [parts[0]] + [exchange(parts[x], count, x) for x in range(1, count)]
    *halves, image_queries = query_rows(rows_all, scale, text.shape[0], ready, w_query, query_bias[None, :])
    outgoing = slots_of(select, image_queries, parts, owners)

    order = sorted(range(1, owners), key=lambda x: (x % 2 == 0, -x if x % 2 else -far(x)))

    def arrived(done):
        rows = [lax.ppermute(outgoing[x], ("group", "dp"), [(i, i ^ x) for i in range(owners)]) for x in order]
        return lax.optimization_barrier((*rows, outgoing[0], done))[:-1]

    halves = [after(half, outgoing[0]) for half in halves]
    return attention(join, place, doc_ids, halves, parts, arrived, [*order, 0], columns)[None]


def general(
    patch_rows,
    ln_gain,
    ln_bias,
    merge_up,
    merge_up_bias,
    merge_down,
    merge_down_bias,
    row_owner,
    text_embed,
    doc_ids,
    rms_gain,
    w_query,
    query_bias,
    w_keyval,
    keyval_bias,
):
    owners = lax.axis_size(("group", "dp"))
    own_index = lax.axis_index(("group", "dp"))
    mp_index = lax.axis_index("mp")
    pixels = patch_rows[0].astype(jnp.float32)
    center = pixels - jnp.mean(pixels, axis=-1, keepdims=True)
    spread = jnp.mean(center * center, axis=-1, keepdims=True)
    normed_patch = (center * lax.rsqrt(spread + 1e-06) * ln_gain + ln_bias).astype(jnp.bfloat16)
    merged = normed_patch.reshape(-1, 4 * pixels.shape[1])
    merged_rows = merged.shape[0]
    hidden = jax.nn.gelu(
        jnp.dot(merged, merge_up, preferred_element_type=jnp.float32) + merge_up_bias,
        approximate=False,
    ).astype(jnp.bfloat16)
    partial_sum = jnp.dot(hidden, merge_down, preferred_element_type=jnp.float32)
    vision = (
        lax.psum_scatter(partial_sum, "mp", scatter_dimension=1, tiled=True) + merge_down_bias
    ).astype(jnp.bfloat16)
    col_width = vision.shape[1]
    capacity = max(2, 2 * merged_rows // owners)
    owner_all = row_owner[:, 0]
    owner_ids = jnp.arange(owners, dtype=jnp.int32)
    onehot = (owner_all[:, None] == owner_ids[None, :]).astype(jnp.int32)
    per_source = jnp.sum(onehot.reshape(owners, merged_rows, owners), axis=1)
    my_block = lax.dynamic_slice_in_dim(onehot, own_index * merged_rows, merged_rows, 0)
    block_rank = jnp.sum((jnp.cumsum(my_block, axis=0) - my_block) * my_block, axis=1)
    my_owner = jnp.sum(my_block * owner_ids[None, :], axis=1)
    slot_id = my_owner * capacity + block_rank
    all_slots = jnp.arange(owners * capacity, dtype=jnp.int32)
    select = (slot_id[:, None] == all_slots[None, :]).astype(jnp.bfloat16)
    outgoing = jnp.einsum("ms,mc->sc", select, vision, preferred_element_type=jnp.float32).astype(
        jnp.bfloat16
    )
    arrived = lax.all_to_all(
        outgoing.reshape(owners, capacity, col_width),
        ("group", "dp"),
        split_axis=0,
        concat_axis=0,
        tiled=True,
    )
    arrived = arrived.reshape(owners * capacity, col_width)
    incoming = lax.dynamic_slice_in_dim(per_source, own_index, 1, 1)[:, 0]
    offsets = jnp.cumsum(incoming) - incoming
    total = jnp.sum(incoming)
    slot_rank = jnp.arange(capacity, dtype=jnp.int32)
    target = jnp.where(
        slot_rank[None, :] < incoming[:, None], offsets[:, None] + slot_rank[None, :], -1
    ).reshape(-1)
    text_rows = text_embed[0]
    seq_len = text_rows.shape[0]
    positions = jnp.arange(seq_len, dtype=jnp.int32)
    source_slot = jnp.sum(
        jnp.where(target[:, None] == positions[None, :], all_slots[:, None], 0), axis=0
    )
    is_image = (positions < total)[:, None]
    image_full = lax.all_gather(arrived, "mp", axis=1, tiled=True)
    sequence = jnp.where(is_image, jnp.take(image_full, source_slot, axis=0), text_rows)
    seq_f = sequence.astype(jnp.float32)
    normed_seq = (
        seq_f * lax.rsqrt(jnp.mean(seq_f * seq_f, axis=-1, keepdims=True) + 1e-06) * rms_gain
    ).astype(jnp.bfloat16)
    queries = (
        jnp.dot(normed_seq, w_query, preferred_element_type=jnp.float32) + query_bias
    ).astype(jnp.bfloat16)
    keyval_local = (
        jnp.einsum("sd,dtc->stc", normed_seq, w_keyval, preferred_element_type=jnp.float32)
        + keyval_bias
    ).astype(jnp.bfloat16)
    keyval_full = lax.all_gather(keyval_local, "mp", axis=2, tiled=True)
    keyval_heads = jnp.transpose(keyval_full.reshape(seq_len, 2, HEAD_DIM, KV_HEADS), (0, 1, 3, 2))
    local_heads = queries.shape[1] // HEAD_DIM
    group_size = HEADS // KV_HEADS
    kv_index = (mp_index * local_heads + jnp.arange(local_heads, dtype=jnp.int32)) // group_size
    keys = jnp.take(keyval_heads[:, 0], kv_index, axis=1)
    values = jnp.take(keyval_heads[:, 1], kv_index, axis=1)
    query_heads = queries.reshape(seq_len, local_heads, HEAD_DIM)
    scores = jnp.einsum(
        "qhd,khd->hqk", query_heads, keys, preferred_element_type=jnp.float32
    ) / math.sqrt(HEAD_DIM)
    documents = doc_ids[0]
    allowed = (documents[:, None] == documents[None, :]) & (
        positions[None, :] <= positions[:, None]
    )
    scores = jnp.where(allowed[None], scores, jnp.float32(-1e30))
    highest = jnp.max(scores, axis=-1, keepdims=True)
    weights = jnp.exp(scores - highest)
    probs = (weights / jnp.sum(weights, axis=-1, keepdims=True)).astype(jnp.bfloat16)
    output = jnp.einsum("hqk,khd->qhd", probs, values, preferred_element_type=jnp.float32)
    return output.astype(jnp.bfloat16).reshape(1, seq_len, local_heads * HEAD_DIM)


def solution(mesh):
    in_specs = (
        P(("group", "dp"), None, None),
        P(),
        P(),
        P(None, "mp"),
        P("mp"),
        P("mp", None),
        P("mp"),
        P(),
        P(("group", "dp"), None, None),
        P(("group", "dp"), None),
        P(),
        P(None, "mp"),
        P("mp"),
        P(None, None, "mp"),
        P(None, "mp"),
    )
    out_specs = P(("group", "dp"), None, "mp")
    count = mesh.shape["mp"]
    owners = mesh.shape["group"] * mesh.shape["dp"]
    narrow = count < 2 or count > KV_HEADS or count & (count - 1) or owners & (owners - 1)
    body = general if narrow else per_device
    return jax.shard_map(body, mesh=mesh, in_specs=in_specs, out_specs=out_specs, check_vma=False)
```

```python
import functools
import math

import jax
import jax.numpy as jnp
from jax import lax
from jax.experimental import pallas as pl
from jax.experimental.pallas import tpu as pltpu
from jax.sharding import PartitionSpec as P

HEADS = 64
KV_HEADS = 8
HEAD_DIM = 128
DOC_MAX = 64

BF16 = jnp.bfloat16
F32 = jnp.float32
VMEM = pl.BlockSpec(memory_space=pltpu.VMEM)
SMEM = pl.BlockSpec(memory_space=pltpu.SMEM)
ANY = pl.BlockSpec(memory_space=pl.ANY)
HBM = pl.BlockSpec(memory_space=pltpu.HBM)
AHEAD = 3
DEEP = 5
TAIL = 1
MIB = 1 << 20


def dot(a, b):
    return jnp.dot(a, b, preferred_element_type=F32)


def in_hbm(x):
    return pltpu.with_memory_space_constraint(x, pltpu.HBM)


def in_vmem(x):
    return pltpu.with_memory_space_constraint(x, pltpu.VMEM)


def params(mib):
    return pltpu.CompilerParams(vmem_limit_bytes=mib * MIB)


def cost(flops, nbytes):
    return pl.CostEstimate(flops=flops, bytes_accessed=nbytes, transcendentals=0)


def rms_scale(x, width):
    return lax.rsqrt(jnp.sum(x * x, axis=-1, keepdims=True) / width + 1e-06)


def stream(count, copy, body, ahead=AHEAD, then=None):
    @pl.loop(0, count)
    def _(i):
        copy(i).wait()

        @pl.when(i + ahead < count)
        def _():
            copy(i + ahead).start()

        if then is not None:

            @pl.when(i + ahead >= count)
            def _():
                then(i + ahead - count).start()

        body(i)


def begin(copy, ahead=AHEAD):
    for i in range(ahead):
        copy(i).start()


def tile(i, width):
    return pl.ds(pl.multiple_of(i * width, width), width)


def merger_kernel(
    where, patch_in, gain_in, bias_in, up, up_bias_in, down, down_bias_in, text, rms_gain_in, send, kept, text_out, hidden_out, bias_row, tail,
    patch, gain, bias, up_bias, down_bias, rms_gain, normed, merged, total, up_buf, down_buf, text_buf,
    small_sem, up_sem, down_sem, text_sem, tail_sem,
):
    slots = DEEP + 1
    step = up_buf.shape[1]
    width = down_buf.shape[2]
    half = send.shape[1]
    per_half = half // width
    mp = where[0]
    mine = mp % 2
    pairs = [(patch_in, patch), (gain_in, gain), (bias_in, bias), (up_bias_in, up_bias), (down_bias_in, down_bias)]
    pairs.append((rms_gain_in, rms_gain))
    small = [pltpu.make_async_copy(x, y, small_sem.at[i]) for i, (x, y) in enumerate(pairs)]
    for copy in small:
        copy.start()

    def up_copy(i):
        return pltpu.make_async_copy(up.at[tile(i, step)], up_buf.at[i % slots], up_sem.at[i % slots])

    def column(i):
        first = jnp.where(i < per_half, 1 - mine, mine)
        return pl.multiple_of(first * half + (i % per_half) * width, width)

    def down_copy(i):
        return pltpu.make_async_copy(
            down.at[:, pl.ds(column(i), width)], down_buf.at[i % slots], down_sem.at[i % slots]
        )

    block = text_buf.shape[1]
    blocks = text.shape[0] // block

    def text_copy(i):
        return pltpu.make_async_copy(text.at[tile(i, block)], text_buf.at[i % slots], text_sem.at[i % slots])

    def text_norm(i):
        text_copy(i).wait()

        @pl.when(i + DEEP < blocks)
        def _():
            text_copy(i + DEEP).start()

        x = text_buf[i % slots].astype(F32)
        text_out[tile(i, block), :] = (x * rms_scale(x, x.shape[1]) * rms_gain[...]).astype(BF16)

    begin(up_copy, DEEP)
    begin(text_copy, DEEP)
    for copy in small:
        copy.wait()
    rows = send.shape[0]
    joined = patch.shape[0] // rows
    features = patch.shape[1]
    pixels = patch[...].astype(F32)
    center = pixels - jnp.mean(pixels, axis=-1, keepdims=True)
    spread = jnp.mean(center * center, axis=-1, keepdims=True)
    patches = center * lax.rsqrt(spread + 1e-06) * gain[...][None, :] + bias[...][None, :]
    for c in range(features // 128):
        normed[c] = patches[:, c * 128 : (c + 1) * 128]
        for j in range(joined):
            merged[:, pl.ds(j * features + c * 128, 128)] = normed[c, pl.ds(j, rows, stride=joined), :].astype(BF16)
    own = down_bias.shape[0]
    bias_row[...] = jnp.zeros_like(bias_row)
    bias_row[:, pl.ds(pl.multiple_of(mp * own, 128), own)] = down_bias[...][None, :]
    total[...] = jnp.broadcast_to(up_bias[...][None, :], total.shape)

    def up_body(i):
        text_norm(i)
        total[...] += dot(merged[:, tile(i, step)], up_buf[i % slots])

    up_steps = up.shape[0] // step
    stream(up_steps, up_copy, up_body, DEEP, down_copy)
    sums = total[...]
    hidden = (0.5 * sums * (1.0 + lax.erf(sums * math.sqrt(0.5)))).astype(BF16)
    hidden_out[...] = hidden
    steps = 2 * per_half - tail.shape[0]

    def tail_copy(i):
        return pltpu.make_async_copy(down.at[:, pl.ds(column(i), width)], tail.at[i - steps], tail_sem.at[i - steps])

    @pl.loop(0, steps)
    def _(i):
        down_copy(i).wait()

        @pl.when(i + DEEP < steps)
        def _():
            down_copy(i + DEEP).start()

        @pl.when((i + DEEP >= steps) & (i + DEEP < 2 * per_half))
        def _():
            tail_copy(i + DEEP).start()

        text_norm(up_steps + i)
        part = (dot(hidden, down_buf[i % slots]) + bias_row[:, pl.ds(column(i), width)]).astype(BF16)

        @pl.when(i < per_half)
        def _():
            send[:, tile(i, width)] = part

        @pl.when(i >= per_half)
        def _():
            kept[:, tile(i - per_half, width)] = part

    for i in range(steps, 2 * per_half):
        text_norm(up_steps + i)
    for i in range(steps, 2 * per_half):
        tail_copy(i).wait()


def merger(where, patch, gain, bias, up, up_bias, down, down_bias, text, rms_gain, rows):
    features = patch.shape[1]
    depth, hidden = up.shape
    columns = down.shape[1]
    step = depth // 8
    width = columns // 8
    slots = DEEP + 1
    return pl.pallas_call(
        merger_kernel,
        out_shape=[
            jax.ShapeDtypeStruct((rows, columns // 2), BF16),
            jax.ShapeDtypeStruct((rows, columns // 2 - TAIL * width), BF16),
            pltpu.VMEM(text.shape, BF16),
            jax.ShapeDtypeStruct((rows, hidden), BF16),
            jax.ShapeDtypeStruct((1, columns), F32),
            pltpu.VMEM((TAIL, hidden, width), BF16),
        ],
        in_specs=[SMEM] + [HBM] * 9,
        out_specs=[VMEM] * 6,
        scratch_shapes=[
            pltpu.VMEM(patch.shape, BF16),
            pltpu.VMEM(gain.shape, F32),
            pltpu.VMEM(bias.shape, F32),
            pltpu.VMEM(up_bias.shape, F32),
            pltpu.VMEM(down_bias.shape, F32),
            pltpu.VMEM(rms_gain.shape, F32),
            pltpu.VMEM((features // 128, patch.shape[0], 128), F32),
            pltpu.VMEM((rows, depth), BF16),
            pltpu.VMEM((rows, hidden), F32),
            pltpu.VMEM((slots, step, hidden), BF16),
            pltpu.VMEM((slots, hidden, width), BF16),
            pltpu.VMEM((slots, text.shape[0] // 16, text.shape[1]), BF16),
            pltpu.SemaphoreType.DMA((6,)),
            pltpu.SemaphoreType.DMA((slots,)),
            pltpu.SemaphoreType.DMA((slots,)),
            pltpu.SemaphoreType.DMA((slots,)),
            pltpu.SemaphoreType.DMA((TAIL,)),
        ],
        compiler_params=params(34),
        cost_estimate=cost(2 * rows * hidden * (depth + columns), 2 * hidden * (depth + columns)),
        name="merger",
    )(where, *map(in_hbm, (patch, gain, bias, up, up_bias, down, down_bias, text, rms_gain)))


def keep_kernel(where, kept, hidden, bias_row, tail, keep):
    done = kept.shape[1]
    half = keep.shape[1]
    keep[:, pl.ds(0, done)] = kept[...]
    for i in range(tail.shape[0]):
        width = tail.shape[2]
        add = bias_row[:, pl.ds(pl.multiple_of((where[0] % 2) * half + done + i * width, width), width)]
        keep[:, pl.ds(done + i * width, width)] = (dot(hidden[...], tail[i]) + add).astype(BF16)


def keep_rest(where, kept, hidden, bias_row, tail):
    rows = kept.shape[0]
    return pl.pallas_call(
        keep_kernel,
        out_shape=jax.ShapeDtypeStruct((rows, bias_row.shape[1] // 2), BF16),
        in_specs=[SMEM] + [VMEM] * 4,
        out_specs=VMEM,
        compiler_params=params(6),
        cost_estimate=cost(2 * rows * tail.size, 2 * tail.size),
        name="keep_rest",
    )(where, kept, hidden, bias_row, in_vmem(tail))


def owner_slots(owner_row, me, rows, capacity, slots):
    total = owner_row.shape[1]
    row = lax.broadcasted_iota(jnp.int32, (total, rows), 0)
    mine = (row == me * rows + lax.broadcasted_iota(jnp.int32, (total, rows), 1)).astype(F32).astype(BF16)
    named = (owner_row[...] ^ me).astype(F32).astype(BF16)
    across = dot(named, mine)
    down = lax.dot_general(mine, named, (((0,), (1,)), ((), ())), preferred_element_type=F32)
    earlier = lax.broadcasted_iota(jnp.int32, (rows, rows), 0) < lax.broadcasted_iota(jnp.int32, (rows, rows), 1)
    rank = jnp.sum(jnp.where((down == across) & earlier, 1.0, 0.0), axis=0, keepdims=True)
    slot = across * capacity + rank
    return (lax.broadcasted_iota(jnp.int32, (slots, rows), 0).astype(F32) == slot).astype(F32).astype(BF16)


def slot_places(owner_row, me, owners, slots):
    total = owner_row.shape[1]
    capacity = slots // owners
    named = (owner_row[...] == me).astype(F32).astype(BF16)
    source = lax.broadcasted_iota(jnp.int32, (total, slots), 0) // (total // owners)
    block = (lax.broadcasted_iota(jnp.int32, (total, slots), 1) // capacity) ^ me
    here = dot(named, (source == block).astype(F32).astype(BF16))
    offset = dot(named, (source < block).astype(F32).astype(BF16))
    index = (lax.broadcasted_iota(jnp.int32, (1, slots), 1) % capacity).astype(F32)
    target = jnp.where(index < here, offset + index, -1.0)
    position = lax.broadcasted_iota(jnp.int32, (slots, slots), 0).astype(F32)
    return (position == target).astype(F32).astype(BF16)


def join_matrix(mp, count, width):
    heads = KV_HEADS // count
    coords = HEAD_DIM // count
    full = 2 * heads * HEAD_DIM
    column = lax.broadcasted_iota(jnp.int32, (width, full), 1)
    row = lax.broadcasted_iota(jnp.int32, (width, full), 0)
    base = (row // coords) * HEAD_DIM + row % coords
    places = [(column == base + (mp ^ x) * coords).astype(F32).astype(BF16) for x in range(count)]
    return jnp.concatenate(places, axis=0)


def weights_kernel(owners, where, owner_row, keyval, query, out, query_out, select, place, join, buf, sem, query_sem):
    depth, _, columns = keyval.shape
    pieces = sem.shape[0]
    step = depth // pieces
    together = step // 128

    def copy(i):
        return pltpu.make_async_copy(keyval.at[tile(i, step)], buf.at[tile(i, step)], sem.at[i])

    for i in range(pieces):
        copy(i).start()
    part = depth // query_sem.shape[0]
    copies = [
        pltpu.make_async_copy(
            query.at[pl.ds(i * part, part), pl.ds(0, query_out.shape[1])],
            query_out.at[pl.ds(i * part, part)],
            query_sem.at[i],
        )
        for i in range(query_sem.shape[0])
    ]
    for query_copy in copies:
        query_copy.start()
    mp, me = where[0], where[1]
    slots, rows = select.shape
    select[...] = owner_slots(owner_row, me, rows, slots // owners, slots)
    place[...] = slot_places(owner_row, me, owners, slots)
    count = KV_HEADS * HEAD_DIM // columns
    join[...] = join_matrix(mp, count, join.shape[0] // count)
    pairs = buf.reshape(2 * depth, columns)
    row = lax.broadcasted_iota(jnp.int32, (256, 256), 0)
    column = lax.broadcasted_iota(jnp.int32, (256, 256), 1)
    apart = (column == 2 * (row % 128) + row // 128).astype(F32).astype(BF16)

    @pl.loop(0, pieces)
    def _(j):
        copy(j).wait()
        blocks = [pairs[tile(j * together + n, 256), :] for n in range(together)]
        ordered = dot(apart, jnp.concatenate(blocks, axis=1)).astype(BF16)
        for n in range(together):
            for side in range(2):
                out[tile(j * together + n, 128), pl.ds(side * columns, columns)] = ordered[
                    side * 128 : (side + 1) * 128, n * columns : (n + 1) * columns
                ]

    for query_copy in copies:
        query_copy.wait()


def weights_ahead(where, owner_row, keyval, query, width, owners, slots):
    depth, _, columns = keyval.shape
    rows = owner_row.shape[1] // owners
    return pl.pallas_call(
        functools.partial(weights_kernel, owners),
        out_shape=[
            pltpu.VMEM((depth, 2 * columns), BF16),
            pltpu.VMEM((depth, width), BF16),
            jax.ShapeDtypeStruct((slots, rows), BF16),
            jax.ShapeDtypeStruct((slots, slots), BF16),
            jax.ShapeDtypeStruct((2 * columns, 2 * columns), BF16),
        ],
        in_specs=[SMEM, VMEM, HBM, HBM],
        out_specs=[VMEM] * 5,
        scratch_shapes=[pltpu.VMEM(keyval.shape, BF16), pltpu.SemaphoreType.DMA((8,)), pltpu.SemaphoreType.DMA((4,))],
        compiler_params=params(16),
        cost_estimate=cost(4 * depth * columns * 256, 4 * depth * columns),
        name="weights_ahead",
    )(where, owner_row, in_hbm(keyval), in_hbm(query))


def keyval_own_kernel(where, text, own, gain, weight, rows_all, sums):
    texts, half = text.shape[0], own.shape[1]
    here = pl.ds(pl.multiple_of((where[0] % 2) * half, half), half)
    rows_all[pl.ds(0, texts), :] = text[...]
    rows_all[pl.ds(texts, own.shape[0]), here] = (own[...].astype(F32) * gain[:, here]).astype(BF16)
    sums[...] = dot(rows_all[:, here], weight[here, :])


def keyval_kernel(where, _, sums_in, own, sibling, gain, weight, bias, rows_all, scale_out, *rest):
    parts, keyval = rest[:-1], rest[-1]
    images, half = own.shape
    texts = rows_all.shape[0] - images
    mp = where[0]
    here = pl.ds(pl.multiple_of((1 - mp % 2) * half, half), half)
    first, second = own[...].astype(F32), sibling[...].astype(F32)
    rows_all[pl.ds(texts, images), here] = (second * gain[:, here]).astype(BF16)
    squares = jnp.sum(first * first, axis=-1, keepdims=True) + jnp.sum(second * second, axis=-1, keepdims=True)
    scale = lax.rsqrt(squares / (2 * half) + 1e-06)
    scale_out[...] = jnp.broadcast_to(scale, scale_out.shape)
    columns = weight.shape[1] // 2
    sums = sums_in[...] + dot(rows_all[:, here], weight[here, :])
    for t in range(2):
        side = slice(t * columns, (t + 1) * columns)
        add = bias[pl.ds(t, 1), :]
        keyval[t, pl.ds(0, texts), :] = (sums[:texts, side] + add).astype(BF16)
        keyval[t, pl.ds(texts, images), :] = (sums[texts:, side] * scale + add).astype(BF16)

    count = len(parts)
    width = parts[0].shape[1]
    heads = KV_HEADS // count
    coords = columns // KV_HEADS
    row = lax.broadcasted_iota(jnp.int32, (columns, width // 2), 0)
    column = lax.broadcasted_iota(jnp.int32, (columns, width // 2), 1)
    for x in range(count):
        head = (mp ^ x) * heads + column // coords
        pick = (row == (column % coords) * KV_HEADS + head).astype(F32).astype(BF16)
        for t in range(2):
            parts[x][:, pl.ds(t * (width // 2), width // 2)] = dot(keyval[t], pick).astype(BF16)


def keyval_parts(where, text, own, sibling, gain, weight, bias, count):
    texts, depth = text.shape
    columns = weight.shape[1] // 2
    images = own.shape[0]
    rows = texts + images
    width = 2 * columns // count
    weight = in_vmem(weight)
    rows_all, sums = pl.pallas_call(
        keyval_own_kernel,
        out_shape=[pltpu.VMEM((rows, depth), BF16), pltpu.VMEM((rows, 2 * columns), F32)],
        in_specs=[SMEM, VMEM, VMEM, VMEM, VMEM],
        out_specs=[VMEM] * 2,
        compiler_params=params(8),
        cost_estimate=cost(2 * rows * depth * columns, 2 * depth * columns),
        name="keyval_own",
    )(where, in_vmem(text), own, gain, weight)
    outs = pl.pallas_call(
        keyval_kernel,
        out_shape=[pltpu.VMEM((rows, depth), BF16), jax.ShapeDtypeStruct((images, 128), F32)]
        + [jax.ShapeDtypeStruct((rows, width), BF16)] * count,
        in_specs=[SMEM] + [VMEM] * 7,
        out_specs=[VMEM] * (2 + count),
        scratch_shapes=[pltpu.VMEM((2, rows, columns), BF16)],
        input_output_aliases={1: 0},
        compiler_params=params(8),
        cost_estimate=cost(2 * rows * depth * columns, 2 * depth * columns),
        name="keyval",
    )(where, in_vmem(rows_all), in_vmem(sums), own, after(sibling, sums), gain, weight, bias)
    return outs[0], outs[1], outs[2:]


def query_kernel(rows_all, scale, ready, weight, bias, first_half, second_half, image_out, buf, sem):
    width = ready.shape[1]
    texts, half = first_half.shape
    later = buf.shape[0]

    def copy(i):
        return pltpu.make_async_copy(weight.at[:, tile(i + 1, width)], buf.at[i], sem.at[i])

    def columns(i, weights, text_out, offset):
        out = dot(rows_all[...], weights)
        add = bias[:, tile(i, width)]
        text_out[:, pl.ds(i * width - offset, width)] = (out[:texts] + add).astype(BF16)
        image_out[:, tile(i, width)] = (out[texts:] * scale[:, :1] + add).astype(BF16)

    begin(copy, 2)
    columns(0, ready[...], first_half, 0)
    for i in range(1, later + 1):
        copy(i - 1).wait()
        if i + 1 < later:
            copy(i + 1).start()
        if i * width < half:
            columns(i, buf[i - 1], first_half, 0)
        else:
            columns(i, buf[i - 1], second_half, half)


def query_rows(rows_all, scale, texts, ready, weight, bias):
    depth = rows_all.shape[1]
    images = rows_all.shape[0] - texts
    columns = weight.shape[1]
    width = ready.shape[1]
    later = columns // width - 1
    return pl.pallas_call(
        query_kernel,
        out_shape=[jax.ShapeDtypeStruct((texts, columns // 2), BF16)] * 2 + [jax.ShapeDtypeStruct((images, columns), BF16)],
        in_specs=[VMEM, VMEM, VMEM, HBM, VMEM],
        out_specs=[VMEM] * 3,
        scratch_shapes=[pltpu.VMEM((later, depth, width), BF16), pltpu.SemaphoreType.DMA((later,))],
        compiler_params=params(30),
        cost_estimate=cost(2 * (texts + images) * depth * columns, 2 * depth * columns),
        name="query",
    )(in_vmem(rows_all), scale, in_vmem(ready), in_hbm(weight), bias)


def slots_kernel(owners, select, queries, *rest):
    parts, outs = rest[:-owners], rest[-owners:]
    rows = queries.shape[0]
    capacity = outs[0].shape[0]
    images = [queries[...]] + [part[pl.ds(part.shape[0] - rows, rows), :] for part in parts]
    chosen = dot(select[...], jnp.concatenate(images, axis=1))
    for x, out in enumerate(outs):
        out[...] = chosen[x * capacity : (x + 1) * capacity].astype(BF16)


def slots_of(select, queries, parts, owners):
    width = queries.shape[1] + len(parts) * parts[0].shape[1]
    capacity = select.shape[0] // owners
    return pl.pallas_call(
        functools.partial(slots_kernel, owners),
        out_shape=[jax.ShapeDtypeStruct((capacity, width), BF16)] * owners,
        in_specs=[VMEM] * (2 + len(parts)),
        out_specs=[VMEM] * owners,
        compiler_params=params(8),
        name="slots",
    )(select, queries, *parts)


def attend(blocks, first, doc_row, queries, kv_all, out):
    q_first, k_first, out_first = first
    groups = kv_all.shape[1] // (2 * HEAD_DIM)
    per_half = groups // len(queries)
    shared = queries[0].shape[1] // HEAD_DIM // per_half
    block = DOC_MAX
    scale = 1.0 / math.sqrt(HEAD_DIM)
    docs = doc_row[...].astype(F32)
    ones = jnp.ones((2 * block, HEAD_DIM), BF16)
    row = lax.broadcasted_iota(jnp.int32, (block, 2 * block), 0)
    column = lax.broadcasted_iota(jnp.int32, (block, 2 * block), 1)
    for b in range(*blocks):
        q0 = b * block
        k0 = max(0, b - 1) * block
        k_doc = docs[:, k0 : k0 + 2 * block]
        q_doc = jnp.sum(jnp.where(k0 + column == q0 + row, k_doc, 0.0), axis=1, keepdims=True)
        allowed = (q_doc == k_doc) & (k0 + column <= q0 + row)
        penalty = jnp.concatenate([jnp.where(allowed, 0.0, -1e30)] * shared, axis=0)
        for g in range(groups):
            keys = kv_all[pl.ds(k0 - k_first, 2 * block), tile(g, HEAD_DIM)]
            values = kv_all[pl.ds(k0 - k_first, 2 * block), tile(groups + g, HEAD_DIM)]
            source = queries[g // per_half]
            columns = [tile((g % per_half) * shared + h, HEAD_DIM) for h in range(shared)]
            q = jnp.concatenate([source[pl.ds(q0 - q_first, block), c] for c in columns], axis=0)
            scores = lax.dot_general(q, keys, (((1,), (1,)), ((), ())), preferred_element_type=F32) * scale
            scores = jnp.where(penalty < 0.0, penalty, scores)
            weights = jnp.exp(scores - jnp.max(scores, axis=-1, keepdims=True))
            result = dot(weights.astype(BF16), jnp.concatenate([values, ones], axis=1))
            result = (result[:, :HEAD_DIM] / result[:, HEAD_DIM:]).astype(BF16)
            for h in range(shared):
                out[pl.ds(q0 - out_first, block), tile(g * shared + h, HEAD_DIM)] = result[h * block : (h + 1) * block]
        yield b


def late_kernel(early, join, doc_row, first_half, second_half, *rest):
    parts, out, kv_all = rest[:-2], rest[-2], rest[-1]
    seq = first_half.shape[0]
    sent = jnp.concatenate([part[pl.ds(0, seq), :] for part in parts], axis=1)
    kv_all[...] = dot(sent, join[...]).astype(BF16)
    blocks = (early // DOC_MAX, seq // DOC_MAX)
    for _ in attend(blocks, (0, 0, early), doc_row, (first_half, second_half), kv_all, out):
        pass


def early_kernel(early, order, doc_row, first_half, second_half, keyval, join, place, *rest):
    arrived = rest[:-7]
    late, out, first, second, kv_all, result, sem = rest[-7:]
    slots = place.shape[0]
    copies = [pltpu.make_async_copy(late, out.at[pl.ds(early, late.shape[0])], sem.at[0])]
    copies[0].start()
    half = first_half.shape[1]
    in_place = [arrived[order.index(x)][...].astype(F32) for x in range(len(order))]
    together = jnp.concatenate(in_place, axis=0).astype(BF16)
    placed = dot(place[...], together).astype(BF16)
    is_image = jnp.sum(place[...].astype(F32), axis=1, keepdims=True) > 0.5
    image_keyval = dot(placed[:, 2 * half :], join[...]).astype(BF16)
    kv_all[...] = keyval[pl.ds(0, early), :]
    kv_all[pl.ds(0, slots), :] = jnp.where(is_image, image_keyval, keyval[pl.ds(0, slots), :])
    for i, (source, target) in enumerate(((first_half, first), (second_half, second))):
        target[...] = source[pl.ds(0, early), :]
        target[pl.ds(0, slots), :] = jnp.where(
            is_image, placed[:, i * half : (i + 1) * half], source[pl.ds(0, slots), :]
        )
    for b in attend((0, early // DOC_MAX), (0, 0, 0), doc_row, (first, second), kv_all, result):
        here = pl.ds(b * DOC_MAX, DOC_MAX)
        copies.append(pltpu.make_async_copy(result.at[here], out.at[here], sem.at[b + 1]))
        copies[-1].start()
    for copy in copies:
        copy.wait()


def attention(join, place, documents, halves, parts, arrived, order, columns):
    seq = documents.shape[1]
    full = join.shape[1]
    slots = place.shape[0]
    owners = len(order)
    early = min(seq, -(-slots // DOC_MAX) * DOC_MAX + DOC_MAX)
    out, keyval = pl.pallas_call(
        functools.partial(late_kernel, early),
        out_shape=[pltpu.VMEM((seq - early, columns), BF16), jax.ShapeDtypeStruct((seq, full), BF16)],
        in_specs=[VMEM] * (4 + len(parts)),
        out_specs=[VMEM] * 2,
        compiler_params=params(12),
        cost_estimate=cost(4 * (seq - early) * columns * 2 * DOC_MAX, 4 * seq * columns),
        name="attention_late",
    )(join, documents, *halves, *parts)
    return pl.pallas_call(
        functools.partial(early_kernel, early, order),
        out_shape=jax.ShapeDtypeStruct((seq, columns), BF16),
        in_specs=[VMEM] * (7 + owners),
        out_specs=HBM,
        scratch_shapes=[pltpu.VMEM((early, columns // 2), BF16)] * 2
        + [pltpu.VMEM((early, full), BF16), pltpu.VMEM((early, columns), BF16), pltpu.SemaphoreType.DMA((1 + early // DOC_MAX,))],
        compiler_params=params(12),
        cost_estimate=cost(4 * early * columns * 2 * DOC_MAX, 4 * seq * columns),
        name="attention_early",
    )(documents, *halves, keyval, join, place, *arrived(out), in_vmem(out))


def after(x, *others):
    return lax.optimization_barrier((x, *others))[0]


def exchange(x, count, bit):
    return lax.ppermute(x, "mp", [(i, i ^ bit) for i in range(count)])


def per_device(
    patch_rows,
    ln_gain,
    ln_bias,
    merge_up,
    merge_up_bias,
    merge_down,
    merge_down_bias,
    row_owner,
    text_embed,
    doc_ids,
    rms_gain,
    w_query,
    query_bias,
    w_keyval,
    keyval_bias,
):
    owners = lax.axis_size(("group", "dp"))
    count = lax.axis_size("mp")
    mp_index = lax.axis_index("mp")
    where = jnp.stack([mp_index, lax.axis_index(("group", "dp"))]).astype(jnp.int32)
    rows = row_owner.shape[0] // owners
    capacity = max(2, 2 * rows // owners)
    owner_row = row_owner.reshape(1, -1)
    groups, line = lax.axis_size("group"), lax.axis_size("dp")

    def far(x):
        return max(abs(i % line - (i ^ x) % line) + (x >= line) for i in range(groups * line))


    send, kept, text, *rest = merger(
        where, patch_rows[0], ln_gain, ln_bias, merge_up, merge_up_bias, merge_down, merge_down_bias,
        text_embed[0], rms_gain[None, :], rows,
    )
    keep = keep_rest(where, kept, *rest)
    own = (keep.astype(F32) + after(exchange(send, count, 1), keep).astype(F32)).astype(BF16)
    slots = owners * capacity
    weight, ready, select, place, join = weights_ahead(
        where, owner_row, after(w_keyval, own), w_query, w_query.shape[1] // 4, owners, slots
    )
    bit = 2
    while bit < count:
        other = after(exchange(own, count, bit), weight)
        own = (own.astype(F32) + other.astype(F32)).astype(BF16)
        bit *= 2
    sibling = exchange(own, count, 1)

    columns = w_query.shape[1]
    rows_all, scale, parts = keyval_parts(where, text, own, sibling, rms_gain[None, :], weight, keyval_bias, count)
    parts = [parts[0]] + [exchange(parts[x], count, x) for x in range(1, count)]
    *halves, image_queries = query_rows(rows_all, scale, text.shape[0], ready, w_query, query_bias[None, :])
    outgoing = slots_of(select, image_queries, parts, owners)

    order = sorted(range(1, owners), key=lambda x: (x % 2 == 0, -x if x % 2 else -far(x)))

    def arrived(done):
        rows = [lax.ppermute(outgoing[x], ("group", "dp"), [(i, i ^ x) for i in range(owners)]) for x in order]
        return lax.optimization_barrier((*rows, outgoing[0], done))[:-1]

    halves = [after(half, outgoing[0]) for half in halves]
    return attention(join, place, doc_ids, halves, parts, arrived, [*order, 0], columns)[None]


def general(
    patch_rows,
    ln_gain,
    ln_bias,
    merge_up,
    merge_up_bias,
    merge_down,
    merge_down_bias,
    row_owner,
    text_embed,
    doc_ids,
    rms_gain,
    w_query,
    query_bias,
    w_keyval,
    keyval_bias,
):
    owners = lax.axis_size(("group", "dp"))
    own_index = lax.axis_index(("group", "dp"))
    mp_index = lax.axis_index("mp")
    pixels = patch_rows[0].astype(jnp.float32)
    center = pixels - jnp.mean(pixels, axis=-1, keepdims=True)
    spread = jnp.mean(center * center, axis=-1, keepdims=True)
    normed_patch = (center * lax.rsqrt(spread + 1e-06) * ln_gain + ln_bias).astype(jnp.bfloat16)
    merged = normed_patch.reshape(-1, 4 * pixels.shape[1])
    merged_rows = merged.shape[0]
    hidden = jax.nn.gelu(
        jnp.dot(merged, merge_up, preferred_element_type=jnp.float32) + merge_up_bias,
        approximate=False,
    ).astype(jnp.bfloat16)
    partial_sum = jnp.dot(hidden, merge_down, preferred_element_type=jnp.float32)
    vision = (
        lax.psum_scatter(partial_sum, "mp", scatter_dimension=1, tiled=True) + merge_down_bias
    ).astype(jnp.bfloat16)
    col_width = vision.shape[1]
    capacity = max(2, 2 * merged_rows // owners)
    owner_all = row_owner[:, 0]
    owner_ids = jnp.arange(owners, dtype=jnp.int32)
    onehot = (owner_all[:, None] == owner_ids[None, :]).astype(jnp.int32)
    per_source = jnp.sum(onehot.reshape(owners, merged_rows, owners), axis=1)
    my_block = lax.dynamic_slice_in_dim(onehot, own_index * merged_rows, merged_rows, 0)
    block_rank = jnp.sum((jnp.cumsum(my_block, axis=0) - my_block) * my_block, axis=1)
    my_owner = jnp.sum(my_block * owner_ids[None, :], axis=1)
    slot_id = my_owner * capacity + block_rank
    all_slots = jnp.arange(owners * capacity, dtype=jnp.int32)
    select = (slot_id[:, None] == all_slots[None, :]).astype(jnp.bfloat16)
    outgoing = jnp.einsum("ms,mc->sc", select, vision, preferred_element_type=jnp.float32).astype(
        jnp.bfloat16
    )
    arrived = lax.all_to_all(
        outgoing.reshape(owners, capacity, col_width),
        ("group", "dp"),
        split_axis=0,
        concat_axis=0,
        tiled=True,
    )
    arrived = arrived.reshape(owners * capacity, col_width)
    incoming = lax.dynamic_slice_in_dim(per_source, own_index, 1, 1)[:, 0]
    offsets = jnp.cumsum(incoming) - incoming
    total = jnp.sum(incoming)
    slot_rank = jnp.arange(capacity, dtype=jnp.int32)
    target = jnp.where(
        slot_rank[None, :] < incoming[:, None], offsets[:, None] + slot_rank[None, :], -1
    ).reshape(-1)
    text_rows = text_embed[0]
    seq_len = text_rows.shape[0]
    positions = jnp.arange(seq_len, dtype=jnp.int32)
    source_slot = jnp.sum(
        jnp.where(target[:, None] == positions[None, :], all_slots[:, None], 0), axis=0
    )
    is_image = (positions < total)[:, None]
    image_full = lax.all_gather(arrived, "mp", axis=1, tiled=True)
    sequence = jnp.where(is_image, jnp.take(image_full, source_slot, axis=0), text_rows)
    seq_f = sequence.astype(jnp.float32)
    normed_seq = (
        seq_f * lax.rsqrt(jnp.mean(seq_f * seq_f, axis=-1, keepdims=True) + 1e-06) * rms_gain
    ).astype(jnp.bfloat16)
    queries = (
        jnp.dot(normed_seq, w_query, preferred_element_type=jnp.float32) + query_bias
    ).astype(jnp.bfloat16)
    keyval_local = (
        jnp.einsum("sd,dtc->stc", normed_seq, w_keyval, preferred_element_type=jnp.float32)
        + keyval_bias
    ).astype(jnp.bfloat16)
    keyval_full = lax.all_gather(keyval_local, "mp", axis=2, tiled=True)
    keyval_heads = jnp.transpose(keyval_full.reshape(seq_len, 2, HEAD_DIM, KV_HEADS), (0, 1, 3, 2))
    local_heads = queries.shape[1] // HEAD_DIM
    group_size = HEADS // KV_HEADS
    kv_index = (mp_index * local_heads + jnp.arange(local_heads, dtype=jnp.int32)) // group_size
    keys = jnp.take(keyval_heads[:, 0], kv_index, axis=1)
    values = jnp.take(keyval_heads[:, 1], kv_index, axis=1)
    query_heads = queries.reshape(seq_len, local_heads, HEAD_DIM)
    scores = jnp.einsum(
        "qhd,khd->hqk", query_heads, keys, preferred_element_type=jnp.float32
    ) / math.sqrt(HEAD_DIM)
    documents = doc_ids[0]
    allowed = (documents[:, None] == documents[None, :]) & (
        positions[None, :] <= positions[:, None]
    )
    scores = jnp.where(allowed[None], scores, jnp.float32(-1e30))
    highest = jnp.max(scores, axis=-1, keepdims=True)
    weights = jnp.exp(scores - highest)
    probs = (weights / jnp.sum(weights, axis=-1, keepdims=True)).astype(jnp.bfloat16)
    output = jnp.einsum("hqk,khd->qhd", probs, values, preferred_element_type=jnp.float32)
    return output.astype(jnp.bfloat16).reshape(1, seq_len, local_heads * HEAD_DIM)


def solution(mesh):
    in_specs = (
        P(("group", "dp"), None, None),
        P(),
        P(),
        P(None, "mp"),
        P("mp"),
        P("mp", None),
        P("mp"),
        P(),
        P(("group", "dp"), None, None),
        P(("group", "dp"), None),
        P(),
        P(None, "mp"),
        P("mp"),
        P(None, None, "mp"),
        P(None, "mp"),
    )
    out_specs = P(("group", "dp"), None, "mp")
    count = mesh.shape["mp"]
    owners = mesh.shape["group"] * mesh.shape["dp"]
    narrow = count < 2 or count > KV_HEADS or count & (count - 1) or owners & (owners - 1)
    body = general if narrow else per_device
    return jax.shard_map(body, mesh=mesh, in_specs=in_specs, out_specs=out_specs, check_vma=False)
```
